128 devices in a mesh: group: 4 (over z), shard: 4 (over y_hi, core), tensor: 8 (over y_lo, x).
Axes of the slice: x: 4, y: 4 (y_hi: 2, y_lo: 2; y = y_hi * 2 + y_lo), z: 4, core: 2. Of those that a mesh axis runs over, the one named last changes fastest.
Arguments:
- prompt_states: bfloat16 [8192, 8192], P(('group', 'shard')), may hold values from -6 to 6
- prompt_lens: int32 [4, 3], replicated, may hold values from 1 to 1024, 2048 in all within a row
- w_query: bfloat16 [8192, 8192], P('shard', 'tensor'), may hold values from -0.06629126 to 0.06629126
- w_keyval: bfloat16 [8192, 2, 1024], P('shard', None, 'tensor'), may hold values from -0.06629126 to 0.06629126
- w_out: bfloat16 [8192, 8192], P('tensor', 'shard'), may hold values from -0.0625 to 0.0625
- decode_states: bfloat16 [64, 8192], P(('group', 'shard')), may hold values from -6 to 6
- kv_cache: bfloat16 [64, 2048, 2, 1024], P(('group', 'shard'), None, None, 'tensor'), may hold values from -6 to 6
- cache_len: int32 [64], P(('group', 'shard')), may hold values from 512 to 2044
- row_prompt: int32 [64], P(('group', 'shard')), may hold values from 0 to 12, as said below
Outputs:
- prompt_context: bfloat16 [8192, 8192], P(('group', 'shard'), 'tensor')
- decode_updates: bfloat16 [4, 64, 8192], P(None, ('group', 'shard'))
The draws below stay inside these ranges and needn't reach their ends.
Inputs may be any that keep to these rules, and one draw needn't show every extreme that they name: `row_prompt`: each prompt 0 to 11 is named by exactly one row; the 4 rows k*4 to (k+1)*4 - 1 of one device name at most one prompt; every other row holds 12.
All inputs are finite; a program needn't handle non-finite values.
Results may differ from the reference program's by a relative error of at most 0.023.
Values may be sent and summed in bfloat16 or wider, within the bound.
A program may use at most 192 MiB of HBM per device.

```python
import math
import jax
import jax.numpy as jnp
import numpy as np
from jax import lax

D = 8192
HEADS = 64
KVH = 8
HD = 128
PPG = 3
ROWS_DEV = 4
CACHE = 2048
STEPS = 4
TOK_GROUP = 2048
PTOK = 8192
NPROMPT = 12
BATCH = 64
MOST = 1024
N_GROUP = 4


def draw_prompt_states(key, part):
    key = jax.random.fold_in(key, 11)
    return jnp.clip(jax.random.normal(key, (PTOK, D), jnp.float32), -6.0, 6.0).astype(jnp.bfloat16)


def draw_decode_states(key, part):
    key = jax.random.fold_in(key, 17)
    return jnp.clip(jax.random.normal(key, (BATCH, D), jnp.float32), -6.0, 6.0).astype(jnp.bfloat16)


def draw_w_query(key, part):
    key = jax.random.fold_in(key, 13)
    return (jnp.clip(jax.random.normal(key, (D, HEADS * HD), jnp.float32), -6.0, 6.0) * D ** (-0.5)).astype(jnp.bfloat16)


def draw_w_keyval(key, part):
    key = jax.random.fold_in(key, 15)
    return (jnp.clip(jax.random.normal(key, (D, 2, KVH * HD), jnp.float32), -6.0, 6.0) * D ** (-0.5)).astype(jnp.bfloat16)


def draw_kv_cache(key, part):
    key = jax.random.fold_in(key, 19)
    return jnp.clip(jax.random.normal(key, (BATCH, CACHE, 2, KVH * HD), jnp.float32), -6.0, 6.0).astype(jnp.bfloat16)


def draw_row_prompt(key, part):
    key = jax.random.fold_in(key, 7)
    key_order, key_slot = jax.random.split(key)
    owners = BATCH // ROWS_DEV
    order = jax.random.permutation(key_order, owners).astype(jnp.int32)
    inverse = jnp.zeros((owners,), jnp.int32).at[order].set(jnp.arange(owners, dtype=jnp.int32))
    labels = jnp.where(inverse < NPROMPT, inverse, NPROMPT).astype(jnp.int32)
    slot = jax.random.randint(key_slot, (owners,), 0, ROWS_DEV).astype(jnp.int32)
    rows = jnp.arange(BATCH, dtype=jnp.int32)
    owner = rows // ROWS_DEV
    within = rows % ROWS_DEV
    return jnp.where(within == slot[owner], labels[owner], NPROMPT).astype(jnp.int32)


def touch_ends(result, stream_key, least, top_value):
    spot = [jax.random.randint(jax.random.fold_in(stream_key, axis), (), 0, length) for axis, length in enumerate(result.shape)]
    widest = result.shape.index(max(result.shape))
    next_to = spot[:widest] + [(spot[widest] + 1) % result.shape[widest]] + spot[widest + 1:]
    return result.at[tuple(spot)].set(least).at[tuple(next_to)].set(top_value)


def levels(own_key, shape, shards, least, largest):
    def one(dim, shards_of):
        steps = jax.random.uniform(jax.random.fold_in(jax.random.fold_in(own_key, 6), dim), (shards_of,), jnp.float32, least / len(shards), largest / len(shards))
        return jnp.repeat(jnp.exp(steps), shape[dim] // shards_of).reshape((-1,) + (1,) * (len(shape) - dim - 1))

    loudness = one(*shards[0])
    for cut in shards[1:]:
        loudness = loudness * one(*cut)
    return loudness


def length_profile(count, total, bound, slope):
    weights = [(1 << 20) // math.isqrt(rank ** slope) + 1 for rank in range(2, count + 1)]
    rest, counts = total - bound - (count - 1), [1] * (count - 1)
    while rest > 0:
        candidates = [i for i in range(count - 1) if counts[i] < bound]
        whole, budget = sum([weights[i] for i in candidates]), rest
        for i in candidates:
            more = min(bound - counts[i], max(1, budget * weights[i] // whole), rest)
            counts[i] = counts[i] + more
            rest = rest - more
    return np.array([bound] + counts)


def ragged_sizes(key, number_of, total, limit, lean):
    if number_of == 2:
        one = jax.random.randint(key, (), max(1, total - limit), min(limit, total - 1) + 1)
        return jnp.stack([one, total - one])
    sizes = jnp.asarray(length_profile(number_of, total, limit, lean), jnp.int32)
    couples = (number_of - 1) // 2
    donor, taker = sizes[1:1 + 2 * couples:2], sizes[2:2 + 2 * couples:2]
    room = jnp.minimum(donor - 1, limit - taker)
    passed = jax.random.randint(jax.random.fold_in(key, 1), (couples,), 0, 1 << 20) % (room + 1)
    sizes = sizes.at[1:1 + 2 * couples:2].set(donor - passed).at[2:2 + 2 * couples:2].set(taker + passed)
    return sizes[jax.random.permutation(jax.random.fold_in(key, 2), number_of)]


def bell_draw(rng, shape, deviation, reach, cuts=(), held_as=jnp.bfloat16):
    array = jax.random.normal(rng, shape, jnp.float32) * deviation
    if len(cuts) > 0:
        array = levels(rng, shape, cuts, -0.22, 0.18) * array
    return jnp.clip(array, min=-reach, max=reach).astype(held_as)


def setup_inputs(seed: int = 0) -> dict:
    seeds = jax.random.split(jax.random.key(seed), 10)
    prompt_states = draw_prompt_states(jax.random.fold_in(seeds[9], 71), 0)
    prompt_lens = jax.vmap(lambda own: ragged_sizes(own, PPG, TOK_GROUP, MOST, 2))(jax.random.split(seeds[1], N_GROUP)).reshape((N_GROUP, PPG)).astype(jnp.int32)
    w_query = draw_w_query(jax.random.fold_in(seeds[9], 71), 0)
    w_keyval = draw_w_keyval(jax.random.fold_in(seeds[9], 71), 0)
    w_out = bell_draw(seeds[4], (HEADS * HD, D), (HEADS * HD) ** -0.5, 0.0625, ((0, 8), (1, 4)))
    decode_states = draw_decode_states(jax.random.fold_in(seeds[9], 71), 0)
    kv_cache = draw_kv_cache(jax.random.fold_in(seeds[9], 71), 0)
    cache_len = touch_ends(jax.random.randint(seeds[7], (BATCH,), CACHE // 4, CACHE - STEPS + 1), jax.random.fold_in(seeds[7], 1), CACHE // 4, CACHE - STEPS).astype(jnp.int32)
    row_prompt = draw_row_prompt(jax.random.fold_in(seeds[9], 71), 0)
    return dict(prompt_states=prompt_states, prompt_lens=prompt_lens, w_query=w_query, w_keyval=w_keyval, w_out=w_out, decode_states=decode_states, kv_cache=kv_cache, cache_len=cache_len, row_prompt=row_prompt)


EPSILON = 1e-05

def normalize(states):
    values = states.astype(jnp.float32)
    return (values * lax.rsqrt(lax.optimization_barrier(jnp.mean(values * values, axis=-1, keepdims=True)) + EPSILON)).astype(jnp.bfloat16)

def round_half(values):
    return lax.optimization_barrier(values.astype(jnp.bfloat16)).astype(jnp.float32)

def prompt_attend(operands):
    queries, keyvals, lengths = operands
    position = jnp.arange(TOK_GROUP, dtype=jnp.int32)
    bounds = jnp.cumsum(lengths).astype(jnp.int32)
    segment = lax.optimization_barrier(jnp.sum((position[:, None] >= bounds[None, :]).astype(jnp.int32), axis=1))
    allowed = (segment[:, None] == segment[None, :]) & (position[None, :] <= position[:, None])
    scores = jnp.einsum('qkgd,nkd->kgqn', queries.astype(jnp.float32), keyvals[:, 0].astype(jnp.float32)) * HD ** (-0.5)
    masked = jnp.where(allowed, scores, -1e+30)
    highest = lax.optimization_barrier(jnp.max(masked, axis=-1, keepdims=True))
    weights = jnp.where(allowed, jnp.exp(masked - highest), 0.0)
    totals = lax.optimization_barrier(jnp.sum(weights, axis=-1))
    mixed = jnp.einsum('kgqn,nkd->kgqd', round_half(weights), keyvals[:, 1].astype(jnp.float32))
    context = (mixed / totals[..., None]).astype(jnp.bfloat16)
    return jnp.transpose(context, (2, 0, 1, 3)).reshape(TOK_GROUP, HEADS * HD)

def reference(prompt_states, prompt_lens, w_query, w_keyval, w_out, decode_states, kv_cache, cache_len, row_prompt):
    groups = HEADS // KVH
    w_joined = jnp.concatenate([w_query, w_keyval.reshape(D, 2 * KVH * HD)], axis=1)
    prompt_normed = normalize(prompt_states)
    projected = jnp.dot(prompt_normed, w_joined, preferred_element_type=jnp.float32).astype(jnp.bfloat16)
    queries = projected[:, :HEADS * HD].reshape(N_GROUP, TOK_GROUP, KVH, groups, HD)
    keyvals = projected[:, HEADS * HD:].reshape(PTOK, 2, KVH * HD)
    grouped = keyvals.reshape(N_GROUP, TOK_GROUP, 2, KVH, HD)
    prompt_context = lax.map(prompt_attend, (queries, grouped, prompt_lens)).reshape(PTOK, HEADS * HD)
    lens_flat = prompt_lens.reshape(-1)
    starts = (jnp.cumsum(lens_flat) - lens_flat).astype(jnp.int32)
    onehot = row_prompt[:, None] == jnp.arange(NPROMPT, dtype=jnp.int32)[None, :]
    is_new = jnp.any(onehot, axis=1)
    row_start = lax.optimization_barrier(jnp.sum(jnp.where(onehot, starts[None, :], 0), axis=1)).astype(jnp.int32)
    new_len = lax.optimization_barrier(jnp.sum(jnp.where(onehot, lens_flat[None, :], 0), axis=1))
    lengths = jnp.where(is_new, new_len, cache_len).astype(jnp.int32)
    padded = jnp.concatenate([keyvals, jnp.zeros((CACHE, 2, KVH * HD), jnp.bfloat16)], axis=0)

    def decode_row(operands):
        query, stored, fresh, begin_at, newflag, length = operands
        taken = lax.dynamic_slice_in_dim(padded, begin_at.astype(jnp.int32), CACHE, 0)
        cache_row = jnp.where(newflag, taken, stored)
        cache_keys = cache_row[:, 0].reshape(CACHE, KVH, HD).astype(jnp.float32)
        cache_vals = cache_row[:, 1].reshape(CACHE, KVH, HD).astype(jnp.float32)
        count = fresh.shape[0]
        fresh_keys = fresh[:, 0].reshape(count, KVH, HD).astype(jnp.float32)
        fresh_vals = fresh[:, 1].reshape(count, KVH, HD).astype(jnp.float32)
        query32 = query.astype(jnp.float32)
        old_scores = jnp.einsum('kgd,ckd->kgc', query32, cache_keys) * HD ** (-0.5)
        new_scores = jnp.einsum('kgd,ckd->kgc', query32, fresh_keys) * HD ** (-0.5)
        valid = jnp.arange(CACHE, dtype=jnp.int32) < length
        old_masked = jnp.where(valid, old_scores, -1e+30)
        highest = jnp.maximum(lax.optimization_barrier(jnp.max(old_masked, axis=-1)), lax.optimization_barrier(jnp.max(new_scores, axis=-1)))[..., None]
        old_weights = jnp.where(valid, jnp.exp(old_masked - highest), 0.0)
        new_weights = jnp.exp(new_scores - highest)
        totals = lax.optimization_barrier(jnp.sum(old_weights, axis=-1)) + lax.optimization_barrier(jnp.sum(new_weights, axis=-1))
        mixed = jnp.einsum('kgc,ckd->kgd', round_half(old_weights), cache_vals)
        mixed = mixed + jnp.einsum('kgc,ckd->kgd', round_half(new_weights), fresh_vals)
        return (mixed / totals[..., None]).astype(jnp.bfloat16).reshape(HEADS * HD)
    state = decode_states.astype(jnp.float32)
    fresh_list = []
    updates = []
    for step in range(STEPS):
        normed = normalize(state)
        fresh_proj = jnp.dot(normed, w_joined, preferred_element_type=jnp.float32).astype(jnp.bfloat16)
        step_queries = fresh_proj[:, :HEADS * HD].reshape(BATCH, KVH, groups, HD)
        fresh_list.append(fresh_proj[:, HEADS * HD:].reshape(BATCH, 2, KVH * HD))
        fresh_all = jnp.stack(fresh_list, axis=1)
        context = lax.map(decode_row, (step_queries, kv_cache, fresh_all, row_start, is_new, lengths))
        update = jnp.dot(context, w_out, preferred_element_type=jnp.float32)
        updates.append(update.astype(jnp.bfloat16))
        state = state + update
    return (prompt_context, jnp.stack(updates, axis=0))
```

```python
import jax
import jax.numpy as jnp
from jax import lax
from jax.experimental import pallas as pl
from jax.experimental.pallas import tpu as pltpu
from jax.sharding import PartitionSpec as P

HD = 128
CACHE = 2048
STEPS = 4


EPSILON = 1e-05


def normalize(states):
    values = states.astype(jnp.float32)
    return (values * lax.rsqrt(jnp.mean(values * values, axis=-1, keepdims=True) + EPSILON)).astype(
        jnp.bfloat16
    )


MESH = pl.DeviceIdType.MESH
NS = 4
NT = 8
WIN = 1152


def decode_kernel(
    meta_ref,
    ds_ref,
    wq_hbm,
    wkv_hbm,
    wo_hbm,
    cache_hbm,
    win_hbm,
    out_ref,
    wq,
    wkv,
    wo,
    cache,
    win,
    a_recv,
    xu,
    xu_send,
    state,
    b_send,
    b_recv,
    qs,
    fkv,
    c_send,
    c_recv,
    d_send,
    d_recv,
    e_send,
    e_recv,
    lsem,
    a_ss,
    a_rs,
    b_ss,
    b_rs,
    c_ss,
    c_rs,
    d_ss,
    d_rs,
    x_ss,
    x_rs,
    e_ss,
    e_rs,
):
    f32, bf16 = jnp.float32, jnp.bfloat16
    s = lax.axis_index("shard")
    t = lax.axis_index("tensor")
    rows = ds_ref.shape[1]
    dblk = wq.shape[0]
    qcols = wq.shape[1]
    piece = dblk // NT
    heads = qcols // HD
    width = NS * dblk

    loads = [
        pltpu.make_async_copy(a, b, lsem.at[i])
        for i, (a, b) in enumerate(
            [(wq_hbm, wq), (wkv_hbm, wkv), (wo_hbm, wo), (cache_hbm, cache), (win_hbm, win)]
        )
    ]
    for load in loads:
        load.start()

    def shard_peer(d):
        return lax.rem(s + d, NS)

    def tensor_peer(d):
        return lax.rem(t + d, NT)

    def remote(src, dst, ssem, rsem, **where):
        return pltpu.make_async_remote_copy(
            src_ref=src,
            dst_ref=dst,
            send_sem=ssem,
            recv_sem=rsem,
            device_id=where,
            device_id_type=MESH,
        )

    barrier = pltpu.get_barrier_semaphore()
    for d in range(1, NS):
        pl.semaphore_signal(barrier, inc=1, device_id={"shard": shard_peer(d)}, device_id_type=MESH)
    for d in range(1, NT):
        pl.semaphore_signal(
            barrier, inc=1, device_id={"tensor": tensor_peer(d)}, device_id_type=MESH
        )
    pl.semaphore_wait(barrier, NS - 1 + NT - 1)

    a_copies = []
    for d in range(1, NS):
        p = shard_peer(d)
        c = remote(ds_ref.at[p], a_recv.at[s], a_ss.at[d - 1], a_rs.at[s], shard=p)
        c.start()
        a_copies.append(c)
    a_recv[s] = ds_ref[s]
    fkv[...] = jnp.zeros_like(fkv)

    for d in range(1, NS):
        src = lax.rem(s + NS - d, NS)
        remote(ds_ref.at[s], a_recv.at[src], a_ss.at[d - 1], a_rs.at[src], shard=src).wait_recv()
    for c in a_copies:
        c.wait_send()
    x0 = jnp.concatenate([a_recv[i] for i in range(NS)], axis=0)
    for i in range(NT):
        xu[i, :, :piece] = x0[:, i * piece : (i + 1) * piece].astype(bf16)
    mine = pl.ds(pl.multiple_of(t * piece, piece), piece)
    state[...] = jnp.concatenate([a_recv[i, :, mine] for i in range(NS)], axis=0)

    for load in loads:
        load.wait()

    cpos = lax.broadcasted_iota(jnp.int32, (heads, cache.shape[1]), 1)
    wpos = lax.broadcasted_iota(jnp.int32, (heads, WIN), 1)
    wvalid = (wpos >= meta_ref[2 * rows : 2 * rows + 1, :1]) & (
        wpos < meta_ref[2 * rows + 1 : 2 * rows + 2, :1]
    )
    fresh_row = [meta_ref[r : r + 1, :] > 0 for r in range(rows)]
    inv_root = HD ** (-0.5)
    nt = (((1,), (1,)), ((), ()))

    def step(k, carry):
        acc = jnp.zeros((NS * rows, qcols + 2 * HD), f32)
        square = jnp.zeros((NS * rows, 1), f32)
        acc_q = jnp.zeros((NS * rows, qcols), f32)
        acc_kv = jnp.zeros((NS * rows, 2 * HD), f32)
        for i in range(NT):
            xi = xu[i, :, :piece]
            acc_q += jnp.dot(xi, wq[i * piece : (i + 1) * piece, :], preferred_element_type=f32)
            acc_kv += jnp.dot(xi, wkv[i * piece : (i + 1) * piece, :], preferred_element_type=f32)
            xf = xi.astype(f32)
            square += jnp.sum(xf * xf, axis=1, keepdims=True)
        squares = jnp.broadcast_to(square, (NS * rows, HD))
        for i in range(NS):
            b_send[i, :, :qcols] = acc_q[i * rows : (i + 1) * rows]
            b_send[i, :, qcols : qcols + 2 * HD] = acc_kv[i * rows : (i + 1) * rows]
            b_send[i, :, qcols + 2 * HD :] = squares[i * rows : (i + 1) * rows]
        copies = []
        for d in range(1, NS):
            p = shard_peer(d)
            c = remote(b_send.at[p], b_recv.at[s], b_ss.at[d - 1], b_rs.at[s], shard=p)
            c.start()
            copies.append(c)
        total = b_send[s]
        for d in range(1, NS):
            src = lax.rem(s + NS - d, NS)
            remote(
                b_send.at[s], b_recv.at[src], b_ss.at[d - 1], b_rs.at[src], shard=src
            ).wait_recv()
            total = total + b_recv[src]
        for c in copies:
            c.wait_send()
        scale = lax.rsqrt(total[:, qcols + 2 * HD : qcols + 2 * HD + 1] / width + EPSILON)
        fresh = (total[:, : qcols + 2 * HD] * scale).astype(bf16).astype(f32)
        fkv[k] = fresh[:, qcols:]
        for r in range(rows):
            for h in range(heads):
                qs[r, h : h + 1, :] = fresh[r : r + 1, h * HD : (h + 1) * HD]

        q_new = jnp.zeros((heads, HD), f32)
        for r in range(rows):
            q_new = jnp.where(fresh_row[r], qs[r], q_new)
        w_scores = (
            lax.dot_general(q_new.astype(bf16), win[:, :HD], nt, preferred_element_type=f32)
            * inv_root
        )
        w_scores = jnp.where(wvalid, w_scores, -1e30)
        w_high = jnp.max(w_scores, axis=1, keepdims=True)
        w_exp = jnp.where(wvalid, jnp.exp(w_scores - w_high), 0.0)
        w_total = jnp.sum(w_exp, axis=1, keepdims=True)
        w_mixed = jnp.dot(w_exp.astype(bf16), win[:, HD:], preferred_element_type=f32)
        for r in range(rows):
            q = qs[r]
            valid = cpos < meta_ref[rows + r : rows + r + 1, :1]
            scores = (
                lax.dot_general(q.astype(bf16), cache[r, :, :HD], nt, preferred_element_type=f32)
                * inv_root
            )
            scores = jnp.where(valid, scores, -1e30)
            high = jnp.max(scores, axis=1, keepdims=True)
            weights = jnp.where(valid, jnp.exp(scores - high), 0.0)
            summed = jnp.sum(weights, axis=1, keepdims=True)
            mixed = jnp.dot(weights.astype(bf16), cache[r, :, HD:], preferred_element_type=f32)
            high = jnp.where(fresh_row[r][:, :1], w_high, high)
            summed = jnp.where(fresh_row[r][:, :1], w_total, summed)
            mixed = jnp.where(fresh_row[r], w_mixed, mixed)
            news = []
            top = high
            for j in range(STEPS):
                new = jnp.sum(q * fkv[j, r : r + 1, :HD], axis=1, keepdims=True) * inv_root
                new = jnp.where(j <= k, new, -1e30)
                news.append(new)
                top = jnp.maximum(top, new)
            rescale = jnp.exp(high - top)
            summed = summed * rescale
            mixed = mixed * rescale
            for j in range(STEPS):
                weight = jnp.where(j <= k, jnp.exp(news[j] - top), 0.0)
                summed = summed + weight
                mixed = mixed + weight.astype(bf16).astype(f32) * fkv[j, r : r + 1, HD:]
            context = (mixed / summed).astype(bf16).astype(f32)
            for h in range(heads):
                c_send[r : r + 1, h * HD : (h + 1) * HD] = context[h : h + 1]

        copies = []
        for d in range(1, NS):
            p = shard_peer(d)
            c = remote(c_send, c_recv.at[s], c_ss.at[d - 1], c_rs.at[s], shard=p)
            c.start()
            copies.append(c)
        c_recv[s] = c_send[...]
        for d in range(1, NS):
            src = lax.rem(s + NS - d, NS)
            remote(c_send, c_recv.at[src], c_ss.at[d - 1], c_rs.at[src], shard=src).wait_recv()
        for c in copies:
            c.wait_send()
        block = jnp.concatenate([c_recv[i] for i in range(NS)], axis=0).astype(bf16)
        for i in range(NT):
            d_send[i] = jnp.dot(
                block, wo[:, i * piece : (i + 1) * piece], preferred_element_type=f32
            ).astype(bf16)

        copies = []
        for d in range(1, NT):
            p = tensor_peer(d)
            c = remote(d_send.at[p], d_recv.at[t], d_ss.at[d - 1], d_rs.at[t], tensor=p)
            c.start()
            copies.append(c)
        update = d_send[t].astype(f32)
        for d in range(1, NT):
            src = lax.rem(t + NT - d, NT)
            remote(
                d_send.at[t], d_recv.at[src], d_ss.at[d - 1], d_rs.at[src], tensor=src
            ).wait_recv()
            update = update + d_recv[src].astype(f32)
        for c in copies:
            c.wait_send()
        after = state[...] + update
        state[...] = after
        xu_send[:, :piece] = after.astype(bf16)
        xu_send[:, piece:] = update.astype(bf16)
        copies = []
        for d in range(1, NT):
            p = tensor_peer(d)
            c = remote(xu_send, xu.at[t], x_ss.at[d - 1], x_rs.at[t], tensor=p)
            c.start()
            copies.append(c)
        xu[t] = xu_send[...]
        for d in range(1, NT):
            src = lax.rem(t + NT - d, NT)
            remote(xu_send, xu.at[src], x_ss.at[d - 1], x_rs.at[src], tensor=src).wait_recv()
        for c in copies:
            c.wait_send()

        for i in range(NT):
            u = xu[i, :, piece:].astype(f32)
            for j in range(NS):
                e_send[k, j, :, i * piece : (i + 1) * piece] = u[j * rows : (j + 1) * rows]
        for d in range(1, NS):
            p = shard_peer(d)
            remote(
                e_send.at[k, p], e_recv.at[k, s], e_ss.at[k, d - 1], e_rs.at[k, s], shard=p
            ).start()
        e_recv[k, s] = e_send[k, s]
        return carry

    lax.fori_loop(0, STEPS, step, 0)

    for k in range(STEPS):
        for d in range(1, NS):
            src = lax.rem(s + NS - d, NS)
            c = remote(
                e_send.at[k, src], e_recv.at[k, src], e_ss.at[k, d - 1], e_rs.at[k, src], shard=src
            )
            c.wait_recv()
            c.wait_send()
        for i in range(NS):
            out_ref[k, :, i * dblk : (i + 1) * dblk] = e_recv[k, i].astype(bf16)


def decode(meta, decode_states, wq, wkv, wo, cache, window):
    rows, width = decode_states.shape
    dblk, qcols = wq.shape
    piece = dblk // NT
    f32, bf16 = jnp.float32, jnp.bfloat16
    states = jnp.transpose(decode_states.astype(f32).reshape(rows, NS, dblk), (1, 0, 2))
    vmem = pl.BlockSpec(memory_space=pltpu.VMEM)
    hbm = pl.BlockSpec(memory_space=pl.ANY)
    dma = pltpu.SemaphoreType.DMA
    bw = qcols + 3 * HD
    return pl.pallas_call(
        decode_kernel,
        out_shape=jax.ShapeDtypeStruct((STEPS, rows, width), bf16),
        in_specs=[vmem, vmem, hbm, hbm, hbm, hbm, hbm],
        out_specs=vmem,
        scratch_shapes=[
            pltpu.VMEM(wq.shape, bf16),
            pltpu.VMEM(wkv.shape, bf16),
            pltpu.VMEM(wo.shape, bf16),
            pltpu.VMEM(cache.shape, bf16),
            pltpu.VMEM(window.shape, bf16),
            pltpu.VMEM((NS, rows, dblk), f32),
            pltpu.VMEM((NT, NS * rows, 2 * piece), bf16),
            pltpu.VMEM((NS * rows, 2 * piece), bf16),
            pltpu.VMEM((NS * rows, piece), f32),
            pltpu.VMEM((NS, rows, bw), f32),
            pltpu.VMEM((NS, rows, bw), f32),
            pltpu.VMEM((rows, qcols // HD, HD), f32),
            pltpu.VMEM((STEPS, rows, 2 * HD), f32),
            pltpu.VMEM((rows, qcols), f32),
            pltpu.VMEM((NS, rows, qcols), f32),
            pltpu.VMEM((NT, NS * rows, piece), bf16),
            pltpu.VMEM((NT, NS * rows, piece), bf16),
            pltpu.VMEM((STEPS, NS, rows, dblk), f32),
            pltpu.VMEM((STEPS, NS, rows, dblk), f32),
            dma((5,)),
            dma((NS - 1,)),
            dma((NS,)),
            dma((NS - 1,)),
            dma((NS,)),
            dma((NS - 1,)),
            dma((NS,)),
            dma((NT - 1,)),
            dma((NT,)),
            dma((NT - 1,)),
            dma((NT,)),
            dma((STEPS, NS - 1)),
            dma((STEPS, NS)),
        ],
        compiler_params=pltpu.CompilerParams(
            collective_id=0, has_side_effects=True, vmem_limit_bytes=50 * 1024 * 1024
        ),
        name="decode",
    )(meta, states, wq, wkv, wo, cache, window)


def body(
    prompt_states,
    prompt_lens,
    w_query,
    w_keyval,
    w_out,
    decode_states,
    kv_cache,
    cache_len,
    row_prompt,
):
    shard_index = lax.axis_index("shard")
    group_index = lax.axis_index("group")
    d_part = w_query.shape[0]
    q_cols = w_query.shape[1]
    kv_cols = w_keyval.shape[2]
    heads_local = q_cols // HD
    kv_local = kv_cols // HD
    groups = heads_local // kv_local
    tok_local = prompt_states.shape[0]
    rows_local = decode_states.shape[0]
    inv_root = HD ** (-0.5)
    prompt_normed = normalize(prompt_states)
    query_piece = lax.all_gather(w_query, "shard", axis=0, tiled=True)
    keyval_piece = lax.all_gather(w_keyval, "shard", axis=0, tiled=True)
    amount = query_piece.shape[0]
    query_sum = jnp.dot(prompt_normed, query_piece, preferred_element_type=jnp.float32)
    keyval_sum = jnp.dot(
        prompt_normed, keyval_piece.reshape(amount, 2 * kv_cols), preferred_element_type=jnp.float32
    )
    queries = query_sum.astype(jnp.bfloat16)
    keyvals = keyval_sum.astype(jnp.bfloat16)
    keyvals = keyvals.reshape(tok_local, 2, kv_cols)
    query_heads = queries.reshape(tok_local, kv_local, groups, HD)
    group_pick = jnp.arange(prompt_lens.shape[0], dtype=jnp.int32) == group_index
    lens_mine = jnp.sum(jnp.where(group_pick[:, None], prompt_lens, 0), axis=0)
    bounds = jnp.cumsum(lens_mine)
    query_pos = shard_index * tok_local + jnp.arange(tok_local, dtype=jnp.int32)
    query_seg = jnp.sum((query_pos[:, None] >= bounds[None, :]).astype(jnp.int32), axis=1)
    piece = lax.all_gather(keyvals, "shard", axis=0, tiled=True)
    highest = jnp.full((kv_local, groups, tok_local), -1e30, jnp.float32)
    amount = piece.shape[0]
    key_pos = jnp.arange(amount, dtype=jnp.int32)
    key_seg = jnp.sum((key_pos[:, None] >= bounds[None, :]).astype(jnp.int32), axis=1)
    allowed = (query_seg[:, None] == key_seg[None, :]) & (key_pos[None, :] <= query_pos[:, None])
    keys = piece[:, 0].reshape(amount, kv_local, HD)
    values = piece[:, 1].reshape(amount, kv_local, HD)
    scores = (
        jnp.einsum("qkgd,nkd->kgqn", query_heads, keys, preferred_element_type=jnp.float32)
        * inv_root
    )
    masked = jnp.where(allowed, scores, -1e30)
    new_high = jnp.maximum(highest, jnp.max(masked, axis=-1))
    weights = jnp.where(allowed, jnp.exp(masked - new_high[..., None]), 0.0)
    totals = jnp.sum(weights, axis=-1)
    mixed = jnp.einsum(
        "kgqn,nkd->kgqd", weights.astype(jnp.bfloat16), values, preferred_element_type=jnp.float32
    )
    highest, totals, mixed = (new_high, totals, mixed)
    context = (mixed / totals[..., None]).astype(jnp.bfloat16)
    prompt_context = jnp.transpose(context, (2, 0, 1, 3)).reshape(tok_local, q_cols)
    lens_flat = prompt_lens.reshape(-1)
    kv_all = lax.all_gather(
        keyvals.reshape(tok_local, 2 * kv_cols), ("group", "shard"), axis=0, tiled=True
    )
    starts = jnp.cumsum(lens_flat) - lens_flat
    onehot = row_prompt[:, None] == jnp.arange(lens_flat.shape[0], dtype=jnp.int32)[None, :]
    is_new = jnp.any(onehot, axis=1)
    first = jnp.sum(jnp.where(onehot, starts[None, :], 0))
    count = jnp.sum(jnp.where(onehot, lens_flat[None, :], 0))
    base = jnp.minimum((first // 16) * 16, kv_all.shape[0] - WIN)
    window = lax.dynamic_slice_in_dim(kv_all, base, WIN, 0)
    bounds_new = jnp.stack([first - base, first - base + count])
    meta = jnp.concatenate([is_new.astype(jnp.int32), cache_len, bounds_new])
    meta = jnp.pad(meta, (0, 16 - meta.shape[0]))
    updates = decode(
        jnp.broadcast_to(meta[:, None], (16, HD)),
        decode_states,
        w_query,
        w_keyval.reshape(d_part, 2 * kv_cols),
        w_out,
        kv_cache.reshape(rows_local, CACHE, 2 * kv_cols),
        window,
    )
    return (prompt_context, updates)


def solution(mesh):
    in_specs = (
        P(("group", "shard"), None),
        P(),
        P("shard", "tensor"),
        P("shard", None, "tensor"),
        P("tensor", "shard"),
        P(("group", "shard"), None),
        P(("group", "shard"), None, None, "tensor"),
        P(("group", "shard")),
        P(("group", "shard")),
    )
    out_specs = (P(("group", "shard"), "tensor"), P(None, ("group", "shard"), None))
    return jax.shard_map(body, mesh=mesh, in_specs=in_specs, out_specs=out_specs, check_vma=False)
```

```python
import functools

import jax
import jax.numpy as jnp
from jax import lax
from jax.experimental import pallas as pl
from jax.experimental.pallas import tpu as pltpu
from jax.sharding import PartitionSpec as P

HD = 128
CACHE = 2048
STEPS = 4
EPSILON = 1e-05
MESH = pl.DeviceIdType.MESH
NG = 4
NS = 4
NT = 8
MOST = 1024
QT = 256
KW = QT + MOST
INV_ROOT = HD**-0.5
LOG2E = 1.4426950408889634
TRANS = (((1,), (1,)), ((), ()))
f32 = jnp.float32
bf16 = jnp.bfloat16


def kernel(names, meta_ref, ds_ref, x_hbm, wkv_hbm, wq_hbm, wo_hbm, cache_hbm, ctx_ref, out_ref, *scratch):
    r = dict(zip(names, scratch))
    xv, wkv, wq, wo, raw, ck, cv = (r[n] for n in ("xv", "wkv", "wq", "wo", "raw", "ck", "cv"))
    kv, qh, acc_q, acc_kv, scale, bias = (r[n] for n in ("kv", "qh", "acc_q", "acc_kv", "scale", "bias"))
    a_recv, xu, xu_send, state = (r[n] for n in ("a_recv", "xu", "xu_send", "state"))
    b_send, b_recv, qs, fkv = (r[n] for n in ("b_send", "b_recv", "qs", "fkv"))
    c_send, c_recv, d_send, d_recv = (r[n] for n in ("c_send", "c_recv", "d_send", "d_recv"))
    e_send, e_recv = r["e_send"], r["e_recv"]

    g = lax.axis_index("group")
    s = lax.axis_index("shard")
    t = lax.axis_index("tensor")
    sc = s + 1 - 2 * lax.rem(s, 2)
    s2 = lax.rem(s + 2, NS)
    s3 = lax.rem(sc + 2, NS)
    tok = xv.shape[0]
    rows = ds_ref.shape[1]
    dblk, qcols = wq.shape[1:]
    piece = dblk // NT
    heads = qcols // HD
    width = NS * dblk
    quarter = dblk // NG
    half = quarter // 2

    def up(base, d, n):
        return lax.rem(base + d, n)

    def remote(src, dst, ssem, rsem, **where):
        return pltpu.make_async_remote_copy(
            src_ref=src, dst_ref=dst, send_sem=ssem, recv_sem=rsem, device_id=where, device_id_type=MESH
        )

    sent = []

    def send(src, dst, ssem, rsem, **where):
        c = remote(src, dst, ssem, rsem, **where)
        c.start()
        sent.append(c)
        return c

    def arrive(dst, ssem, rsem, **where):
        remote(dst, dst, ssem, rsem, **where).wait_recv()

    def load(a, b, i):
        c = pltpu.make_async_copy(a, b, r["lsem"].at[i])
        c.start()
        return c

    load_x = load(x_hbm, xv, 0)
    load_wkv = load(wkv_hbm, wkv.at[s], 1)
    load_wq = load(wq_hbm, wq.at[s], 2)
    load_raw = load(cache_hbm, raw, 3)
    load_wo = load(wo_hbm, wo, 4)

    barrier = pltpu.get_barrier_semaphore()
    for d in range(1, NS):
        pl.semaphore_signal(barrier, inc=1, device_id={"shard": up(s, d, NS)}, device_id_type=MESH)
    for d in range(1, NG):
        pl.semaphore_signal(barrier, inc=1, device_id={"group": up(g, d, NG)}, device_id_type=MESH)
    for d in range(1, NT):
        pl.semaphore_signal(barrier, inc=1, device_id={"tensor": up(t, d, NT)}, device_id_type=MESH)
    pl.semaphore_wait(barrier, NS - 1 + NG - 1 + NT - 1)

    def krows(blk, q):
        return wkv.at[blk, pl.ds(pl.multiple_of(q * quarter, quarter), quarter)]

    def qrows(blk, q, h):
        return wq.at[blk, pl.ds(pl.multiple_of(q * quarter + h * half, half), half)]

    q_of = [g, up(g, 2, NG), up(g, 3, NG), up(g, 1, NG)]
    ky_s, ky_r, kz_s, kz_r, kc_s, kc_r = (r[n] for n in ("ky_s", "ky_r", "kz_s", "kz_r", "kc_s", "kc_r"))
    qy_s, qy_r, qz_s, qz_r, qc_s, qc_r = (r[n] for n in ("qy_s", "qy_r", "qz_s", "qz_r", "qc_s", "qc_r"))

    for i in range(2):
        src = wkv_hbm.at[pl.ds(pl.multiple_of(q_of[i] * quarter, quarter), quarter)]
        send(src, krows(s, q_of[i]), ky_s.at[i], ky_r.at[i], shard=s2)
    send(wkv_hbm, wkv.at[s], kc_s.at[4], kc_r.at[4], shard=sc)
    for d in range(1, NS):
        p = up(s, d, NS)
        send(ds_ref.at[p], a_recv.at[s], r["a_s"].at[d - 1], r["a_r"].at[s], shard=p)
    send(wq_hbm, wq.at[s], qc_s.at[8], qc_r.at[8], shard=sc)
    a_recv[s] = ds_ref[s]
    r["fkv"][...] = jnp.zeros_like(fkv)
    kv[:MOST, :] = jnp.zeros((MOST, 2 * HD), bf16)

    def k_arrive_y(i):
        arrive(krows(s2, q_of[i]), ky_s.at[i], ky_r.at[i], shard=s2)

    def k_arrive_z(i):
        arrive(krows(s2, q_of[2 + i]), kz_s.at[i], kz_r.at[i], group=q_of[2 + i])

    def k_forward(role):
        ref = krows(s2, q_of[role])
        send(ref, ref, kc_s.at[role], kc_r.at[role], shard=sc)

    def k_forward_z():
        ref = krows(s2, g)
        send(ref, ref, kz_s.at[0], kz_r.at[0], group=up(g, 1, NG))
        send(ref, ref, kz_s.at[1], kz_r.at[1], group=up(g, 3, NG))

    def q_send_y(i):
        src = wq_hbm.at[pl.ds(pl.multiple_of(q_of[i // 2] * quarter + i % 2 * half, half), half)]
        send(src, qrows(s, q_of[i // 2], i % 2), qy_s.at[i], qy_r.at[i], shard=s2)

    def q_arrive_y(i):
        arrive(qrows(s2, q_of[i // 2], i % 2), qy_s.at[i], qy_r.at[i], shard=s2)

    def q_forward_z(h):
        ref = qrows(s2, g, h)
        send(ref, ref, qz_s.at[h], qz_r.at[h], group=up(g, 1, NG))
        send(ref, ref, qz_s.at[2 + h], qz_r.at[2 + h], group=up(g, 3, NG))

    def q_arrive_z(i):
        arrive(qrows(s2, q_of[2 + i // 2], i % 2), qz_s.at[i], qz_r.at[i], group=q_of[2 + i // 2])

    def q_forward(i):
        ref = qrows(s2, q_of[i // 2], i % 2)
        send(ref, ref, qc_s.at[i], qc_r.at[i], shard=sc)

    def q_arrive_core(i):
        arrive(qrows(s3, q_of[i // 2], i % 2), qc_s.at[i], qc_r.at[i], shard=sc)

    def x_block(blk):
        return xv[:, pl.ds(pl.multiple_of(blk * dblk, dblk), dblk)]

    def kv_block(blk, first):
        prod = jnp.dot(x_block(blk), wkv[blk], preferred_element_type=f32)
        acc_kv[...] = prod if first else acc_kv[...] + prod

    def q_block(blk, first, lo=0, hi=None):
        hi = qcols // 256 if hi is None else hi

        def part(n, c):
            cols = pl.ds(pl.multiple_of(n * 256, 256), 256)
            prod = jnp.dot(x_block(blk), wq[blk, :, cols], preferred_element_type=f32)
            acc_q[:, cols] = prod if first else acc_q[:, cols] + prod
            return c

        lax.fori_loop(lo, hi, part, 0)

    load_x.wait()

    def squares(i, c):
        part = pl.ds(pl.multiple_of(i * 32, 32), 32)
        v = xv[part, :].astype(f32)
        mean = jnp.sum(v * v, axis=1, keepdims=True) / width
        scale[part, :] = jnp.broadcast_to(lax.rsqrt(mean + EPSILON), (32, HD))
        return c

    lax.fori_loop(0, tok // 32, squares, 0)
    load_wkv.wait()
    kv_block(s, True)

    k_arrive_y(0)
    k_forward_z()
    k_forward(0)

    for d in range(1, NS):
        src = up(s, NS - d, NS)
        arrive(a_recv.at[src], r["a_s"].at[d - 1], r["a_r"].at[src], shard=src)
    x0 = jnp.concatenate([a_recv[i] for i in range(NS)], axis=0)
    for i in range(NT):
        xu[i, :, :piece] = x0[:, i * piece : (i + 1) * piece].astype(bf16)
    mine = pl.ds(pl.multiple_of(t * piece, piece), piece)
    state[...] = jnp.concatenate([a_recv[i, :, mine] for i in range(NS)], axis=0)

    load_wq.wait()
    q_block(s, True)

    k_arrive_y(1)
    k_forward(1)
    q_send_y(0)
    arrive(wkv.at[sc], kc_s.at[4], kc_r.at[4], shard=sc)
    kv_block(sc, False)
    k_arrive_z(0)
    k_forward(2)
    k_arrive_z(1)
    k_forward(3)
    kv_block(s2, False)
    for role in range(4):
        arrive(krows(s3, q_of[role]), kc_s.at[role], kc_r.at[role], shard=sc)
    kv_block(s3, False)

    def slot(gg, ss):
        return kv.at[pl.ds(pl.multiple_of(MOST + (gg * NS + ss) * tok, tok), tok)]

    both = jnp.concatenate([scale[...], scale[...]], axis=1)
    kv[pl.ds(pl.multiple_of(MOST + (g * NS + s) * tok, tok), tok), :] = (acc_kv[...] * both).astype(bf16)
    vy_s, vy_r, vz_s, vz_r, vc_s, vc_r = (r[n] for n in ("vy_s", "vy_r", "vz_s", "vz_r", "vc_s", "vc_r"))
    own = slot(g, s)
    send(own, own, vy_s.at[0], vy_r.at[0], shard=s2)
    for d in (1, 3, 2):
        send(own, own, vz_s.at[d - 1], vz_r.at[d - 1], group=up(g, d, NG))
    send(own, own, vc_s.at[0], vc_r.at[0], shard=sc)

    def decode_project():
        acc = jnp.zeros((NS * rows, qcols), f32)
        acc2 = jnp.zeros((NS * rows, 2 * HD), f32)
        square = jnp.zeros((NS * rows, 1), f32)
        for i in range(NT):
            xi = xu[i, :, :piece]
            acc += jnp.dot(xi, wq[s, i * piece : (i + 1) * piece, :], preferred_element_type=f32)
            acc2 += jnp.dot(xi, wkv[s, i * piece : (i + 1) * piece, :], preferred_element_type=f32)
            xf = xi.astype(f32)
            square += jnp.sum(xf * xf, axis=1, keepdims=True)
        wide = jnp.broadcast_to(square, (NS * rows, HD))
        for i in range(NS):
            b_send[i, :, :qcols] = acc[i * rows : (i + 1) * rows]
            b_send[i, :, qcols : qcols + 2 * HD] = acc2[i * rows : (i + 1) * rows]
            b_send[i, :, qcols + 2 * HD :] = wide[i * rows : (i + 1) * rows]
        copies = []
        for d in range(1, NS):
            p = up(s, d, NS)
            c = remote(b_send.at[p], b_recv.at[s], r["b_s"].at[d - 1], r["b_r"].at[s], shard=p)
            c.start()
            copies.append(c)
        return copies

    b_copies = decode_project()

    load_raw.wait()
    out_i = lax.broadcasted_iota(jnp.int32, (256, 256), 0)
    in_i = lax.broadcasted_iota(jnp.int32, (256, 256), 1)
    want = jnp.where(out_i < 128, 2 * out_i, 2 * (out_i - 128) + 1)
    pick = (in_i == want).astype(bf16)

    def separate(i, c):
        src = pl.ds(pl.multiple_of(i * 256, 256), 256)
        dst = pl.ds(pl.multiple_of(i * 128, 128), 128)
        for row in range(0, rows, 2):
            pair = jnp.concatenate([raw[row, src, :], raw[row + 1, src, :]], axis=1)
            split = jnp.dot(pick, pair, preferred_element_type=f32).astype(bf16)
            for j in range(2):
                ck[row + j, dst, :] = split[:128, j * HD : (j + 1) * HD]
                cv[row + j, dst, :] = split[128:, j * HD : (j + 1) * HD]
        return c

    lax.fori_loop(0, 2 * ck.shape[1] // 256, separate, 0)
    arrive(wq.at[sc], qc_s.at[8], qc_r.at[8], shard=sc)
    q_block(sc, False)

    for i in range(tok // QT):
        q_pos = s * tok + i * QT + lax.broadcasted_iota(jnp.int32, (QT, KW), 0)
        k_pos = s * tok + i * QT - MOST + lax.broadcasted_iota(jnp.int32, (QT, KW), 1)
        b0 = meta_ref[3 * rows : 3 * rows + 1, :1]
        b1 = meta_ref[3 * rows + 1 : 3 * rows + 2, :1]
        start = jnp.where(q_pos >= b1, b1, jnp.where(q_pos >= b0, b0, 0))
        bias[i] = jnp.where((k_pos >= start) & (k_pos <= q_pos), 0.0, -1e30)

    arrive(slot(g, s2), vy_s.at[0], vy_r.at[0], shard=s2)
    theirs = slot(g, s2)
    for d in (1, 3, 2):
        send(theirs, theirs, vz_s.at[2 + d], vz_r.at[2 + d], group=up(g, d, NG))
    send(theirs, theirs, vc_s.at[1], vc_r.at[1], shard=sc)
    q_send_y(1)
    for d in range(1, NG):
        ref = slot(up(g, NG - d, NG), s)
        arrive(ref, vz_s.at[d - 1], vz_r.at[d - 1], group=up(g, NG - d, NG))
        send(ref, ref, vc_s.at[1 + d], vc_r.at[1 + d], shard=sc)
    q_send_y(2)
    q_send_y(3)
    for d in range(1, NG):
        ref = slot(up(g, NG - d, NG), s2)
        arrive(ref, vz_s.at[2 + d], vz_r.at[2 + d], group=up(g, NG - d, NG))
        send(ref, ref, vc_s.at[4 + d], vc_r.at[4 + d], shard=sc)
    q_arrive_y(0)
    q_forward_z(0)
    q_forward(0)
    arrive(slot(g, sc), vc_s.at[0], vc_r.at[0], shard=sc)
    arrive(slot(g, s3), vc_s.at[1], vc_r.at[1], shard=sc)
    for d in range(1, NG):
        arrive(slot(up(g, NG - d, NG), sc), vc_s.at[1 + d], vc_r.at[1 + d], shard=sc)
        arrive(slot(up(g, NG - d, NG), s3), vc_s.at[4 + d], vc_r.at[4 + d], shard=sc)

    spots = NG * NS * tok // MOST - 1
    first = 3 * rows + 2
    at_spot = [meta_ref[first + j : first + j + 1, :1].astype(f32).astype(bf16) for j in range(spots)]
    takes = [meta_ref[row : row + 1, :1].astype(f32).astype(bf16) for row in range(rows)]

    def place(i, c):
        dst = pl.ds(pl.multiple_of(i * HD, HD), HD)
        window = jnp.zeros((HD, 2 * HD), bf16)
        for j in range(spots):
            src = pl.ds(pl.multiple_of((1 + j) * MOST + i * HD, HD), HD)
            window = window + kv[src, :] * at_spot[j]
        for row in range(rows):
            old = 1 - takes[row]
            ck[row, dst, :] = ck[row, dst, :] * old + window[:, :HD] * takes[row]
            cv[row, dst, :] = cv[row, dst, :] * old + window[:, HD:] * takes[row]
        return c

    lax.fori_loop(0, 2 * MOST // HD, place, 0)

    def attend(u, c):
        h = lax.rem(u, heads)
        i = u // heads
        part = pl.ds(pl.multiple_of(i * QT, QT), QT)
        keys = pl.ds(pl.multiple_of((g * NS + s) * tok + i * QT, QT), KW)
        scores = lax.dot_general(qh[h, part, :], kv[keys, :HD], TRANS, preferred_element_type=f32)
        scores = scores + bias[i]
        high = jnp.max(scores, axis=1, keepdims=True)
        weights = jnp.exp2((scores - high) * (INV_ROOT * LOG2E))
        summed = jnp.sum(weights, axis=1, keepdims=True)
        mixed = jnp.dot(weights.astype(bf16), kv[keys, HD:], preferred_element_type=f32)
        cols = pl.ds(pl.multiple_of(h * HD, HD), HD)
        ctx_ref[part, cols] = (mixed / summed).astype(bf16)
        return c

    def attend_units(lo, hi):
        lax.fori_loop(lo, hi, attend, 0)

    def finish_queries():
        for h in range(heads):
            qh[h] = (acc_q[:, h * HD : (h + 1) * HD] * scale[...]).astype(bf16)

    def s2_early():
        q_arrive_y(1)
        q_forward_z(1)
        q_forward(1)

    def s2_late():
        for i in (2, 3):
            q_arrive_y(i)
            q_forward(i)

    def s2_sides(h):
        for i in (h, 2 + h):
            q_arrive_z(i)
            q_forward(4 + i)

    def s3_ready():
        for i in range(8):
            q_arrive_core(i)

    units = heads * (tok // QT)
    fills = {
        (0, 0): [s2_early],
        (0, 3): [s2_late, lambda: s2_sides(0)],
        (1, 0): [lambda: s2_sides(1)],
        (1, 1): [lambda: q_block(s2, False)],
        (1, 2): [s3_ready, lambda: q_block(s3, False)],
        (1, 3): [finish_queries, lambda: attend_units(0, 1)],
        (2, 0): [lambda: attend_units(1, 3)],
        (2, 1): [lambda: attend_units(3, 5)],
        (2, 2): [lambda: attend_units(5, 7)],
        (2, 3): [lambda: attend_units(7, 9)],
        (3, 0): [lambda: attend_units(9, 11)],
        (3, 1): [lambda: attend_units(11, 13)],
        (3, 2): [lambda: attend_units(13, units)],
    }

    def fill(k, i):
        for task in fills.get((k, i), []):
            task()

    cpos = lax.broadcasted_iota(jnp.int32, (heads, ck.shape[1]), 1)
    load_wo.wait()
    e_copies = []
    for k in range(STEPS):
        total = b_send[s]
        for d in range(1, NS):
            src = up(s, NS - d, NS)
            arrive(b_recv.at[src], r["b_s"].at[d - 1], r["b_r"].at[src], shard=src)
            total = total + b_recv[src]
        for c in b_copies:
            c.wait_send()
        norm = lax.rsqrt(total[:, qcols + 2 * HD : qcols + 2 * HD + 1] / width + EPSILON)
        fresh = (total[:, : qcols + 2 * HD] * norm).astype(bf16).astype(f32)
        fkv[k] = fresh[:, qcols:]
        for row in range(rows):
            for h in range(heads):
                qs[row, h : h + 1, :] = fresh[row : row + 1, h * HD : (h + 1) * HD]
        for row in range(rows):
            q = qs[row]
            valid = (cpos >= meta_ref[rows + row : rows + row + 1, :1]) & (
                cpos < meta_ref[2 * rows + row : 2 * rows + row + 1, :1]
            )
            scores = lax.dot_general(q.astype(bf16), ck[row], TRANS, preferred_element_type=f32) * INV_ROOT
            scores = jnp.where(valid, scores, -1e30)
            top = jnp.max(scores, axis=1, keepdims=True)
            news = []
            for j in range(k + 1):
                new = jnp.sum(q * fkv[j, row : row + 1, :HD], axis=1, keepdims=True) * INV_ROOT
                news.append(new)
                top = jnp.maximum(top, new)
            weights = jnp.where(valid, jnp.exp(scores - top), 0.0)
            summed = jnp.sum(weights, axis=1, keepdims=True)
            mixed = jnp.dot(weights.astype(bf16), cv[row], preferred_element_type=f32)
            for j in range(k + 1):
                weight = jnp.exp(news[j] - top)
                summed = summed + weight
                mixed = mixed + weight.astype(bf16).astype(f32) * fkv[j, row : row + 1, HD:]
            context = (mixed / summed).astype(bf16).astype(f32)
            for h in range(heads):
                c_send[row : row + 1, h * HD : (h + 1) * HD] = context[h : h + 1]

        copies = []
        for d in range(1, NS):
            p = up(s, d, NS)
            c = remote(c_send, c_recv.at[s], r["c_s"].at[d - 1], r["c_r"].at[s], shard=p)
            c.start()
            copies.append(c)
        c_recv[s] = c_send[...]
        fill(k, 0)
        for d in range(1, NS):
            src = up(s, NS - d, NS)
            arrive(c_recv.at[src], r["c_s"].at[d - 1], r["c_r"].at[src], shard=src)
        for c in copies:
            c.wait_send()
        block = jnp.concatenate([c_recv[i] for i in range(NS)], axis=0).astype(bf16)
        for i in range(NT):
            d_send[i] = jnp.dot(block, wo[:, i * piece : (i + 1) * piece], preferred_element_type=f32).astype(bf16)

        copies = []
        for d in range(1, NT):
            p = up(t, d, NT)
            c = remote(d_send.at[p], d_recv.at[t], r["d_s"].at[d - 1], r["d_r"].at[t], tensor=p)
            c.start()
            copies.append(c)
        fill(k, 1)
        update = d_send[t].astype(f32)
        for d in range(1, NT):
            src = up(t, NT - d, NT)
            arrive(d_recv.at[src], r["d_s"].at[d - 1], r["d_r"].at[src], tensor=src)
            update = update + d_recv[src].astype(f32)
        for c in copies:
            c.wait_send()
        after = state[...] + update
        state[...] = after
        xu_send[:, :piece] = after.astype(bf16)
        xu_send[:, piece:] = update.astype(bf16)
        copies = []
        for d in range(1, NT):
            p = up(t, d, NT)
            c = remote(xu_send, xu.at[t], r["x_s"].at[d - 1], r["x_r"].at[t], tensor=p)
            c.start()
            copies.append(c)
        xu[t] = xu_send[...]
        fill(k, 2)
        for d in range(1, NT):
            src = up(t, NT - d, NT)
            arrive(xu.at[src], r["x_s"].at[d - 1], r["x_r"].at[src], tensor=src)
        for c in copies:
            c.wait_send()
        if k < STEPS - 1:
            b_copies = decode_project()
        for i in range(NT):
            u = xu[i, :, piece:].astype(f32)
            for j in range(NS):
                e_send[k, j, :, i * piece : (i + 1) * piece] = u[j * rows : (j + 1) * rows]
        for d in range(1, NS):
            p = up(s, d, NS)
            send(e_send.at[k, p], e_recv.at[k, s], r["e_s"].at[k, d - 1], r["e_r"].at[k, s], shard=p)
        e_recv[k, s] = e_send[k, s]
        fill(k, 3)

    for k in range(STEPS):
        for d in range(1, NS):
            src = up(s, NS - d, NS)
            arrive(e_recv.at[k, src], r["e_s"].at[k, d - 1], r["e_r"].at[k, src], shard=src)
        for i in range(NS):
            out_ref[k, :, i * dblk : (i + 1) * dblk] = e_recv[k, i].astype(bf16)
    for c in sent:
        c.wait_send()


def layer(meta, states, x, wkv, wq, wo, cache):
    rows, dblk = states.shape[1:]
    tok, width = x.shape
    qcols = wq.shape[1]
    piece = dblk // NT
    heads = qcols // HD
    vm = pltpu.VMEM
    dma = pltpu.SemaphoreType.DMA
    bw = qcols + 3 * HD
    scratch = dict(
        xv=vm((tok, width), bf16),
        wkv=vm((NS, dblk, 2 * HD), bf16),
        wq=vm((NS, dblk, qcols), bf16),
        wo=vm(wo.shape, bf16),
        raw=vm(cache.shape, bf16),
        ck=vm((rows, CACHE, HD), bf16),
        cv=vm((rows, CACHE, HD), bf16),
        kv=vm((MOST + NG * NS * tok, 2 * HD), bf16),
        qh=vm((heads, tok, HD), bf16),
        acc_q=vm((tok, qcols), f32),
        acc_kv=vm((tok, 2 * HD), f32),
        scale=vm((tok, HD), f32),
        bias=vm((tok // QT, QT, KW), f32),
        a_recv=vm((NS, rows, dblk), f32),
        xu=vm((NT, NS * rows, 2 * piece), bf16),
        xu_send=vm((NS * rows, 2 * piece), bf16),
        state=vm((NS * rows, piece), f32),
        b_send=vm((NS, rows, bw), f32),
        b_recv=vm((NS, rows, bw), f32),
        qs=vm((rows, heads, HD), f32),
        fkv=vm((STEPS, rows, 2 * HD), f32),
        c_send=vm((rows, qcols), f32),
        c_recv=vm((NS, rows, qcols), f32),
        d_send=vm((NT, NS * rows, piece), bf16),
        d_recv=vm((NT, NS * rows, piece), bf16),
        e_send=vm((STEPS, NS, rows, dblk), f32),
        e_recv=vm((STEPS, NS, rows, dblk), f32),
        lsem=dma((5,)),
        ky_s=dma((2,)),
        ky_r=dma((2,)),
        kz_s=dma((2,)),
        kz_r=dma((2,)),
        kc_s=dma((5,)),
        kc_r=dma((5,)),
        qy_s=dma((4,)),
        qy_r=dma((4,)),
        qz_s=dma((4,)),
        qz_r=dma((4,)),
        qc_s=dma((9,)),
        qc_r=dma((9,)),
        vy_s=dma((1,)),
        vy_r=dma((1,)),
        vz_s=dma((6,)),
        vz_r=dma((6,)),
        vc_s=dma((8,)),
        vc_r=dma((8,)),
        a_s=dma((NS - 1,)),
        a_r=dma((NS,)),
        b_s=dma((NS - 1,)),
        b_r=dma((NS,)),
        c_s=dma((NS - 1,)),
        c_r=dma((NS,)),
        d_s=dma((NT - 1,)),
        d_r=dma((NT,)),
        x_s=dma((NT - 1,)),
        x_r=dma((NT,)),
        e_s=dma((STEPS, NS - 1)),
        e_r=dma((STEPS, NS)),
    )
    vmem = pl.BlockSpec(memory_space=pltpu.VMEM)
    hbm = pl.BlockSpec(memory_space=pl.ANY)
    return pl.pallas_call(
        functools.partial(kernel, tuple(scratch)),
        out_shape=(
            jax.ShapeDtypeStruct((tok, qcols), bf16),
            jax.ShapeDtypeStruct((STEPS, rows, width), bf16),
        ),
        in_specs=[vmem, vmem, hbm, hbm, hbm, hbm, hbm],
        out_specs=(vmem, vmem),
        scratch_shapes=list(scratch.values()),
        compiler_params=pltpu.CompilerParams(
            collective_id=0, has_side_effects=True, vmem_limit_bytes=62 * 1024 * 1024
        ),
        name="attention_layer",
    )(meta, states, x, wkv, wq, wo, cache)


def body(
    prompt_states,
    prompt_lens,
    w_query,
    w_keyval,
    w_out,
    decode_states,
    kv_cache,
    cache_len,
    row_prompt,
):
    group_index = lax.axis_index("group")
    dblk = w_query.shape[0]
    rows, width = decode_states.shape
    kv_cols = w_keyval.shape[2]
    tokens = NG * NS * prompt_states.shape[0]
    lens = prompt_lens.reshape(-1)
    count = lens.shape[0]
    index = jnp.arange(count, dtype=jnp.int32)
    starts = jnp.sum(jnp.where(index[None, :] < index[:, None], lens[None, :], 0), axis=1)
    onehot = row_prompt[:, None] == index[None, :]
    is_new = jnp.any(onehot, axis=1)
    first = jnp.sum(jnp.where(onehot, starts[None, :], 0))
    length = jnp.sum(jnp.where(onehot, lens[None, :], 0))
    spots = tokens // MOST - 1
    spot = jnp.minimum(first // MOST, spots - 1)
    base = spot * MOST
    low = jnp.where(is_new, first - base, 0)
    high = jnp.where(is_new, first - base + length, cache_len)
    mine = jnp.arange(prompt_lens.shape[0], dtype=jnp.int32) == group_index
    own = jnp.sum(jnp.where(mine[:, None], prompt_lens, 0), axis=0)
    bounds = jnp.stack([own[0], own[0] + own[1]])
    at_spot = (jnp.arange(spots, dtype=jnp.int32) == spot).astype(jnp.int32)
    meta = jnp.concatenate([is_new.astype(jnp.int32), low, high, bounds, at_spot])
    meta = jnp.pad(meta, (0, 24 - meta.shape[0]))
    states = jnp.transpose(decode_states.astype(f32).reshape(rows, NS, dblk), (1, 0, 2))
    return layer(
        jnp.broadcast_to(meta[:, None], (24, HD)),
        states,
        prompt_states,
        w_keyval.reshape(dblk, 2 * kv_cols),
        w_query,
        w_out,
        kv_cache.reshape(rows, 2 * CACHE, kv_cols),
    )


def solution(mesh):
    in_specs = (
        P(("group", "shard"), None),
        P(),
        P("shard", "tensor"),
        P("shard", None, "tensor"),
        P("tensor", "shard"),
        P(("group", "shard"), None),
        P(("group", "shard"), None, None, "tensor"),
        P(("group", "shard")),
        P(("group", "shard")),
    )
    out_specs = (P(("group", "shard"), "tensor"), P(None, ("group", "shard"), None))
    return jax.shard_map(body, mesh=mesh, in_specs=in_specs, out_specs=out_specs, check_vma=False)
```

```python
import functools

import jax
import jax.numpy as jnp
from jax import lax
from jax.experimental import pallas as pl
from jax.experimental.pallas import tpu as pltpu
from jax.sharding import PartitionSpec as P

HD = 128
CACHE = 2048
STEPS = 4
EPSILON = 1e-05
MESH = pl.DeviceIdType.MESH
NG = 4
NS = 4
NT = 8
MOST = 1024
QT = 256
KW = QT + MOST
INV_ROOT = HD**-0.5
LOG2E = 1.4426950408889634
TRANS = (((1,), (1,)), ((), ()))
f32 = jnp.float32
bf16 = jnp.bfloat16


def kernel(names, lens_ref, rowp_ref, clen_ref, ds_ref, x_hbm, wkv_hbm, wq_hbm, wo_hbm, cache_hbm, ctx_ref, out_ref, *scratch):
    r = dict(zip(names, scratch))
    xv, wkv, wq, wo, raw, ck, cv = (r[n] for n in ("xv", "wkv", "wq", "wo", "raw", "ck", "cv"))
    kv, qh, acc_q, acc_kv, scale, bias = (r[n] for n in ("kv", "qh", "acc_q", "acc_kv", "scale", "bias"))
    a_recv, xu, xu_send, state = (r[n] for n in ("a_recv", "xu", "xu_send", "state"))
    b_send, b_recv, qs, fkv = (r[n] for n in ("b_send", "b_recv", "qs", "fkv"))
    c_send, c_recv, d_send, d_recv = (r[n] for n in ("c_send", "c_recv", "d_send", "d_recv"))
    e_send, e_recv = r["e_send"], r["e_recv"]

    g = lax.axis_index("group")
    s = lax.axis_index("shard")
    t = lax.axis_index("tensor")
    sc = s + 1 - 2 * lax.rem(s, 2)
    s2 = lax.rem(s + 2, NS)
    s3 = lax.rem(sc + 2, NS)
    tok = xv.shape[0]
    rows = ds_ref.shape[0]
    dblk, qcols = wq.shape[1:]
    piece = dblk // NT
    heads = qcols // HD
    width = NS * dblk
    quarter = dblk // NG
    half = quarter // 2

    def up(base, d, n):
        return lax.rem(base + d, n)

    def remote(src, dst, ssem, rsem, **where):
        return pltpu.make_async_remote_copy(
            src_ref=src, dst_ref=dst, send_sem=ssem, recv_sem=rsem, device_id=where, device_id_type=MESH
        )

    sent = []

    def send(src, dst, ssem, rsem, **where):
        c = remote(src, dst, ssem, rsem, **where)
        c.start()
        sent.append(c)
        return c

    def arrive(dst, ssem, rsem, **where):
        remote(dst, dst, ssem, rsem, **where).wait_recv()

    def load(a, b, i):
        c = pltpu.make_async_copy(a, b, r["lsem"].at[i])
        c.start()
        return c

    load_wkv = load(wkv_hbm, r["kraw"], 1)
    load_x = load(x_hbm, xv, 0)
    load_wq = load(wq_hbm, wq.at[s], 2)

    barrier = pltpu.get_barrier_semaphore()
    for d in range(1, NS):
        pl.semaphore_signal(barrier, inc=1, device_id={"shard": up(s, d, NS)}, device_id_type=MESH)
    for d in range(1, NG):
        pl.semaphore_signal(barrier, inc=1, device_id={"group": up(g, d, NG)}, device_id_type=MESH)
    for d in range(1, NT):
        pl.semaphore_signal(barrier, inc=1, device_id={"tensor": up(t, d, NT)}, device_id_type=MESH)

    begin = jnp.int32(0)
    prompts = NG * lens_ref.shape[1]
    starts = [jnp.int32(0)] * rows
    sizes = [jnp.int32(0)] * rows
    for i in range(prompts):
        here = lens_ref[i // lens_ref.shape[1], i % lens_ref.shape[1]]
        for row in range(rows):
            hit = (rowp_ref[row] == i).astype(jnp.int32)
            starts[row] = starts[row] + hit * begin
            sizes[row] = sizes[row] + hit * here
        begin = begin + here
    b0 = lens_ref[g, 0]
    b1 = b0 + lens_ref[g, 1]
    is_new = [(rowp_ref[row] < prompts).astype(jnp.int32) for row in range(rows)]
    spots = NG * NS * tok // MOST - 1
    begin = sum(starts)
    spot = jnp.minimum(begin // MOST, spots - 1)
    low = [is_new[row] * (starts[row] - spot * MOST) for row in range(rows)]
    high = [low[row] + is_new[row] * sizes[row] + (1 - is_new[row]) * clen_ref[row] for row in range(rows)]

    out_i = lax.broadcasted_iota(jnp.int32, (256, 256), 0)
    in_i = lax.broadcasted_iota(jnp.int32, (256, 256), 1)
    want = jnp.where(out_i < 128, 2 * out_i, 2 * (out_i - 128) + 1)
    pick = (in_i == want).astype(bf16)

    load_wkv.wait()

    def separate_weights(i, c):
        pair = jnp.concatenate(
            [r["kraw"][pl.ds(pl.multiple_of((2 * i + j) * 256, 256), 256), :] for j in range(2)], axis=1
        )
        split = jnp.dot(pick, pair, preferred_element_type=f32).astype(bf16)
        for j in range(2):
            dst = pl.ds(pl.multiple_of((2 * i + j) * 128, 128), 128)
            wkv[s, dst, :] = jnp.concatenate(
                [split[:128, j * HD : (j + 1) * HD], split[128:, j * HD : (j + 1) * HD]], axis=1
            )
        return c

    lax.fori_loop(0, dblk // 256, separate_weights, 0)
    ds = r["ds"]
    for i in range(NS):
        ds[i] = ds_ref[:, i * dblk : (i + 1) * dblk].astype(f32)
    pl.semaphore_wait(barrier, NS - 1 + NG - 1 + NT - 1)

    def krows(blk, q):
        return wkv.at[blk, pl.ds(pl.multiple_of(q * quarter, quarter), quarter)]

    def qrows(blk, q, h):
        return wq.at[blk, pl.ds(pl.multiple_of(q * quarter + h * half, half), half)]

    q_of = [g, up(g, 2, NG), up(g, 3, NG), up(g, 1, NG)]
    ky_s, ky_r, kz_s, kz_r, kc_s, kc_r = (r[n] for n in ("ky_s", "ky_r", "kz_s", "kz_r", "kc_s", "kc_r"))
    qy_s, qy_r, qz_s, qz_r, qc_s, qc_r = (r[n] for n in ("qy_s", "qy_r", "qz_s", "qz_r", "qc_s", "qc_r"))

    for i in range(2):
        send(krows(s, q_of[i]), krows(s, q_of[i]), ky_s.at[i], ky_r.at[i], shard=s2)
    send(wkv.at[s], wkv.at[s], kc_s.at[4], kc_r.at[4], shard=sc)
    for d in range(1, NS):
        p = up(s, d, NS)
        send(ds.at[p], a_recv.at[s], r["a_s"].at[d - 1], r["a_r"].at[s], shard=p)
    send(wq_hbm, wq.at[s], qc_s.at[8], qc_r.at[8], shard=sc)
    a_recv[s] = ds[s]
    r["fkv"][...] = jnp.zeros_like(fkv)
    kv[:MOST, :] = jnp.zeros((MOST, 2 * HD), bf16)

    def k_arrive_y(i):
        arrive(krows(s2, q_of[i]), ky_s.at[i], ky_r.at[i], shard=s2)

    def k_arrive_z(i):
        arrive(krows(s2, q_of[2 + i]), kz_s.at[i], kz_r.at[i], group=q_of[2 + i])

    def k_forward(role):
        ref = krows(s2, q_of[role])
        send(ref, ref, kc_s.at[role], kc_r.at[role], shard=sc)

    def k_forward_z():
        ref = krows(s2, g)
        send(ref, ref, kz_s.at[0], kz_r.at[0], group=up(g, 1, NG))
        send(ref, ref, kz_s.at[1], kz_r.at[1], group=up(g, 3, NG))

    def q_send_y(i):
        ref = qrows(s, g, i)
        send(ref, ref, qy_s.at[i], qy_r.at[i], shard=s2)

    def q_arrive_y(i):
        arrive(qrows(s2, g, i), qy_s.at[i], qy_r.at[i], shard=s2)

    def q_second(h):
        ref = qrows(s2, q_of[2 + h], h)
        send(ref, ref, qz_s.at[4 + h], qz_r.at[4 + h], group=up(g, 1 + 2 * h, NG))

    def q_arrive_second(h):
        arrive(qrows(s2, q_of[1], h), qz_s.at[4 + h], qz_r.at[4 + h], group=q_of[2 + h])

    def q_forward_z(h):
        ref = qrows(s2, g, h)
        send(ref, ref, qz_s.at[h], qz_r.at[h], group=up(g, 1, NG))
        send(ref, ref, qz_s.at[2 + h], qz_r.at[2 + h], group=up(g, 3, NG))

    def q_arrive_z(i):
        arrive(qrows(s2, q_of[2 + i // 2], i % 2), qz_s.at[i], qz_r.at[i], group=q_of[2 + i // 2])

    def q_forward(i):
        ref = qrows(s2, q_of[i // 2], i % 2)
        send(ref, ref, qc_s.at[i], qc_r.at[i], shard=sc)

    def q_arrive_core(i):
        arrive(qrows(s3, q_of[i // 2], i % 2), qc_s.at[i], qc_r.at[i], shard=sc)

    def x_block(blk):
        return xv[:, pl.ds(pl.multiple_of(blk * dblk, dblk), dblk)]

    def kv_block(blk, first):
        prod = jnp.dot(x_block(blk), wkv[blk], preferred_element_type=f32)
        acc_kv[...] = prod if first else acc_kv[...] + prod

    def q_block(blk, first, lo=0, hi=None):
        hi = qcols // 256 if hi is None else hi

        def part(n, c):
            cols = pl.ds(pl.multiple_of(n * 256, 256), 256)
            prod = jnp.dot(x_block(blk), wq[blk, :, cols], preferred_element_type=f32)
            acc_q[:, cols] = prod if first else acc_q[:, cols] + prod
            return c

        lax.fori_loop(lo, hi, part, 0)

    load_x.wait()
    load_raw = load(cache_hbm, raw, 3)
    load_wo = load(wo_hbm, wo, 4)

    def squares(i, c):
        part = pl.ds(pl.multiple_of(i * 32, 32), 32)
        v = xv[part, :].astype(f32)
        mean = jnp.sum(v * v, axis=1, keepdims=True) / width
        scale[part, :] = jnp.broadcast_to(lax.rsqrt(mean + EPSILON), (32, HD))
        return c

    lax.fori_loop(0, tok // 32, squares, 0)
    kv_block(s, True)

    k_arrive_y(0)
    k_forward_z()
    k_forward(0)

    for d in range(1, NS):
        src = up(s, NS - d, NS)
        arrive(a_recv.at[src], r["a_s"].at[d - 1], r["a_r"].at[src], shard=src)
    x0 = jnp.concatenate([a_recv[i] for i in range(NS)], axis=0)
    for i in range(NT):
        xu[i] = x0[:, i * piece : (i + 1) * piece].astype(bf16)
    mine = pl.ds(pl.multiple_of(t * piece, piece), piece)
    state[...] = jnp.concatenate([a_recv[i, :, mine] for i in range(NS)], axis=0)

    load_wq.wait()
    q_block(s, True)

    k_arrive_y(1)
    k_forward(1)
    arrive(wkv.at[sc], kc_s.at[4], kc_r.at[4], shard=sc)
    kv_block(sc, False)
    k_arrive_z(0)
    k_forward(2)
    k_arrive_z(1)
    k_forward(3)
    kv_block(s2, False)
    for role in range(4):
        arrive(krows(s3, q_of[role]), kc_s.at[role], kc_r.at[role], shard=sc)
    kv_block(s3, False)

    def slot(gg, ss):
        return kv.at[pl.ds(pl.multiple_of(MOST + (gg * NS + ss) * tok, tok), tok)]

    both = jnp.concatenate([scale[...], scale[...]], axis=1)
    kv[pl.ds(pl.multiple_of(MOST + (g * NS + s) * tok, tok), tok), :] = (acc_kv[...] * both).astype(bf16)
    vy_s, vy_r, vz_s, vz_r, vc_s, vc_r = (r[n] for n in ("vy_s", "vy_r", "vz_s", "vz_r", "vc_s", "vc_r"))
    below, above = up(g, 3, NG), up(g, 1, NG)

    def half_slot(gg, ss, h):
        n = tok // 2
        return kv.at[pl.ds(pl.multiple_of(MOST + (gg * NS + ss) * tok + h * n, n), n)]

    def v_core(ref, i):
        send(ref, ref, vc_s.at[i], vc_r.at[i], shard=sc)

    def v_sides(ss, i):
        ref = slot(g, ss)
        send(ref, ref, vz_s.at[i], vz_r.at[i], group=above)
        send(ref, ref, vz_s.at[i + 1], vz_r.at[i + 1], group=below)

    def v_pass(ss, i, core):
        for h, (source, target) in enumerate([(below, above), (above, below)]):
            arrive(slot(source, ss), vz_s.at[i + h], vz_r.at[i + h], group=source)
            ref = half_slot(source, ss, h)
            send(ref, ref, vz_s.at[i + 4 + h], vz_r.at[i + 4 + h], group=target)
            v_core(slot(source, ss), core + h)

    def v_last(ss, i, core):
        for h, source in enumerate([below, above]):
            ref = half_slot(up(g, 2, NG), ss, h)
            arrive(ref, vz_s.at[i + 4 + h], vz_r.at[i + 4 + h], group=source)
            v_core(ref, core + h)

    own = slot(g, s)
    send(own, own, vy_s.at[0], vy_r.at[0], shard=s2)
    v_sides(s, 0)
    v_core(own, 0)
    q_send_y(0)
    q_send_y(1)

    def decode_project():
        acc = jnp.zeros((NS * rows, qcols), f32)
        acc2 = jnp.zeros((NS * rows, 2 * HD), f32)
        square = jnp.zeros((NS * rows, 1), f32)
        for i in range(NT):
            xi = xu[i]
            acc += jnp.dot(xi, wq[s, i * piece : (i + 1) * piece, :], preferred_element_type=f32)
            acc2 += jnp.dot(xi, wkv[s, i * piece : (i + 1) * piece, :], preferred_element_type=f32)
            xf = xi.astype(f32)
            square += jnp.sum(xf * xf, axis=1, keepdims=True)
        wide = jnp.broadcast_to(square, (NS * rows, HD))
        for i in range(NS):
            b_send[i, :, :qcols] = acc[i * rows : (i + 1) * rows]
            b_send[i, :, qcols : qcols + 2 * HD] = acc2[i * rows : (i + 1) * rows]
            b_send[i, :, qcols + 2 * HD :] = wide[i * rows : (i + 1) * rows]
        copies = []
        for d in range(1, NS):
            p = up(s, d, NS)
            c = remote(b_send.at[p], b_recv.at[s], r["b_s"].at[d - 1], r["b_r"].at[s], shard=p)
            c.start()
            copies.append(c)
        return copies

    b_copies = decode_project()

    load_raw.wait()
    def separate(i, c):
        src = pl.ds(pl.multiple_of(i * 256, 256), 256)
        dst = pl.ds(pl.multiple_of(i * 128, 128), 128)
        for row in range(0, rows, 2):
            pair = jnp.concatenate([raw[row, src, :], raw[row + 1, src, :]], axis=1)
            split = jnp.dot(pick, pair, preferred_element_type=f32).astype(bf16)
            for j in range(2):
                ck[row + j, dst, :] = split[:128, j * HD : (j + 1) * HD]
                cv[row + j, dst, :] = split[128:, j * HD : (j + 1) * HD]
        return c

    lax.fori_loop(0, 2 * ck.shape[1] // 256, separate, 0)
    arrive(wq.at[sc], qc_s.at[8], qc_r.at[8], shard=sc)
    q_block(sc, False)

    for i in range(tok // QT):
        q_pos = s * tok + i * QT + lax.broadcasted_iota(jnp.int32, (QT, KW), 0)
        k_pos = s * tok + i * QT - MOST + lax.broadcasted_iota(jnp.int32, (QT, KW), 1)
        start = jnp.where(q_pos >= b1, b1, jnp.where(q_pos >= b0, b0, 0))
        bias[i] = jnp.where((k_pos >= start) & (k_pos <= q_pos), 0.0, -1e30)

    arrive(slot(g, s2), vy_s.at[0], vy_r.at[0], shard=s2)
    v_sides(s2, 2)
    v_core(slot(g, s2), 1)
    v_pass(s, 0, 2)
    v_pass(s2, 2, 4)
    v_last(s, 0, 6)
    v_last(s2, 2, 8)
    for i, ref in enumerate(
        [slot(g, sc), slot(g, s3)]
        + [slot(gg, ss) for ss in (sc, s3) for gg in (below, above)]
        + [half_slot(up(g, 2, NG), ss, h) for ss in (sc, s3) for h in range(2)]
    ):
        arrive(ref, vc_s.at[i], vc_r.at[i], shard=sc)
    q_arrive_y(0)
    q_forward_z(0)
    q_forward(0)

    def splat(flag):
        return jnp.broadcast_to(flag, (HD, HD)).astype(f32).astype(bf16)

    at_spot = [splat((spot == j).astype(jnp.int32)) for j in range(spots)]
    at_spot = [jnp.concatenate([v, v], axis=1) for v in at_spot]
    takes = [splat(is_new[row]) for row in range(rows)]

    def place(i, c):
        dst = pl.ds(pl.multiple_of(i * HD, HD), HD)
        window = jnp.zeros((HD, 2 * HD), bf16)
        for j in range(spots):
            src = pl.ds(pl.multiple_of((1 + j) * MOST + i * HD, HD), HD)
            window = window + kv[src, :] * at_spot[j]
        for row in range(rows):
            old = 1 - takes[row]
            ck[row, dst, :] = ck[row, dst, :] * old + window[:, :HD] * takes[row]
            cv[row, dst, :] = cv[row, dst, :] * old + window[:, HD:] * takes[row]
        return c

    lax.fori_loop(0, 2 * MOST // HD, place, 0)

    def attend(u, c):
        h = lax.rem(u, heads)
        i = u // heads
        part = pl.ds(pl.multiple_of(i * QT, QT), QT)
        keys = pl.ds(pl.multiple_of((g * NS + s) * tok + i * QT, QT), KW)
        scores = lax.dot_general(qh[h, part, :], kv[keys, :HD], TRANS, preferred_element_type=f32)
        scores = scores + bias[i]
        high = jnp.max(scores, axis=1, keepdims=True)
        weights = jnp.exp2((scores - high) * (INV_ROOT * LOG2E))
        summed = jnp.sum(weights, axis=1, keepdims=True)
        mixed = jnp.dot(weights.astype(bf16), kv[keys, HD:], preferred_element_type=f32)
        cols = pl.ds(pl.multiple_of(h * HD, HD), HD)
        ctx_ref[part, cols] = (mixed / summed).astype(bf16)
        return c

    def attend_units(lo, hi):
        lax.fori_loop(lo, hi, attend, 0)

    def finish_queries():
        for h in range(heads):
            qh[h] = (acc_q[:, h * HD : (h + 1) * HD] * scale[...]).astype(bf16)

    def s2_early():
        q_arrive_y(1)
        q_forward_z(1)
        q_forward(1)

    def s2_sides(h):
        for i in (h, 2 + h):
            q_arrive_z(i)
            q_forward(4 + i)
        q_second(h)

    def s2_last():
        for h in range(2):
            q_arrive_second(h)
            q_forward(2 + h)

    def s3_ready():
        for i in range(8):
            q_arrive_core(i)

    units = heads * (tok // QT)
    fills = {
        (0, 1): [s2_early],
        (0, 3): [lambda: s2_sides(0)],
        (1, 1): [lambda: s2_sides(1)],
        (2, 0): [s2_last, lambda: q_block(s2, False)],
        (2, 1): [s3_ready, lambda: q_block(s3, False)],
        (2, 2): [finish_queries, lambda: attend_units(0, 2)],
        (2, 3): [lambda: attend_units(2, 5)],
        (3, 0): [lambda: attend_units(5, 8)],
        (3, 1): [lambda: attend_units(8, 12)],
        (3, 2): [lambda: attend_units(12, units)],
    }

    def fill(k, i):
        for task in fills.get((k, i), []):
            task()

    def all_shards(src_of, dst, ssem, rsem):
        copies = []
        for d in range(1, NS):
            p = up(s, d, NS)
            c = remote(src_of(p), dst, ssem.at[d - 1], rsem, shard=p)
            c.start()
            copies.append(c)
        return copies

    def all_tensors(src_of, dst, ssem, rsem):
        copies = []
        for d in (4, 6, 2, 5, 3, 7, 1):
            p = up(t, d, NT)
            c = remote(src_of(p), dst, ssem.at[d - 1], rsem, tensor=p)
            c.start()
            copies.append(c)
        return copies

    def settle(copies):
        for c in copies:
            c.wait_send()

    u_send, u_recv = r["u_send"], r["u_recv"]

    def give_update(k):
        sent.extend(all_tensors(lambda p: u_send.at[k], u_recv.at[k, t], r["u_s"].at[k], r["u_r"].at[k, t]))
        u_recv[k, t] = u_send[k]

    def spread_update(k):
        for d in range(1, NT):
            src = up(t, NT - d, NT)
            arrive(u_recv.at[k, src], r["u_s"].at[k, d - 1], r["u_r"].at[k, src], tensor=src)
        for i in range(NT):
            u = u_recv[k, i].astype(f32)
            for j in range(NS):
                e_send[k, j, :, i * piece : (i + 1) * piece] = u[j * rows : (j + 1) * rows]
        sent.extend(all_shards(lambda p: e_send.at[k, p], e_recv.at[k, s], r["e_s"].at[k], r["e_r"].at[k, s]))
        e_recv[k, s] = e_send[k, s]

    cpos = lax.broadcasted_iota(jnp.int32, (heads, ck.shape[1]), 1)
    load_wo.wait()
    for k in range(STEPS):
        total = b_send[s]
        for d in range(1, NS):
            src = up(s, NS - d, NS)
            arrive(b_recv.at[src], r["b_s"].at[d - 1], r["b_r"].at[src], shard=src)
            total = total + b_recv[src]
        norm = lax.rsqrt(total[:, qcols + 2 * HD : qcols + 2 * HD + 1] / width + EPSILON)
        fresh = (total[:, : qcols + 2 * HD] * norm).astype(bf16).astype(f32)
        fkv[k] = fresh[:, qcols:]
        for row in range(rows):
            for h in range(heads):
                qs[row, h : h + 1, :] = fresh[row : row + 1, h * HD : (h + 1) * HD]
        for row in range(rows):
            q = qs[row]
            valid = (cpos >= low[row]) & (cpos < high[row])
            scores = lax.dot_general(q.astype(bf16), ck[row], TRANS, preferred_element_type=f32) * INV_ROOT
            scores = jnp.where(valid, scores, -1e30)
            top = jnp.max(scores, axis=1, keepdims=True)
            news = []
            for j in range(k + 1):
                new = jnp.sum(q * fkv[j, row : row + 1, :HD], axis=1, keepdims=True) * INV_ROOT
                news.append(new)
                top = jnp.maximum(top, new)
            weights = jnp.where(valid, jnp.exp(scores - top), 0.0)
            summed = jnp.sum(weights, axis=1, keepdims=True)
            mixed = jnp.dot(weights.astype(bf16), cv[row], preferred_element_type=f32)
            for j in range(k + 1):
                weight = jnp.exp(news[j] - top)
                summed = summed + weight
                mixed = mixed + weight.astype(bf16).astype(f32) * fkv[j, row : row + 1, HD:]
            context = (mixed / summed).astype(bf16).astype(f32)
            for h in range(heads):
                c_send[row : row + 1, h * HD : (h + 1) * HD] = context[h : h + 1]

        c_copies = all_shards(lambda p: c_send, c_recv.at[s], r["c_s"], r["c_r"].at[s])
        c_recv[s] = c_send[...]
        settle(b_copies)
        fill(k, 0)
        for d in range(1, NS):
            src = up(s, NS - d, NS)
            arrive(c_recv.at[src], r["c_s"].at[d - 1], r["c_r"].at[src], shard=src)
        block = jnp.concatenate([c_recv[i] for i in range(NS)], axis=0).astype(bf16)
        for i in range(NT):
            d_send[i] = jnp.dot(block, wo[:, i * piece : (i + 1) * piece], preferred_element_type=f32).astype(bf16)

        d_copies = all_tensors(lambda p: d_send.at[p], d_recv.at[t], r["d_s"], r["d_r"].at[t])
        settle(c_copies)
        if k > 0:
            spread_update(k - 1)
        fill(k, 1)
        update = d_send[t].astype(f32)
        for d in range(1, NT):
            src = up(t, NT - d, NT)
            arrive(d_recv.at[src], r["d_s"].at[d - 1], r["d_r"].at[src], tensor=src)
            update = update + d_recv[src].astype(f32)
        u_send[k] = update.astype(bf16)
        if k == STEPS - 1:
            give_update(k)
            settle(d_copies)
            fill(k, 2)
            spread_update(k)
            break
        after = state[...] + update
        state[...] = after
        xu_send[...] = after.astype(bf16)
        x_copies = all_tensors(lambda p: xu_send, xu.at[t], r["x_s"], r["x_r"].at[t])
        xu[t] = xu_send[...]
        settle(d_copies)
        fill(k, 2)
        for d in range(1, NT):
            src = up(t, NT - d, NT)
            arrive(xu.at[src], r["x_s"].at[d - 1], r["x_r"].at[src], tensor=src)
        b_copies = decode_project()
        settle(x_copies)
        give_update(k)
        fill(k, 3)

    for k in range(STEPS):
        for d in range(1, NS):
            src = up(s, NS - d, NS)
            arrive(e_recv.at[k, src], r["e_s"].at[k, d - 1], r["e_r"].at[k, src], shard=src)
        for i in range(NS):
            out_ref[k, :, i * dblk : (i + 1) * dblk] = e_recv[k, i].astype(bf16)
    settle(sent)


def layer(lens, row_prompt, cache_len, states, x, wkv, wq, wo, cache):
    rows = states.shape[0]
    tok, width = x.shape
    dblk, qcols = wq.shape
    piece = dblk // NT
    heads = qcols // HD
    vm = pltpu.VMEM
    dma = pltpu.SemaphoreType.DMA
    bw = qcols + 3 * HD
    scratch = dict(
        xv=vm((tok, width), bf16),
        wkv=vm((NS, dblk, 2 * HD), bf16),
        wq=vm((NS, dblk, qcols), bf16),
        wo=vm(wo.shape, bf16),
        raw=vm(cache.shape, bf16),
        ck=vm((rows, CACHE, HD), bf16),
        cv=vm((rows, CACHE, HD), bf16),
        kv=vm((MOST + NG * NS * tok, 2 * HD), bf16),
        qh=vm((heads, tok, HD), bf16),
        acc_q=vm((tok, qcols), f32),
        acc_kv=vm((tok, 2 * HD), f32),
        scale=vm((tok, HD), f32),
        bias=vm((tok // QT, QT, KW), f32),
        kraw=vm((2 * dblk, HD), bf16),
        ds=vm((NS, rows, dblk), f32),
        a_recv=vm((NS, rows, dblk), f32),
        xu=vm((NT, NS * rows, piece), bf16),
        xu_send=vm((NS * rows, piece), bf16),
        u_send=vm((STEPS, NS * rows, piece), bf16),
        u_recv=vm((STEPS, NT, NS * rows, piece), bf16),
        state=vm((NS * rows, piece), f32),
        b_send=vm((NS, rows, bw), f32),
        b_recv=vm((NS, rows, bw), f32),
        qs=vm((rows, heads, HD), f32),
        fkv=vm((STEPS, rows, 2 * HD), f32),
        c_send=vm((rows, qcols), f32),
        c_recv=vm((NS, rows, qcols), f32),
        d_send=vm((NT, NS * rows, piece), bf16),
        d_recv=vm((NT, NS * rows, piece), bf16),
        e_send=vm((STEPS, NS, rows, dblk), f32),
        e_recv=vm((STEPS, NS, rows, dblk), f32),
        lsem=dma((5,)),
        ky_s=dma((2,)),
        ky_r=dma((2,)),
        kz_s=dma((2,)),
        kz_r=dma((2,)),
        kc_s=dma((5,)),
        kc_r=dma((5,)),
        qy_s=dma((2,)),
        qy_r=dma((2,)),
        qz_s=dma((6,)),
        qz_r=dma((6,)),
        qc_s=dma((9,)),
        qc_r=dma((9,)),
        vy_s=dma((1,)),
        vy_r=dma((1,)),
        vz_s=dma((8,)),
        vz_r=dma((8,)),
        vc_s=dma((10,)),
        vc_r=dma((10,)),
        a_s=dma((NS - 1,)),
        a_r=dma((NS,)),
        b_s=dma((NS - 1,)),
        b_r=dma((NS,)),
        c_s=dma((NS - 1,)),
        c_r=dma((NS,)),
        d_s=dma((NT - 1,)),
        d_r=dma((NT,)),
        x_s=dma((NT - 1,)),
        x_r=dma((NT,)),
        u_s=dma((STEPS, NT - 1)),
        u_r=dma((STEPS, NT)),
        e_s=dma((STEPS, NS - 1)),
        e_r=dma((STEPS, NS)),
    )
    smem = pl.BlockSpec(memory_space=pltpu.SMEM)
    vmem = pl.BlockSpec(memory_space=pltpu.VMEM)
    hbm = pl.BlockSpec(memory_space=pl.ANY)
    return pl.pallas_call(
        functools.partial(kernel, tuple(scratch)),
        out_shape=(
            jax.ShapeDtypeStruct((tok, qcols), bf16),
            jax.ShapeDtypeStruct((STEPS, rows, width), bf16),
        ),
        in_specs=[smem, smem, smem, vmem, hbm, hbm, hbm, hbm, hbm],
        out_specs=(vmem, vmem),
        scratch_shapes=list(scratch.values()),
        compiler_params=pltpu.CompilerParams(
            collective_id=0, has_side_effects=True, vmem_limit_bytes=62 * 1024 * 1024
        ),
        name="attention_layer",
    )(lens, row_prompt, cache_len, states, x, wkv, wq, wo, cache)


def body(
    prompt_states,
    prompt_lens,
    w_query,
    w_keyval,
    w_out,
    decode_states,
    kv_cache,
    cache_len,
    row_prompt,
):
    dblk = w_query.shape[0]
    rows = decode_states.shape[0]
    return layer(
        prompt_lens,
        row_prompt,
        cache_len,
        decode_states,
        prompt_states,
        w_keyval.reshape(2 * dblk, HD),
        w_query,
        w_out,
        kv_cache.reshape(rows, 2 * CACHE, HD),
    )


def solution(mesh):
    in_specs = (
        P(("group", "shard"), None),
        P(),
        P("shard", "tensor"),
        P("shard", None, "tensor"),
        P("tensor", "shard"),
        P(("group", "shard"), None),
        P(("group", "shard"), None, None, "tensor"),
        P(("group", "shard")),
        P(("group", "shard")),
    )
    out_specs = (P(("group", "shard"), "tensor"), P(None, ("group", "shard"), None))
    return jax.shard_map(body, mesh=mesh, in_specs=in_specs, out_specs=out_specs, check_vma=False)
```

```python
import functools

import jax
import jax.numpy as jnp
from jax import lax
from jax.experimental import pallas as pl
from jax.experimental.pallas import tpu as pltpu
from jax.sharding import PartitionSpec as P

HD = 128
CACHE = 2048
STEPS = 4
EPSILON = 1e-05
MESH = pl.DeviceIdType.MESH
NG = 4
NS = 4
NT = 8
MOST = 1024
QT = 256
KW = QT + MOST
INV_ROOT = HD**-0.5
LOG2E = 1.4426950408889634
TRANS = (((1,), (1,)), ((), ()))
f32 = jnp.float32
bf16 = jnp.bfloat16


def kernel(names, lens_ref, rowp_ref, clen_ref, ds_ref, x_hbm, wkv_hbm, wq_hbm, wo_hbm, cache_hbm, ctx_ref, out_ref, *scratch):
    r = dict(zip(names, scratch))
    xv, wk, wv, wq, wo, raw, ck, cv = (r[n] for n in ("xv", "wk", "wv", "wq", "wo", "raw", "ck", "cv"))
    kk, vv, qh, acc_q, acc_kv, scale, bias = (r[n] for n in ("kk", "vv", "qh", "acc_q", "acc_kv", "scale", "bias"))
    a_recv, xu, xu_send, state = (r[n] for n in ("a_recv", "xu", "xu_send", "state"))
    b_send, b_recv, qs, fkv = (r[n] for n in ("b_send", "b_recv", "qs", "fkv"))
    c_send, c_recv, d_send, d_recv = (r[n] for n in ("c_send", "c_recv", "d_send", "d_recv"))
    e_send, e_recv = r["e_send"], r["e_recv"]

    g = lax.axis_index("group")
    s = lax.axis_index("shard")
    t = lax.axis_index("tensor")
    sc = s + 1 - 2 * lax.rem(s, 2)
    s2 = lax.rem(s + 2, NS)
    s3 = lax.rem(sc + 2, NS)
    tok = xv.shape[0]
    rows = ds_ref.shape[0]
    dblk, qcols = wq.shape[1:]
    piece = dblk // NT
    heads = qcols // HD
    width = NS * dblk
    quarter = dblk // NG
    half = quarter // 2

    def up(base, d, n):
        return lax.rem(base + d, n)

    def remote(src, dst, ssem, rsem, **where):
        return pltpu.make_async_remote_copy(
            src_ref=src, dst_ref=dst, send_sem=ssem, recv_sem=rsem, device_id=where, device_id_type=MESH
        )

    sent = []

    def send(src, dst, ssem, rsem, **where):
        c = remote(src, dst, ssem, rsem, **where)
        c.start()
        sent.append(c)
        return c

    def arrive(dst, ssem, rsem, **where):
        remote(dst, dst, ssem, rsem, **where).wait_recv()

    def load(a, b, i):
        c = pltpu.make_async_copy(a, b, r["lsem"].at[i])
        c.start()
        return c

    load_wkv = load(wkv_hbm, r["kraw"], 1)
    load_x = load(x_hbm, xv, 0)
    load_wq = load(wq_hbm, wq.at[s], 2)

    barrier = pltpu.get_barrier_semaphore()
    for d in range(1, NS):
        pl.semaphore_signal(barrier, inc=1, device_id={"shard": up(s, d, NS)}, device_id_type=MESH)
    for d in range(1, NG):
        pl.semaphore_signal(barrier, inc=1, device_id={"group": up(g, d, NG)}, device_id_type=MESH)
    for d in range(1, NT):
        pl.semaphore_signal(barrier, inc=1, device_id={"tensor": up(t, d, NT)}, device_id_type=MESH)

    begin = jnp.int32(0)
    prompts = NG * lens_ref.shape[1]
    starts = [jnp.int32(0)] * rows
    sizes = [jnp.int32(0)] * rows
    for i in range(prompts):
        here = lens_ref[i // lens_ref.shape[1], i % lens_ref.shape[1]]
        for row in range(rows):
            hit = (rowp_ref[row] == i).astype(jnp.int32)
            starts[row] = starts[row] + hit * begin
            sizes[row] = sizes[row] + hit * here
        begin = begin + here
    b0 = lens_ref[g, 0]
    b1 = b0 + lens_ref[g, 1]
    is_new = [(rowp_ref[row] < prompts).astype(jnp.int32) for row in range(rows)]
    spots = NG * NS * tok // MOST - 1
    begin = sum(starts)
    spot = jnp.minimum(begin // MOST, spots - 1)
    low = [is_new[row] * (starts[row] - spot * MOST) for row in range(rows)]
    high = [low[row] + is_new[row] * sizes[row] + (1 - is_new[row]) * clen_ref[row] for row in range(rows)]

    out_i = lax.broadcasted_iota(jnp.int32, (256, 256), 0)
    in_i = lax.broadcasted_iota(jnp.int32, (256, 256), 1)
    want = jnp.where(out_i < 128, 2 * out_i, 2 * (out_i - 128) + 1)
    pick = (in_i == want).astype(bf16)

    load_wkv.wait()

    def separate_weights(i, c):
        pair = jnp.concatenate(
            [r["kraw"][pl.ds(pl.multiple_of((2 * i + j) * 256, 256), 256), :] for j in range(2)], axis=1
        )
        split = jnp.dot(pick, pair, preferred_element_type=f32).astype(bf16)
        for j in range(2):
            dst = pl.ds(pl.multiple_of((2 * i + j) * 128, 128), 128)
            wk[s, dst, :] = split[:128, j * HD : (j + 1) * HD]
            wv[s, dst, :] = split[128:, j * HD : (j + 1) * HD]
        return c

    lax.fori_loop(0, dblk // 256, separate_weights, 0)
    ds = r["ds"]
    for i in range(NS):
        ds[i] = ds_ref[:, i * dblk : (i + 1) * dblk].astype(f32)
    pl.semaphore_wait(barrier, NS - 1 + NG - 1 + NT - 1)

    weights_of, cached = (wk, wv), (kk, vv)

    def krows(j, blk, q):
        return weights_of[j].at[blk, pl.ds(pl.multiple_of(q * quarter, quarter), quarter)]

    def qrows(blk, q, h):
        return wq.at[blk, pl.ds(pl.multiple_of(q * quarter + h * half, half), half)]

    q_of = [g, up(g, 2, NG), up(g, 3, NG), up(g, 1, NG)]
    ky_s, ky_r, kz_s, kz_r, kc_s, kc_r = (r[n] for n in ("ky_s", "ky_r", "kz_s", "kz_r", "kc_s", "kc_r"))
    qy_s, qy_r, qz_s, qz_r, qc_s, qc_r = (r[n] for n in ("qy_s", "qy_r", "qz_s", "qz_r", "qc_s", "qc_r"))

    for i, j in ((0, 0), (0, 1), (1, 0), (1, 1)):
        ref = krows(j, s, q_of[i])
        send(ref, ref, ky_s.at[j, i], ky_r.at[j, i], shard=s2)
    for j in range(2):
        ref = weights_of[j].at[s]
        send(ref, ref, kc_s.at[j, 4], kc_r.at[j, 4], shard=sc)
    for d in range(1, NS):
        p = up(s, d, NS)
        send(ds.at[p], a_recv.at[s], r["a_s"].at[d - 1], r["a_r"].at[s], shard=p)
    a_recv[s] = ds[s]
    r["fkv"][...] = jnp.zeros_like(fkv)
    for ref in cached:
        ref[:MOST, :] = jnp.zeros((MOST, HD), bf16)

    def k_arrive_y(j, i):
        arrive(krows(j, s2, q_of[i]), ky_s.at[j, i], ky_r.at[j, i], shard=s2)

    def k_arrive_z(j, i):
        arrive(krows(j, s2, q_of[2 + i]), kz_s.at[j, i], kz_r.at[j, i], group=q_of[2 + i])

    def k_arrive_core(j, role):
        arrive(krows(j, s3, q_of[role]), kc_s.at[j, role], kc_r.at[j, role], shard=sc)

    def k_forward(j, role):
        ref = krows(j, s2, q_of[role])
        send(ref, ref, kc_s.at[j, role], kc_r.at[j, role], shard=sc)

    def k_forward_z(j):
        ref = krows(j, s2, g)
        send(ref, ref, kz_s.at[j, 0], kz_r.at[j, 0], group=up(g, 1, NG))
        send(ref, ref, kz_s.at[j, 1], kz_r.at[j, 1], group=up(g, 3, NG))

    def q_core(q):
        ref = wq.at[s, pl.ds(q * quarter, quarter)]
        send(ref, ref, qc_s.at[8 + q], qc_r.at[8 + q], shard=sc)

    def q_core_ready():
        for q in range(NG):
            ref = wq.at[sc, pl.ds(q * quarter, quarter)]
            arrive(ref, qc_s.at[8 + q], qc_r.at[8 + q], shard=sc)

    def q_send_y(i):
        ref = qrows(s, g, i)
        send(ref, ref, qy_s.at[i], qy_r.at[i], shard=s2)

    def q_arrive_y(i):
        arrive(qrows(s2, g, i), qy_s.at[i], qy_r.at[i], shard=s2)

    def q_second(h):
        ref = qrows(s2, q_of[2 + h], h)
        send(ref, ref, qz_s.at[4 + h], qz_r.at[4 + h], group=up(g, 1 + 2 * h, NG))

    def q_arrive_second(h):
        arrive(qrows(s2, q_of[1], h), qz_s.at[4 + h], qz_r.at[4 + h], group=q_of[2 + h])

    def q_forward_z(h):
        ref = qrows(s2, g, h)
        send(ref, ref, qz_s.at[h], qz_r.at[h], group=up(g, 1, NG))
        send(ref, ref, qz_s.at[2 + h], qz_r.at[2 + h], group=up(g, 3, NG))

    def q_arrive_z(i):
        arrive(qrows(s2, q_of[2 + i // 2], i % 2), qz_s.at[i], qz_r.at[i], group=q_of[2 + i // 2])

    def q_forward(i):
        ref = qrows(s2, q_of[i // 2], i % 2)
        send(ref, ref, qc_s.at[i], qc_r.at[i], shard=sc)

    def q_arrive_core(i):
        arrive(qrows(s3, q_of[i // 2], i % 2), qc_s.at[i], qc_r.at[i], shard=sc)

    def x_block(blk):
        return xv[:, pl.ds(pl.multiple_of(blk * dblk, dblk), dblk)]

    def kv_block(j, blk, first):
        prod = jnp.dot(x_block(blk), weights_of[j][blk], preferred_element_type=f32)
        acc_kv[j] = prod if first else acc_kv[j] + prod

    def q_block(blk, first, lo=0, hi=None):
        hi = qcols // 256 if hi is None else hi

        def part(n, c):
            cols = pl.ds(pl.multiple_of(n * 256, 256), 256)
            prod = jnp.dot(x_block(blk), wq[blk, :, cols], preferred_element_type=f32)
            acc_q[:, cols] = prod if first else acc_q[:, cols] + prod
            return c

        lax.fori_loop(lo, hi, part, 0)

    load_x.wait()
    load_raw = load(cache_hbm, raw, 3)
    load_wo = load(wo_hbm, wo, 4)

    def squares(i, c):
        part = pl.ds(pl.multiple_of(i * 32, 32), 32)
        v = xv[part, :].astype(f32)
        mean = jnp.sum(v * v, axis=1, keepdims=True) / width
        scale[part, :] = jnp.broadcast_to(lax.rsqrt(mean + EPSILON), (32, HD))
        return c

    for j in range(2):
        kv_block(j, s, True)
    k_arrive_y(0, 0)
    k_forward_z(0)
    k_forward(0, 0)
    lax.fori_loop(0, tok // 32, squares, 0)
    k_arrive_y(1, 0)
    k_forward_z(1)
    k_forward(1, 0)

    for d in range(1, NS):
        src = up(s, NS - d, NS)
        arrive(a_recv.at[src], r["a_s"].at[d - 1], r["a_r"].at[src], shard=src)
    x0 = jnp.concatenate([a_recv[i] for i in range(NS)], axis=0)
    for i in range(NT):
        xu[i] = x0[:, i * piece : (i + 1) * piece].astype(bf16)
    mine = pl.ds(pl.multiple_of(t * piece, piece), piece)
    state[...] = jnp.concatenate([a_recv[i, :, mine] for i in range(NS)], axis=0)

    def slot(j, gg, ss):
        return cached[j].at[pl.ds(pl.multiple_of(MOST + (gg * NS + ss) * tok, tok), tok)]

    def half_slot(j, gg, ss, h):
        n = tok // 2
        return cached[j].at[pl.ds(pl.multiple_of(MOST + (gg * NS + ss) * tok + h * n, n), n)]

    vy_s, vy_r, vz_s, vz_r, vc_s, vc_r = (r[n] for n in ("vy_s", "vy_r", "vz_s", "vz_r", "vc_s", "vc_r"))
    below, above = up(g, 3, NG), up(g, 1, NG)

    def v_core(j, ref, i):
        send(ref, ref, vc_s.at[j, i], vc_r.at[j, i], shard=sc)

    def v_sides(j, ss, i):
        ref = slot(j, g, ss)
        send(ref, ref, vz_s.at[j, i], vz_r.at[j, i], group=above)
        send(ref, ref, vz_s.at[j, i + 1], vz_r.at[j, i + 1], group=below)

    def v_pass(j, ss, i, core):
        for h, (source, target) in enumerate([(below, above), (above, below)]):
            arrive(slot(j, source, ss), vz_s.at[j, i + h], vz_r.at[j, i + h], group=source)
            ref = half_slot(j, source, ss, h)
            send(ref, ref, vz_s.at[j, i + 4 + h], vz_r.at[j, i + 4 + h], group=target)
            v_core(j, slot(j, source, ss), core + h)

    def v_last(j, ss, i, core):
        for h, source in enumerate([below, above]):
            ref = half_slot(j, up(g, 2, NG), ss, h)
            arrive(ref, vz_s.at[j, i + 4 + h], vz_r.at[j, i + 4 + h], group=source)
            v_core(j, ref, core + h)

    def v_theirs(j):
        ref = slot(j, g, s2)
        arrive(ref, vy_s.at[j], vy_r.at[j], shard=s2)
        v_sides(j, s2, 2)
        v_core(j, ref, 1)

    def v_core_ready(j):
        for i, ref in enumerate(
            [slot(j, g, sc), slot(j, g, s3)]
            + [slot(j, gg, ss) for ss in (sc, s3) for gg in (below, above)]
            + [half_slot(j, up(g, 2, NG), ss, h) for ss in (sc, s3) for h in range(2)]
        ):
            arrive(ref, vc_s.at[j, i], vc_r.at[j, i], shard=sc)

    for j in range(2):
        k_arrive_z(j, 0)
        k_forward(j, 2)
        k_arrive_z(j, 1)
        k_forward(j, 3)
        k_arrive_y(j, 1)
        k_forward(j, 1)
        arrive(weights_of[j].at[sc], kc_s.at[j, 4], kc_r.at[j, 4], shard=sc)
        kv_block(j, sc, False)
        kv_block(j, s2, False)
        for role in (0, 2, 3, 1):
            k_arrive_core(j, role)
        kv_block(j, s3, False)
        cached[j][pl.ds(pl.multiple_of(MOST + (g * NS + s) * tok, tok), tok), :] = (acc_kv[j] * scale[...]).astype(
            bf16
        )
        own = slot(j, g, s)
        send(own, own, vy_s.at[j], vy_r.at[j], shard=s2)
        v_sides(j, s, 0)
        v_core(j, own, 0)

    def decode_project():
        acc = jnp.zeros((NS * rows, qcols), f32)
        acc2 = jnp.zeros((NS * rows, 2 * HD), f32)
        square = jnp.zeros((NS * rows, 1), f32)
        for i in range(NT):
            xi = xu[i]
            acc += jnp.dot(xi, wq[s, i * piece : (i + 1) * piece, :], preferred_element_type=f32)
            part = slice(i * piece, (i + 1) * piece)
            joined = jnp.concatenate([wk[s, part, :], wv[s, part, :]], axis=1)
            acc2 += jnp.dot(xi, joined, preferred_element_type=f32)
            xf = xi.astype(f32)
            square += jnp.sum(xf * xf, axis=1, keepdims=True)
        wide = jnp.broadcast_to(square, (NS * rows, HD))
        for i in range(NS):
            b_send[i, :, :qcols] = acc[i * rows : (i + 1) * rows]
            b_send[i, :, qcols : qcols + 2 * HD] = acc2[i * rows : (i + 1) * rows]
            b_send[i, :, qcols + 2 * HD :] = wide[i * rows : (i + 1) * rows]
        copies = []
        for d in range(1, NS):
            p = up(s, d, NS)
            c = remote(b_send.at[p], b_recv.at[s], r["b_s"].at[d - 1], r["b_r"].at[s], shard=p)
            c.start()
            copies.append(c)
        return copies

    load_wq.wait()
    b_copies = decode_project()
    q_send_y(0)
    q_send_y(1)

    load_raw.wait()
    def separate(i, c):
        src = pl.ds(pl.multiple_of(i * 256, 256), 256)
        dst = pl.ds(pl.multiple_of(i * 128, 128), 128)
        for row in range(0, rows, 2):
            pair = jnp.concatenate([raw[row, src, :], raw[row + 1, src, :]], axis=1)
            split = jnp.dot(pick, pair, preferred_element_type=f32).astype(bf16)
            for j in range(2):
                ck[row + j, dst, :] = split[:128, j * HD : (j + 1) * HD]
                cv[row + j, dst, :] = split[128:, j * HD : (j + 1) * HD]
        return c

    for i in range(tok // QT):
        q_pos = s * tok + i * QT + lax.broadcasted_iota(jnp.int32, (QT, KW), 0)
        k_pos = s * tok + i * QT - MOST + lax.broadcasted_iota(jnp.int32, (QT, KW), 1)
        start = jnp.where(q_pos >= b1, b1, jnp.where(q_pos >= b0, b0, 0))
        bias[i] = jnp.where((k_pos >= start) & (k_pos <= q_pos), 0.0, -1e30)

    v_theirs(0)
    v_pass(0, s, 0, 2)
    v_theirs(1)
    v_pass(1, s, 0, 2)
    lax.fori_loop(0, 2 * ck.shape[1] // 256, separate, 0)
    v_last(0, s, 0, 6)
    v_pass(0, s2, 2, 4)
    v_last(1, s, 0, 6)
    v_pass(1, s2, 2, 4)
    v_last(0, s2, 2, 8)
    v_core_ready(0)

    def splat(flag):
        return jnp.broadcast_to(flag, (HD, HD)).astype(f32).astype(bf16)

    at_spot = [splat((spot == j).astype(jnp.int32)) for j in range(spots)]
    takes = [splat(is_new[row]) for row in range(rows)]

    def place(j):
        stored = (ck, cv)[j]

        def part(i, c):
            dst = pl.ds(pl.multiple_of(i * HD, HD), HD)
            window = jnp.zeros((HD, HD), bf16)
            for n in range(spots):
                src = pl.ds(pl.multiple_of((1 + n) * MOST + i * HD, HD), HD)
                window = window + cached[j][src, :] * at_spot[n]
            for row in range(rows):
                stored[row, dst, :] = stored[row, dst, :] * (1 - takes[row]) + window * takes[row]
            return c

        lax.fori_loop(0, 2 * MOST // HD, part, 0)

    place(0)
    v_last(1, s2, 2, 8)
    v_core_ready(1)
    place(1)
    q_arrive_y(0)
    q_forward_z(0)
    q_forward(0)

    def attend(u, c):
        h = lax.rem(u, heads)
        i = u // heads
        part = pl.ds(pl.multiple_of(i * QT, QT), QT)
        keys = pl.ds(pl.multiple_of((g * NS + s) * tok + i * QT, QT), KW)
        scores = lax.dot_general(qh[h, part, :], kk[keys, :], TRANS, preferred_element_type=f32)
        scores = scores + bias[i]
        high = jnp.max(scores, axis=1, keepdims=True)
        weights = jnp.exp2((scores - high) * (INV_ROOT * LOG2E))
        summed = jnp.sum(weights, axis=1, keepdims=True)
        mixed = jnp.dot(weights.astype(bf16), vv[keys, :], preferred_element_type=f32)
        cols = pl.ds(pl.multiple_of(h * HD, HD), HD)
        ctx_ref[part, cols] = (mixed / summed).astype(bf16)
        return c

    def attend_units(lo, hi):
        lax.fori_loop(lo, hi, attend, 0)

    def finish_queries():
        for h in range(heads):
            qh[h] = (acc_q[:, h * HD : (h + 1) * HD] * scale[...]).astype(bf16)

    def s2_early():
        q_arrive_y(1)
        q_forward_z(1)
        q_forward(1)

    def s2_sides(h):
        for i in (h, 2 + h):
            q_arrive_z(i)
            q_forward(4 + i)
        q_second(h)

    def s2_last():
        for h in range(2):
            q_arrive_second(h)
            q_forward(2 + h)

    def s3_ready():
        for i in range(8):
            q_arrive_core(i)

    units = heads * (tok // QT)
    fills = {
        (0, 0): [lambda: q_core(0), lambda: q_block(s, True)],
        (0, 1): [s2_early, lambda: q_core(1)],
        (0, 2): [lambda: q_core(2)],
        (0, 3): [lambda: s2_sides(0), lambda: q_core(3)],
        (1, 0): [q_core_ready, lambda: q_block(sc, False)],
        (1, 1): [lambda: s2_sides(1)],
        (2, 0): [s2_last, lambda: q_block(s2, False)],
        (2, 1): [s3_ready, lambda: q_block(s3, False)],
        (2, 2): [finish_queries, lambda: attend_units(0, 2)],
        (2, 3): [lambda: attend_units(2, 5)],
        (3, 0): [lambda: attend_units(5, 8)],
        (3, 1): [lambda: attend_units(8, 12)],
        (3, 2): [lambda: attend_units(12, units)],
    }

    def fill(k, i):
        for task in fills.get((k, i), []):
            task()

    def all_shards(src_of, dst, ssem, rsem):
        copies = []
        for d in range(1, NS):
            p = up(s, d, NS)
            c = remote(src_of(p), dst, ssem.at[d - 1], rsem, shard=p)
            c.start()
            copies.append(c)
        return copies

    def all_tensors(src_of, dst, ssem, rsem):
        copies = []
        for d in (4, 6, 2, 5, 3, 7, 1):
            p = up(t, d, NT)
            c = remote(src_of(p), dst, ssem.at[d - 1], rsem, tensor=p)
            c.start()
            copies.append(c)
        return copies

    def settle(copies):
        for c in copies:
            c.wait_send()

    u_send, u_recv = r["u_send"], r["u_recv"]

    def give_update(k):
        sent.extend(all_tensors(lambda p: u_send.at[k], u_recv.at[k, t], r["u_s"].at[k], r["u_r"].at[k, t]))
        u_recv[k, t] = u_send[k]

    def spread_update(k):
        for d in range(1, NT):
            src = up(t, NT - d, NT)
            arrive(u_recv.at[k, src], r["u_s"].at[k, d - 1], r["u_r"].at[k, src], tensor=src)
        for i in range(NT):
            u = u_recv[k, i].astype(f32)
            for j in range(NS):
                e_send[k, j, :, i * piece : (i + 1) * piece] = u[j * rows : (j + 1) * rows]
        sent.extend(all_shards(lambda p: e_send.at[k, p], e_recv.at[k, s], r["e_s"].at[k], r["e_r"].at[k, s]))
        e_recv[k, s] = e_send[k, s]

    cpos = lax.broadcasted_iota(jnp.int32, (heads, ck.shape[1]), 1)
    load_wo.wait()
    for k in range(STEPS):
        total = b_send[s]
        for d in range(1, NS):
            src = up(s, NS - d, NS)
            arrive(b_recv.at[src], r["b_s"].at[d - 1], r["b_r"].at[src], shard=src)
            total = total + b_recv[src]
        norm = lax.rsqrt(total[:, qcols + 2 * HD : qcols + 2 * HD + 1] / width + EPSILON)
        fresh = (total[:, : qcols + 2 * HD] * norm).astype(bf16).astype(f32)
        fkv[k] = fresh[:, qcols:]
        for row in range(rows):
            for h in range(heads):
                qs[row, h : h + 1, :] = fresh[row : row + 1, h * HD : (h + 1) * HD]
        for row in range(rows):
            q = qs[row]
            valid = (cpos >= low[row]) & (cpos < high[row])
            scores = lax.dot_general(q.astype(bf16), ck[row], TRANS, preferred_element_type=f32) * INV_ROOT
            scores = jnp.where(valid, scores, -1e30)
            top = jnp.max(scores, axis=1, keepdims=True)
            news = []
            for j in range(k + 1):
                new = jnp.sum(q * fkv[j, row : row + 1, :HD], axis=1, keepdims=True) * INV_ROOT
                news.append(new)
                top = jnp.maximum(top, new)
            weights = jnp.where(valid, jnp.exp(scores - top), 0.0)
            summed = jnp.sum(weights, axis=1, keepdims=True)
            mixed = jnp.dot(weights.astype(bf16), cv[row], preferred_element_type=f32)
            for j in range(k + 1):
                weight = jnp.exp(news[j] - top)
                summed = summed + weight
                mixed = mixed + weight.astype(bf16).astype(f32) * fkv[j, row : row + 1, HD:]
            context = (mixed / summed).astype(bf16).astype(f32)
            for h in range(heads):
                c_send[row : row + 1, h * HD : (h + 1) * HD] = context[h : h + 1]

        c_copies = all_shards(lambda p: c_send, c_recv.at[s], r["c_s"], r["c_r"].at[s])
        c_recv[s] = c_send[...]
        settle(b_copies)
        fill(k, 0)
        for d in range(1, NS):
            src = up(s, NS - d, NS)
            arrive(c_recv.at[src], r["c_s"].at[d - 1], r["c_r"].at[src], shard=src)
        block = jnp.concatenate([c_recv[i] for i in range(NS)], axis=0).astype(bf16)
        for i in range(NT):
            d_send[i] = jnp.dot(block, wo[:, i * piece : (i + 1) * piece], preferred_element_type=f32).astype(bf16)

        d_copies = all_tensors(lambda p: d_send.at[p], d_recv.at[t], r["d_s"], r["d_r"].at[t])
        settle(c_copies)
        if k > 0:
            spread_update(k - 1)
        fill(k, 1)
        update = d_send[t].astype(f32)
        for d in range(1, NT):
            src = up(t, NT - d, NT)
            arrive(d_recv.at[src], r["d_s"].at[d - 1], r["d_r"].at[src], tensor=src)
            update = update + d_recv[src].astype(f32)
        u_send[k] = update.astype(bf16)
        if k == STEPS - 1:
            give_update(k)
            settle(d_copies)
            fill(k, 2)
            spread_update(k)
            break
        after = state[...] + update
        state[...] = after
        xu_send[...] = after.astype(bf16)
        x_copies = all_tensors(lambda p: xu_send, xu.at[t], r["x_s"], r["x_r"].at[t])
        xu[t] = xu_send[...]
        settle(d_copies)
        fill(k, 2)
        for d in range(1, NT):
            src = up(t, NT - d, NT)
            arrive(xu.at[src], r["x_s"].at[d - 1], r["x_r"].at[src], tensor=src)
        b_copies = decode_project()
        settle(x_copies)
        give_update(k)
        fill(k, 3)

    for k in range(STEPS):
        for d in range(1, NS):
            src = up(s, NS - d, NS)
            arrive(e_recv.at[k, src], r["e_s"].at[k, d - 1], r["e_r"].at[k, src], shard=src)
        for i in range(NS):
            out_ref[k, :, i * dblk : (i + 1) * dblk] = e_recv[k, i].astype(bf16)
    settle(sent)


def layer(lens, row_prompt, cache_len, states, x, wkv, wq, wo, cache):
    rows = states.shape[0]
    tok, width = x.shape
    dblk, qcols = wq.shape
    piece = dblk // NT
    heads = qcols // HD
    vm = pltpu.VMEM
    dma = pltpu.SemaphoreType.DMA
    bw = qcols + 3 * HD
    scratch = dict(
        xv=vm((tok, width), bf16),
        wk=vm((NS, dblk, HD), bf16),
        wv=vm((NS, dblk, HD), bf16),
        wq=vm((NS, dblk, qcols), bf16),
        wo=vm(wo.shape, bf16),
        raw=vm(cache.shape, bf16),
        ck=vm((rows, CACHE, HD), bf16),
        cv=vm((rows, CACHE, HD), bf16),
        kk=vm((MOST + NG * NS * tok, HD), bf16),
        vv=vm((MOST + NG * NS * tok, HD), bf16),
        qh=vm((heads, tok, HD), bf16),
        acc_q=vm((tok, qcols), f32),
        acc_kv=vm((2, tok, HD), f32),
        scale=vm((tok, HD), f32),
        bias=vm((tok // QT, QT, KW), f32),
        kraw=vm((2 * dblk, HD), bf16),
        ds=vm((NS, rows, dblk), f32),
        a_recv=vm((NS, rows, dblk), f32),
        xu=vm((NT, NS * rows, piece), bf16),
        xu_send=vm((NS * rows, piece), bf16),
        u_send=vm((STEPS, NS * rows, piece), bf16),
        u_recv=vm((STEPS, NT, NS * rows, piece), bf16),
        state=vm((NS * rows, piece), f32),
        b_send=vm((NS, rows, bw), f32),
        b_recv=vm((NS, rows, bw), f32),
        qs=vm((rows, heads, HD), f32),
        fkv=vm((STEPS, rows, 2 * HD), f32),
        c_send=vm((rows, qcols), f32),
        c_recv=vm((NS, rows, qcols), f32),
        d_send=vm((NT, NS * rows, piece), bf16),
        d_recv=vm((NT, NS * rows, piece), bf16),
        e_send=vm((STEPS, NS, rows, dblk), f32),
        e_recv=vm((STEPS, NS, rows, dblk), f32),
        lsem=dma((5,)),
        ky_s=dma((2, 2)),
        ky_r=dma((2, 2)),
        kz_s=dma((2, 2)),
        kz_r=dma((2, 2)),
        kc_s=dma((2, 5)),
        kc_r=dma((2, 5)),
        qy_s=dma((2,)),
        qy_r=dma((2,)),
        qz_s=dma((6,)),
        qz_r=dma((6,)),
        qc_s=dma((12,)),
        qc_r=dma((12,)),
        vy_s=dma((2,)),
        vy_r=dma((2,)),
        vz_s=dma((2, 8)),
        vz_r=dma((2, 8)),
        vc_s=dma((2, 10)),
        vc_r=dma((2, 10)),
        a_s=dma((NS - 1,)),
        a_r=dma((NS,)),
        b_s=dma((NS - 1,)),
        b_r=dma((NS,)),
        c_s=dma((NS - 1,)),
        c_r=dma((NS,)),
        d_s=dma((NT - 1,)),
        d_r=dma((NT,)),
        x_s=dma((NT - 1,)),
        x_r=dma((NT,)),
        u_s=dma((STEPS, NT - 1)),
        u_r=dma((STEPS, NT)),
        e_s=dma((STEPS, NS - 1)),
        e_r=dma((STEPS, NS)),
    )
    smem = pl.BlockSpec(memory_space=pltpu.SMEM)
    vmem = pl.BlockSpec(memory_space=pltpu.VMEM)
    hbm = pl.BlockSpec(memory_space=pl.ANY)
    return pl.pallas_call(
        functools.partial(kernel, tuple(scratch)),
        out_shape=(
            jax.ShapeDtypeStruct((tok, qcols), bf16),
            jax.ShapeDtypeStruct((STEPS, rows, width), bf16),
        ),
        in_specs=[smem, smem, smem, vmem, hbm, hbm, hbm, hbm, hbm],
        out_specs=(vmem, vmem),
        scratch_shapes=list(scratch.values()),
        compiler_params=pltpu.CompilerParams(
            collective_id=0, has_side_effects=True, vmem_limit_bytes=62 * 1024 * 1024
        ),
        name="attention_layer",
    )(lens, row_prompt, cache_len, states, x, wkv, wq, wo, cache)


def body(
    prompt_states,
    prompt_lens,
    w_query,
    w_keyval,
    w_out,
    decode_states,
    kv_cache,
    cache_len,
    row_prompt,
):
    dblk = w_query.shape[0]
    rows = decode_states.shape[0]
    return layer(
        prompt_lens,
        row_prompt,
        cache_len,
        decode_states,
        prompt_states,
        w_keyval.reshape(2 * dblk, HD),
        w_query,
        w_out,
        kv_cache.reshape(rows, 2 * CACHE, HD),
    )


def solution(mesh):
    in_specs = (
        P(("group", "shard"), None),
        P(),
        P("shard", "tensor"),
        P("shard", None, "tensor"),
        P("tensor", "shard"),
        P(("group", "shard"), None),
        P(("group", "shard"), None, None, "tensor"),
        P(("group", "shard")),
        P(("group", "shard")),
    )
    out_specs = (P(("group", "shard"), "tensor"), P(None, ("group", "shard"), None))
    return jax.shard_map(body, mesh=mesh, in_specs=in_specs, out_specs=out_specs, check_vma=False)
```

```python
import functools

import jax
import jax.numpy as jnp
from jax import lax
from jax.experimental import pallas as pl
from jax.experimental.pallas import tpu as pltpu
from jax.sharding import PartitionSpec as P

HD = 128
CACHE = 2048
STEPS = 4
EPSILON = 1e-05
MESH = pl.DeviceIdType.MESH
NG = 4
NS = 4
NT = 8
MOST = 1024
QT = 256
KW = QT + MOST
INV_ROOT = HD**-0.5
LOG2E = 1.4426950408889634
TRANS = (((1,), (1,)), ((), ()))
f32 = jnp.float32
bf16 = jnp.bfloat16


def kernel(names, lens_ref, rowp_ref, clen_ref, ds_ref, x_hbm, wkv_hbm, wq_hbm, wo_hbm, cache_hbm, ctx_ref, out_ref, *scratch):
    r = dict(zip(names, scratch))
    xv, wk, wv, wq, wo, raw, ck, cv = (r[n] for n in ("xv", "wk", "wv", "wq", "wo", "raw", "ck", "cv"))
    kk, vv, qh, acc_q, acc_kv, scale, bias = (r[n] for n in ("kk", "vv", "qh", "acc_q", "acc_kv", "scale", "bias"))
    a_recv, xu, xu_send, state = (r[n] for n in ("a_recv", "xu", "xu_send", "state"))
    b_send, b_recv, qs, fkv = (r[n] for n in ("b_send", "b_recv", "qs", "fkv"))
    c_send, c_recv, d_send, d_recv = (r[n] for n in ("c_send", "c_recv", "d_send", "d_recv"))
    e_send, e_recv = r["e_send"], r["e_recv"]

    g = lax.axis_index("group")
    s = lax.axis_index("shard")
    t = lax.axis_index("tensor")
    sc = s + 1 - 2 * lax.rem(s, 2)
    s2 = lax.rem(s + 2, NS)
    s3 = lax.rem(sc + 2, NS)
    tok = xv.shape[0]
    rows = ds_ref.shape[0]
    dblk, qcols = wq.shape[1:]
    piece = dblk // NT
    heads = qcols // HD
    width = NS * dblk
    quarter = dblk // NG
    half = quarter // 2
    wide = qcols // 2

    def up(base, d, n):
        return lax.rem(base + d, n)

    def remote(src, dst, ssem, rsem, **where):
        return pltpu.make_async_remote_copy(
            src_ref=src, dst_ref=dst, send_sem=ssem, recv_sem=rsem, device_id=where, device_id_type=MESH
        )

    sent = []

    def send(src, dst, ssem, rsem, **where):
        c = remote(src, dst, ssem, rsem, **where)
        c.start()
        sent.append(c)
        return c

    def arrive(dst, ssem, rsem, **where):
        remote(dst, dst, ssem, rsem, **where).wait_recv()

    def load(a, b, i):
        c = pltpu.make_async_copy(a, b, r["lsem"].at[i])
        c.start()
        return c

    load_wkv = load(wkv_hbm, r["kraw"], 1)
    load_x = load(x_hbm, xv, 0)

    barrier = pltpu.get_barrier_semaphore()
    flat = g * NS + s
    everyone = NG * NS

    def flat_peer(d):
        f = up(flat, d, everyone)
        return f, {"group": f // NS, "shard": lax.rem(f, NS)}

    for d in range(1, everyone):
        pl.semaphore_signal(barrier, inc=1, device_id=flat_peer(d)[1], device_id_type=MESH)
    for d in range(1, NT):
        pl.semaphore_signal(barrier, inc=1, device_id={"tensor": up(t, d, NT)}, device_id_type=MESH)

    begin = jnp.int32(0)
    prompts = NG * lens_ref.shape[1]
    starts = [jnp.int32(0)] * rows
    sizes = [jnp.int32(0)] * rows
    for i in range(prompts):
        here = lens_ref[i // lens_ref.shape[1], i % lens_ref.shape[1]]
        for row in range(rows):
            hit = (rowp_ref[row] == i).astype(jnp.int32)
            starts[row] = starts[row] + hit * begin
            sizes[row] = sizes[row] + hit * here
        begin = begin + here
    b0 = lens_ref[g, 0]
    b1 = b0 + lens_ref[g, 1]
    is_new = [(rowp_ref[row] < prompts).astype(jnp.int32) for row in range(rows)]
    spots = NG * NS * tok // MOST - 1
    begin = sum(starts)
    spot = jnp.minimum(begin // MOST, spots - 1)
    low = [is_new[row] * (starts[row] - spot * MOST) for row in range(rows)]
    high = [low[row] + is_new[row] * sizes[row] + (1 - is_new[row]) * clen_ref[row] for row in range(rows)]

    out_i = lax.broadcasted_iota(jnp.int32, (256, 256), 0)
    in_i = lax.broadcasted_iota(jnp.int32, (256, 256), 1)
    want = jnp.where(out_i < 128, 2 * out_i, 2 * (out_i - 128) + 1)
    pick = (in_i == want).astype(bf16)

    load_wkv.wait()

    def separate_weights(i, c):
        pair = jnp.concatenate(
            [r["kraw"][pl.ds(pl.multiple_of((2 * i + j) * 256, 256), 256), :] for j in range(2)], axis=1
        )
        split = jnp.dot(pick, pair, preferred_element_type=f32).astype(bf16)
        for j in range(2):
            dst = pl.ds(pl.multiple_of((2 * i + j) * 128, 128), 128)
            wk[s, dst, :] = split[:128, j * HD : (j + 1) * HD]
            wv[s, dst, :] = split[128:, j * HD : (j + 1) * HD]
        return c

    lax.fori_loop(0, dblk // 256, separate_weights, 0)
    ds = r["ds"]
    for i in range(NS):
        ds[i] = ds_ref[:, i * dblk : (i + 1) * dblk].astype(f32)
    pl.semaphore_wait(barrier, everyone - 1 + NT - 1)

    weights_of, cached = (wk, wv), (kk, vv)

    def krows(j, blk, q):
        return weights_of[j].at[blk, pl.ds(pl.multiple_of(q * quarter, quarter), quarter)]

    def qrows(blk, q, h):
        return wq.at[blk, pl.ds(pl.multiple_of(q * quarter, quarter), quarter), h * wide : (h + 1) * wide]

    def qhalf(blk, q, h, n):
        return wq.at[blk, pl.ds(pl.multiple_of(q * quarter + n * half, half), half), h * wide : (h + 1) * wide]

    q_of = [g, up(g, 2, NG), up(g, 3, NG), up(g, 1, NG)]
    ky_s, ky_r, kz_s, kz_r, kc_s, kc_r = (r[n] for n in ("ky_s", "ky_r", "kz_s", "kz_r", "kc_s", "kc_r"))
    qy_s, qy_r, qz_s, qz_r, qc_s, qc_r = (r[n] for n in ("qy_s", "qy_r", "qz_s", "qz_r", "qc_s", "qc_r"))

    for i, j in ((0, 0), (0, 1), (1, 0), (1, 1)):
        ref = krows(j, s, q_of[i])
        send(ref, ref, ky_s.at[j, i], ky_r.at[j, i], shard=s2)
    for j in range(2):
        ref = weights_of[j].at[s]
        send(ref, ref, kc_s.at[j, 4], kc_r.at[j, 4], shard=sc)
    for d in range(1, NS):
        p = up(s, d, NS)
        send(ds.at[p], a_recv.at[s], r["a_s"].at[d - 1], r["a_r"].at[s], shard=p)
    a_recv[s] = ds[s]
    r["fkv"][...] = jnp.zeros_like(fkv)
    for ref in cached:
        ref[:MOST, :] = jnp.zeros((MOST, HD), bf16)

    def k_arrive_y(j, i):
        arrive(krows(j, s2, q_of[i]), ky_s.at[j, i], ky_r.at[j, i], shard=s2)

    def k_arrive_z(j, i):
        arrive(krows(j, s2, q_of[2 + i]), kz_s.at[j, i], kz_r.at[j, i], group=q_of[2 + i])

    def k_arrive_core(j, role):
        arrive(krows(j, s3, q_of[role]), kc_s.at[j, role], kc_r.at[j, role], shard=sc)

    def k_forward(j, role):
        ref = krows(j, s2, q_of[role])
        send(ref, ref, kc_s.at[j, role], kc_r.at[j, role], shard=sc)

    def k_forward_z(j):
        ref = krows(j, s2, g)
        send(ref, ref, kz_s.at[j, 0], kz_r.at[j, 0], group=up(g, 1, NG))
        send(ref, ref, kz_s.at[j, 1], kz_r.at[j, 1], group=up(g, 3, NG))

    def q_core(q):
        ref = wq.at[s, pl.ds(q * quarter, quarter)]
        send(ref, ref, qc_s.at[8 + q], qc_r.at[8 + q], shard=sc)

    def q_core_ready():
        for q in range(NG):
            ref = wq.at[sc, pl.ds(q * quarter, quarter)]
            arrive(ref, qc_s.at[8 + q], qc_r.at[8 + q], shard=sc)

    def q_send_y(i):
        ref = qrows(s, g, i)
        send(ref, ref, qy_s.at[i], qy_r.at[i], shard=s2)

    def q_arrive_y(i):
        arrive(qrows(s2, g, i), qy_s.at[i], qy_r.at[i], shard=s2)

    def q_second(h):
        for n in range(2):
            ref = qhalf(s2, q_of[2 + n], h, n)
            i = 4 + 2 * h + n
            send(ref, ref, qz_s.at[i], qz_r.at[i], group=up(g, 1 + 2 * n, NG))

    def q_arrive_second(h):
        for n in range(2):
            i = 4 + 2 * h + n
            arrive(qhalf(s2, q_of[1], h, n), qz_s.at[i], qz_r.at[i], group=q_of[2 + n])

    def q_forward_z(h):
        ref = qrows(s2, g, h)
        send(ref, ref, qz_s.at[h], qz_r.at[h], group=up(g, 1, NG))
        send(ref, ref, qz_s.at[2 + h], qz_r.at[2 + h], group=up(g, 3, NG))

    def q_arrive_z(i):
        arrive(qrows(s2, q_of[2 + i // 2], i % 2), qz_s.at[i], qz_r.at[i], group=q_of[2 + i // 2])

    def q_forward(i):
        ref = qrows(s2, q_of[i // 2], i % 2)
        send(ref, ref, qc_s.at[i], qc_r.at[i], shard=sc)

    def q_arrive_core(i):
        arrive(qrows(s3, q_of[i // 2], i % 2), qc_s.at[i], qc_r.at[i], shard=sc)

    def x_block(blk):
        return xv[:, pl.ds(pl.multiple_of(blk * dblk, dblk), dblk)]

    def kv_block(j, blk, first):
        prod = jnp.dot(x_block(blk), weights_of[j][blk], preferred_element_type=f32)
        acc_kv[j] = prod if first else acc_kv[j] + prod

    def q_block(blk, h, first=False):
        def part(n, c):
            cols = pl.ds(pl.multiple_of(n * 256, 256), 256)
            prod = jnp.dot(x_block(blk), wq[blk, :, cols], preferred_element_type=f32)
            acc_q[:, cols] = prod if first else acc_q[:, cols] + prod
            return c

        lax.fori_loop(h * wide // 256, (h + 1) * wide // 256, part, 0)

    load_x.wait()
    load_wq = load(wq_hbm, wq.at[s], 2)
    load_raw = load(cache_hbm, raw, 3)
    load_wo = load(wo_hbm, wo, 4)

    def squares(i, c):
        part = pl.ds(pl.multiple_of(i * 32, 32), 32)
        v = xv[part, :].astype(f32)
        mean = jnp.sum(v * v, axis=1, keepdims=True) / width
        scale[part, :] = jnp.broadcast_to(lax.rsqrt(mean + EPSILON), (32, HD))
        return c

    def all_shards(src_of, dst, ssem, rsem):
        copies = []
        for d in range(1, NS):
            p = up(s, d, NS)
            c = remote(src_of(p), dst, ssem.at[d - 1], rsem, shard=p)
            c.start()
            copies.append(c)
        return copies

    def all_tensors(src_of, dst, ssem, rsem):
        copies = []
        for d in (4, 6, 2, 5, 3, 7, 1):
            p = up(t, d, NT)
            c = remote(src_of(p), dst, ssem.at[d - 1], rsem, tensor=p)
            c.start()
            copies.append(c)
        return copies

    def settle(copies):
        for c in copies:
            c.wait_send()

    def decode_project():
        acc = jnp.zeros((NS * rows, qcols), f32)
        acc2 = jnp.zeros((NS * rows, 2 * HD), f32)
        square = jnp.zeros((NS * rows, 1), f32)
        for i in range(NT):
            xi = xu[i]
            acc += jnp.dot(xi, wq[s, i * piece : (i + 1) * piece, :], preferred_element_type=f32)
            part = slice(i * piece, (i + 1) * piece)
            joined = jnp.concatenate([wk[s, part, :], wv[s, part, :]], axis=1)
            acc2 += jnp.dot(xi, joined, preferred_element_type=f32)
            xf = xi.astype(f32)
            square += jnp.sum(xf * xf, axis=1, keepdims=True)
        wide = jnp.broadcast_to(square, (NS * rows, HD))
        for i in range(NS):
            b_send[i, :, :qcols] = acc[i * rows : (i + 1) * rows]
            b_send[i, :, qcols : qcols + 2 * HD] = acc2[i * rows : (i + 1) * rows]
            b_send[i, :, qcols + 2 * HD :] = wide[i * rows : (i + 1) * rows]
        copies = []
        for d in range(1, NS):
            p = up(s, d, NS)
            c = remote(b_send.at[p], b_recv.at[s], r["b_s"].at[d - 1], r["b_r"].at[s], shard=p)
            c.start()
            copies.append(c)
        return copies

    def take_fresh(k):
        total = b_send[s]
        for d in range(1, NS):
            src = up(s, NS - d, NS)
            arrive(b_recv.at[src], r["b_s"].at[d - 1], r["b_r"].at[src], shard=src)
            total = total + b_recv[src]
        norm = lax.rsqrt(total[:, qcols + 2 * HD : qcols + 2 * HD + 1] / width + EPSILON)
        fresh = (total[:, : qcols + 2 * HD] * norm).astype(bf16).astype(f32)
        fkv[k] = fresh[:, qcols:]
        for row in range(rows):
            for h in range(heads):
                qs[row, h : h + 1, :] = fresh[row : row + 1, h * HD : (h + 1) * HD]

    cpos = lax.broadcasted_iota(jnp.int32, (heads, ck.shape[1]), 1)

    def attend_stored(row):
        valid = (cpos >= low[row]) & (cpos < high[row])
        scores = lax.dot_general(qs[row].astype(bf16), ck[row], TRANS, preferred_element_type=f32) * INV_ROOT
        scores = jnp.where(valid, scores, -1e30)
        top = jnp.max(scores, axis=1, keepdims=True)
        weights = jnp.where(valid, jnp.exp(scores - top), 0.0)
        summed = jnp.sum(weights, axis=1, keepdims=True)
        return top, summed, jnp.dot(weights.astype(bf16), cv[row], preferred_element_type=f32)

    def join_fresh(k, row, old, summed, mixed):
        q = qs[row]
        top = old
        news = []
        for j in range(k + 1):
            new = jnp.sum(q * fkv[j, row : row + 1, :HD], axis=1, keepdims=True) * INV_ROOT
            news.append(new)
            top = jnp.maximum(top, new)
        rescale = jnp.exp(old - top)
        summed = summed * rescale
        mixed = mixed * rescale
        for j in range(k + 1):
            weight = jnp.exp(news[j] - top)
            summed = summed + weight
            mixed = mixed + weight.astype(bf16).astype(f32) * fkv[j, row : row + 1, HD:]
        context = (mixed / summed).astype(bf16).astype(f32)
        for h in range(heads):
            c_send[row : row + 1, h * HD : (h + 1) * HD] = context[h : h + 1]

    n_send, n_recv, m_send, m_recv, part0 = (r[n] for n in ("n_send", "n_recv", "m_send", "m_recv", "part0"))
    takes32 = [jnp.broadcast_to(is_new[row], (heads, HD)).astype(f32) for row in range(rows)]

    def ask():
        q = jnp.zeros((heads, HD), f32)
        for row in range(rows):
            q = q + qs[row] * takes32[row]
        n_send[:, :HD] = q
        n_send[:, HD : 2 * HD] = jnp.broadcast_to(begin, (heads, HD)).astype(f32)
        n_send[:, 2 * HD :] = jnp.broadcast_to(begin + sum(sizes), (heads, HD)).astype(f32)
        for d in (10, 9, 11, 6, 5, 7, 8, 2, 14, 4, 12, 13, 3, 15, 1):
            send(n_send, n_recv.at[flat], r["n_s"].at[d - 1], r["n_r"].at[flat], **flat_peer(d)[1])
        n_recv[flat] = n_send[...]

    def answer():
        for d in range(1, everyone):
            f, where = flat_peer(d)
            arrive(n_recv.at[f], r["n_s"].at[d - 1], r["n_r"].at[f], **where)
        asked = n_recv[...].reshape(everyone * heads, 3 * HD)
        here = pl.ds(pl.multiple_of(MOST + flat * tok, tok), tok)
        pos = (flat * tok + lax.broadcasted_iota(jnp.int32, (everyone * heads, tok), 1)).astype(f32)
        valid = (pos >= asked[:, HD : HD + 1]) & (pos < asked[:, 2 * HD : 2 * HD + 1])
        scores = lax.dot_general(asked[:, :HD].astype(bf16), kk[here, :], TRANS, preferred_element_type=f32)
        scores = jnp.where(valid, scores * INV_ROOT, -1e30)
        top = jnp.max(scores, axis=1, keepdims=True)
        weights = jnp.where(valid, jnp.exp(scores - top), 0.0)
        summed = jnp.sum(weights, axis=1, keepdims=True)
        mixed = jnp.dot(weights.astype(bf16), vv[here, :], preferred_element_type=f32)
        shape = (everyone, heads, HD)
        m_send[:, :, :HD] = mixed.reshape(shape)
        m_send[:, :, HD : 2 * HD] = jnp.broadcast_to(top, mixed.shape).reshape(shape)
        m_send[:, :, 2 * HD :] = jnp.broadcast_to(summed, mixed.shape).reshape(shape)
        for d in (10, 9, 11, 6, 5, 7, 8, 2, 14, 4, 12, 13, 3, 15, 1):
            f, where = flat_peer(d)
            send(m_send.at[f], m_recv.at[flat], r["m_s"].at[d - 1], r["m_r"].at[flat], **where)
        m_recv[flat] = m_send[flat]

    def first_context():
        for d in range(1, everyone):
            f, where = flat_peer(d)
            arrive(m_recv.at[f], r["m_s"].at[d - 1], r["m_r"].at[f], **where)
        top = m_recv[0, :, HD : 2 * HD]
        for i in range(1, everyone):
            top = jnp.maximum(top, m_recv[i, :, HD : 2 * HD])
        summed = jnp.zeros((heads, HD), f32)
        mixed = jnp.zeros((heads, HD), f32)
        for i in range(everyone):
            rescale = jnp.exp(m_recv[i, :, HD : 2 * HD] - top)
            summed = summed + m_recv[i, :, 2 * HD :] * rescale
            mixed = mixed + m_recv[i, :, :HD] * rescale
        for row in range(rows):
            new = takes32[row] > 0
            mine = [part0[row, :, i * HD : (i + 1) * HD] for i in range(3)]
            join_fresh(
                0,
                row,
                jnp.where(new, top, mine[0])[:, :1],
                jnp.where(new, summed, mine[1])[:, :1],
                jnp.where(new, mixed, mine[2]),
            )

    for j in range(2):
        kv_block(j, s, True)
    k_arrive_y(0, 0)
    k_forward_z(0)
    k_forward(0, 0)

    for d in range(1, NS):
        src = up(s, NS - d, NS)
        arrive(a_recv.at[src], r["a_s"].at[d - 1], r["a_r"].at[src], shard=src)
    x0 = jnp.concatenate([a_recv[i] for i in range(NS)], axis=0)
    for i in range(NT):
        xu[i] = x0[:, i * piece : (i + 1) * piece].astype(bf16)
    mine = pl.ds(pl.multiple_of(t * piece, piece), piece)
    state[...] = jnp.concatenate([a_recv[i, :, mine] for i in range(NS)], axis=0)

    load_wq.wait()
    b_copies = decode_project()
    k_arrive_y(1, 0)
    k_forward_z(1)
    k_forward(1, 0)
    lax.fori_loop(0, tok // 32, squares, 0)

    def slot(j, gg, ss):
        return cached[j].at[pl.ds(pl.multiple_of(MOST + (gg * NS + ss) * tok, tok), tok)]

    def half_slot(j, gg, ss, h):
        n = tok // 2
        return cached[j].at[pl.ds(pl.multiple_of(MOST + (gg * NS + ss) * tok + h * n, n), n)]

    vy_s, vy_r, vz_s, vz_r, vc_s, vc_r = (r[n] for n in ("vy_s", "vy_r", "vz_s", "vz_r", "vc_s", "vc_r"))
    below, above = up(g, 3, NG), up(g, 1, NG)

    def v_core(j, ref, i):
        send(ref, ref, vc_s.at[j, i], vc_r.at[j, i], shard=sc)

    def v_sides(j, ss, i):
        ref = slot(j, g, ss)
        send(ref, ref, vz_s.at[j, i], vz_r.at[j, i], group=above)
        send(ref, ref, vz_s.at[j, i + 1], vz_r.at[j, i + 1], group=below)

    def v_pass(j, ss, i, core):
        for h, (source, target) in enumerate([(below, above), (above, below)]):
            arrive(slot(j, source, ss), vz_s.at[j, i + h], vz_r.at[j, i + h], group=source)
            ref = half_slot(j, source, ss, h)
            send(ref, ref, vz_s.at[j, i + 4 + h], vz_r.at[j, i + 4 + h], group=target)
            v_core(j, slot(j, source, ss), core + h)

    def v_last(j, ss, i, core):
        for h, source in enumerate([below, above]):
            ref = half_slot(j, up(g, 2, NG), ss, h)
            arrive(ref, vz_s.at[j, i + 4 + h], vz_r.at[j, i + 4 + h], group=source)
            v_core(j, ref, core + h)

    def v_theirs(j):
        ref = slot(j, g, s2)
        arrive(ref, vy_s.at[j], vy_r.at[j], shard=s2)
        v_sides(j, s2, 2)
        v_core(j, ref, 1)

    def v_core_ready(j):
        for i, ref in enumerate(
            [slot(j, g, sc), slot(j, g, s3)]
            + [slot(j, gg, ss) for ss in (sc, s3) for gg in (below, above)]
            + [half_slot(j, up(g, 2, NG), ss, h) for ss in (sc, s3) for h in range(2)]
        ):
            arrive(ref, vc_s.at[j, i], vc_r.at[j, i], shard=sc)

    for j in range(2):
        k_arrive_z(j, 0)
        k_forward(j, 2)
        k_arrive_z(j, 1)
        k_forward(j, 3)
        k_arrive_y(j, 1)
        k_forward(j, 1)
        arrive(weights_of[j].at[sc], kc_s.at[j, 4], kc_r.at[j, 4], shard=sc)
        kv_block(j, sc, False)
        kv_block(j, s2, False)
        for role in (0, 2, 3, 1):
            k_arrive_core(j, role)
        kv_block(j, s3, False)
        cached[j][pl.ds(pl.multiple_of(MOST + (g * NS + s) * tok, tok), tok), :] = (acc_kv[j] * scale[...]).astype(
            bf16
        )
        own = slot(j, g, s)
        send(own, own, vy_s.at[j], vy_r.at[j], shard=s2)
        v_sides(j, s, 0)
        v_core(j, own, 0)
        if j == 0:
            take_fresh(0)
            ask()

    answer()
    q_send_y(0)
    q_send_y(1)

    load_raw.wait()
    def separate(i, c):
        src = pl.ds(pl.multiple_of(i * 256, 256), 256)
        dst = pl.ds(pl.multiple_of(i * 128, 128), 128)
        for row in range(0, rows, 2):
            pair = jnp.concatenate([raw[row, src, :], raw[row + 1, src, :]], axis=1)
            split = jnp.dot(pick, pair, preferred_element_type=f32).astype(bf16)
            for j in range(2):
                ck[row + j, dst, :] = split[:128, j * HD : (j + 1) * HD]
                cv[row + j, dst, :] = split[128:, j * HD : (j + 1) * HD]
        return c

    lax.fori_loop(0, 2 * ck.shape[1] // 256, separate, 0)
    v_theirs(0)
    v_pass(0, s, 0, 2)
    for row in range(rows):
        for i, v in enumerate(attend_stored(row)):
            part0[row, :, i * HD : (i + 1) * HD] = jnp.broadcast_to(v, (heads, HD))
    v_theirs(1)
    v_pass(1, s, 0, 2)

    for i in range(tok // QT):
        q_pos = s * tok + i * QT + lax.broadcasted_iota(jnp.int32, (QT, KW), 0)
        k_pos = s * tok + i * QT - MOST + lax.broadcasted_iota(jnp.int32, (QT, KW), 1)
        start = jnp.where(q_pos >= b1, b1, jnp.where(q_pos >= b0, b0, 0))
        bias[i] = jnp.where((k_pos >= start) & (k_pos <= q_pos), 0.0, -1e30)

    def splat(flag):
        return jnp.broadcast_to(flag, (HD, HD)).astype(f32).astype(bf16)

    at_spot = [splat((spot == j).astype(jnp.int32)) for j in range(spots)]
    takes = [splat(is_new[row]) for row in range(rows)]

    def place(j):
        stored = (ck, cv)[j]

        def part(i, c):
            dst = pl.ds(pl.multiple_of(i * HD, HD), HD)
            window = jnp.zeros((HD, HD), bf16)
            for n in range(spots):
                src = pl.ds(pl.multiple_of((1 + n) * MOST + i * HD, HD), HD)
                window = window + cached[j][src, :] * at_spot[n]
            for row in range(rows):
                stored[row, dst, :] = stored[row, dst, :] * (1 - takes[row]) + window * takes[row]
            return c

        lax.fori_loop(0, 2 * MOST // HD, part, 0)

    def attend(u, c):
        h = u // (tok // QT)
        i = lax.rem(u, tok // QT)
        part = pl.ds(pl.multiple_of(i * QT, QT), QT)
        keys = pl.ds(pl.multiple_of((g * NS + s) * tok + i * QT, QT), KW)
        scores = lax.dot_general(qh[h, part, :], kk[keys, :], TRANS, preferred_element_type=f32)
        scores = scores + bias[i]
        high = jnp.max(scores, axis=1, keepdims=True)
        weights = jnp.exp2((scores - high) * (INV_ROOT * LOG2E))
        summed = jnp.sum(weights, axis=1, keepdims=True)
        mixed = jnp.dot(weights.astype(bf16), vv[keys, :], preferred_element_type=f32)
        cols = pl.ds(pl.multiple_of(h * HD, HD), HD)
        ctx_ref[part, cols] = (mixed / summed).astype(bf16)
        return c

    def attend_units(lo, hi):
        lax.fori_loop(lo, hi, attend, 0)

    def finish_queries(half):
        for h in range(half * heads // 2, (half + 1) * heads // 2):
            qh[h] = (acc_q[:, h * HD : (h + 1) * HD] * scale[...]).astype(bf16)

    def q_stage_y(h):
        q_arrive_y(h)
        q_forward_z(h)
        q_forward(h)

    def q_stage_z(h):
        for i in (h, 2 + h):
            q_arrive_z(i)
            q_forward(4 + i)
        q_second(h)

    def q_stage_last(h):
        q_arrive_second(h)
        q_forward(2 + h)

    def q_rest(h):
        q_block(s2, h)
        for role in range(4):
            q_arrive_core(2 * role + h)
        q_block(s3, h)

    def in_place():
        for j in range(2):
            v_core_ready(j)
            place(j)

    units = heads * (tok // QT)
    per = units // 2
    fills = {
        (0, 0): [lambda: v_last(0, s, 0, 6), lambda: v_last(1, s, 0, 6)],
        (0, 1): [lambda: v_pass(0, s2, 2, 4), lambda: v_pass(1, s2, 2, 4), lambda: q_core(0)],
        (0, 2): [lambda: v_last(0, s2, 2, 8), lambda: v_last(1, s2, 2, 8), lambda: q_stage_y(0)],
        (0, 3): [in_place],
        (1, 0): [lambda: q_block(s, 0, True), lambda: q_block(s, 1, True)],
        (1, 1): [lambda: q_stage_z(0), lambda: q_stage_y(1), lambda: q_core(1), lambda: q_core(2)],
        (1, 2): [lambda: q_core(3)],
        (1, 3): [lambda: q_stage_last(0), q_core_ready, lambda: q_block(sc, 0), lambda: q_block(sc, 1)],
        (2, 0): [lambda: q_stage_z(1), lambda: q_rest(0)],
        (2, 1): [lambda: finish_queries(0), lambda: attend_units(0, 2)],
        (2, 2): [lambda: attend_units(2, 5)],
        (2, 3): [lambda: attend_units(5, per)],
        (3, 0): [lambda: q_stage_last(1), lambda: q_rest(1)],
        (3, 1): [lambda: finish_queries(1), lambda: attend_units(per, per + 2)],
        (3, 2): [lambda: attend_units(per + 2, per + 5)],
        (3, 3): [lambda: attend_units(per + 5, units)],
    }

    def fill(k, i):
        for task in fills.get((k, i), []):
            task()

    u_send, u_recv = r["u_send"], r["u_recv"]

    def give_update(k):
        sent.extend(all_tensors(lambda p: u_send.at[k], u_recv.at[k, t], r["u_s"].at[k], r["u_r"].at[k, t]))
        u_recv[k, t] = u_send[k]

    def spread_update(k):
        for d in range(1, NT):
            src = up(t, NT - d, NT)
            arrive(u_recv.at[k, src], r["u_s"].at[k, d - 1], r["u_r"].at[k, src], tensor=src)
        for i in range(NT):
            u = u_recv[k, i].astype(f32)
            for j in range(NS):
                e_send[k, j, :, i * piece : (i + 1) * piece] = u[j * rows : (j + 1) * rows]
        sent.extend(all_shards(lambda p: e_send.at[k, p], e_recv.at[k, s], r["e_s"].at[k], r["e_r"].at[k, s]))
        e_recv[k, s] = e_send[k, s]

    load_wo.wait()
    for k in range(STEPS):
        if k == 0:
            first_context()
        else:
            take_fresh(k)
            for row in range(rows):
                join_fresh(k, row, *attend_stored(row))
        c_copies = all_shards(lambda p: c_send, c_recv.at[s], r["c_s"], r["c_r"].at[s])
        c_recv[s] = c_send[...]
        settle(b_copies)
        fill(k, 0)
        for d in range(1, NS):
            src = up(s, NS - d, NS)
            arrive(c_recv.at[src], r["c_s"].at[d - 1], r["c_r"].at[src], shard=src)
        block = jnp.concatenate([c_recv[i] for i in range(NS)], axis=0).astype(bf16)
        for i in range(NT):
            d_send[i] = jnp.dot(block, wo[:, i * piece : (i + 1) * piece], preferred_element_type=f32).astype(bf16)

        d_copies = all_tensors(lambda p: d_send.at[p], d_recv.at[t], r["d_s"], r["d_r"].at[t])
        settle(c_copies)
        if k > 0:
            spread_update(k - 1)
        fill(k, 1)
        update = d_send[t].astype(f32)
        for d in range(1, NT):
            src = up(t, NT - d, NT)
            arrive(d_recv.at[src], r["d_s"].at[d - 1], r["d_r"].at[src], tensor=src)
            update = update + d_recv[src].astype(f32)
        u_send[k] = update.astype(bf16)
        if k == STEPS - 1:
            give_update(k)
            settle(d_copies)
            fill(k, 2)
            spread_update(k)
            fill(k, 3)
            break
        after = state[...] + update
        state[...] = after
        xu_send[...] = after.astype(bf16)
        x_copies = all_tensors(lambda p: xu_send, xu.at[t], r["x_s"], r["x_r"].at[t])
        xu[t] = xu_send[...]
        settle(d_copies)
        fill(k, 2)
        for d in range(1, NT):
            src = up(t, NT - d, NT)
            arrive(xu.at[src], r["x_s"].at[d - 1], r["x_r"].at[src], tensor=src)
        b_copies = decode_project()
        settle(x_copies)
        give_update(k)
        fill(k, 3)

    for k in range(STEPS):
        for d in range(1, NS):
            src = up(s, NS - d, NS)
            arrive(e_recv.at[k, src], r["e_s"].at[k, d - 1], r["e_r"].at[k, src], shard=src)
        for i in range(NS):
            out_ref[k, :, i * dblk : (i + 1) * dblk] = e_recv[k, i].astype(bf16)
    settle(sent)


def write_out(context, updates, context_out, updates_out, sem):
    copies = [
        pltpu.make_async_copy(context, context_out, sem.at[0]),
        pltpu.make_async_copy(updates, updates_out, sem.at[1]),
    ]
    for c in copies:
        c.start()
    for c in copies:
        c.wait()


def layer(lens, row_prompt, cache_len, states, x, wkv, wq, wo, cache):
    rows = states.shape[0]
    tok, width = x.shape
    dblk, qcols = wq.shape
    piece = dblk // NT
    heads = qcols // HD
    vm = pltpu.VMEM
    dma = pltpu.SemaphoreType.DMA
    bw = qcols + 3 * HD
    scratch = dict(
        xv=vm((tok, width), bf16),
        wk=vm((NS, dblk, HD), bf16),
        wv=vm((NS, dblk, HD), bf16),
        wq=vm((NS, dblk, qcols), bf16),
        wo=vm(wo.shape, bf16),
        raw=vm(cache.shape, bf16),
        ck=vm((rows, CACHE, HD), bf16),
        cv=vm((rows, CACHE, HD), bf16),
        kk=vm((MOST + NG * NS * tok, HD), bf16),
        vv=vm((MOST + NG * NS * tok, HD), bf16),
        qh=vm((heads, tok, HD), bf16),
        acc_q=vm((tok, qcols), f32),
        acc_kv=vm((2, tok, HD), f32),
        scale=vm((tok, HD), f32),
        bias=vm((tok // QT, QT, KW), f32),
        kraw=vm((2 * dblk, HD), bf16),
        ds=vm((NS, rows, dblk), f32),
        a_recv=vm((NS, rows, dblk), f32),
        xu=vm((NT, NS * rows, piece), bf16),
        xu_send=vm((NS * rows, piece), bf16),
        u_send=vm((STEPS, NS * rows, piece), bf16),
        u_recv=vm((STEPS, NT, NS * rows, piece), bf16),
        state=vm((NS * rows, piece), f32),
        b_send=vm((NS, rows, bw), f32),
        b_recv=vm((NS, rows, bw), f32),
        qs=vm((rows, heads, HD), f32),
        fkv=vm((STEPS, rows, 2 * HD), f32),
        c_send=vm((rows, qcols), f32),
        c_recv=vm((NS, rows, qcols), f32),
        d_send=vm((NT, NS * rows, piece), bf16),
        d_recv=vm((NT, NS * rows, piece), bf16),
        e_send=vm((STEPS, NS, rows, dblk), f32),
        e_recv=vm((STEPS, NS, rows, dblk), f32),
        lsem=dma((5,)),
        ky_s=dma((2, 2)),
        ky_r=dma((2, 2)),
        kz_s=dma((2, 2)),
        kz_r=dma((2, 2)),
        kc_s=dma((2, 5)),
        kc_r=dma((2, 5)),
        qy_s=dma((2,)),
        qy_r=dma((2,)),
        qz_s=dma((8,)),
        qz_r=dma((8,)),
        qc_s=dma((12,)),
        qc_r=dma((12,)),
        vy_s=dma((2,)),
        vy_r=dma((2,)),
        vz_s=dma((2, 8)),
        vz_r=dma((2, 8)),
        vc_s=dma((2, 10)),
        vc_r=dma((2, 10)),
        n_send=vm((heads, 3 * HD), f32),
        n_recv=vm((NG * NS, heads, 3 * HD), f32),
        m_send=vm((NG * NS, heads, 3 * HD), f32),
        m_recv=vm((NG * NS, heads, 3 * HD), f32),
        part0=vm((rows, heads, 3 * HD), f32),
        n_s=dma((NG * NS - 1,)),
        n_r=dma((NG * NS,)),
        m_s=dma((NG * NS - 1,)),
        m_r=dma((NG * NS,)),
        a_s=dma((NS - 1,)),
        a_r=dma((NS,)),
        b_s=dma((NS - 1,)),
        b_r=dma((NS,)),
        c_s=dma((NS - 1,)),
        c_r=dma((NS,)),
        d_s=dma((NT - 1,)),
        d_r=dma((NT,)),
        x_s=dma((NT - 1,)),
        x_r=dma((NT,)),
        u_s=dma((STEPS, NT - 1)),
        u_r=dma((STEPS, NT)),
        e_s=dma((STEPS, NS - 1)),
        e_r=dma((STEPS, NS)),
    )
    smem = pl.BlockSpec(memory_space=pltpu.SMEM)
    vmem = pl.BlockSpec(memory_space=pltpu.VMEM)
    hbm = pl.BlockSpec(memory_space=pl.ANY)
    return pl.pallas_call(
        functools.partial(kernel, tuple(scratch)),
        out_shape=(
            jax.ShapeDtypeStruct((tok, qcols), bf16),
            jax.ShapeDtypeStruct((STEPS, rows, width), bf16),
        ),
        in_specs=[smem, smem, smem, vmem, hbm, hbm, hbm, hbm, hbm],
        out_specs=(vmem, vmem),
        scratch_shapes=list(scratch.values()),
        compiler_params=pltpu.CompilerParams(
            collective_id=0, has_side_effects=True, vmem_limit_bytes=62 * 1024 * 1024
        ),
        name="attention_layer",
    )(lens, row_prompt, cache_len, states, x, wkv, wq, wo, cache)


def body(
    prompt_states,
    prompt_lens,
    w_query,
    w_keyval,
    w_out,
    decode_states,
    kv_cache,
    cache_len,
    row_prompt,
):
    dblk = w_query.shape[0]
    rows = decode_states.shape[0]
    context, updates = layer(
        prompt_lens,
        row_prompt,
        cache_len,
        decode_states,
        prompt_states,
        w_keyval.reshape(2 * dblk, HD),
        w_query,
        w_out,
        kv_cache.reshape(rows, 2 * CACHE, HD),
    )
    hbm = pl.BlockSpec(memory_space=pl.ANY)
    return pl.pallas_call(
        write_out,
        out_shape=tuple(jax.ShapeDtypeStruct(v.shape, v.dtype) for v in (context, updates)),
        in_specs=[hbm, hbm],
        out_specs=(hbm, hbm),
        scratch_shapes=[pltpu.SemaphoreType.DMA((2,))],
        compiler_params=pltpu.CompilerParams(vmem_limit_bytes=62 * 1024 * 1024),
        name="write_out",
    )(context, updates)


def solution(mesh):
    in_specs = (
        P(("group", "shard"), None),
        P(),
        P("shard", "tensor"),
        P("shard", None, "tensor"),
        P("tensor", "shard"),
        P(("group", "shard"), None),
        P(("group", "shard"), None, None, "tensor"),
        P(("group", "shard")),
        P(("group", "shard")),
    )
    out_specs = (P(("group", "shard"), "tensor"), P(None, ("group", "shard"), None))
    return jax.shard_map(body, mesh=mesh, in_specs=in_specs, out_specs=out_specs, check_vma=False)
```

```python
import functools

import jax
import jax.numpy as jnp
from jax import lax
from jax.experimental import pallas as pl
from jax.experimental.pallas import tpu as pltpu
from jax.sharding import PartitionSpec as P

HD = 128
CACHE = 2048
STEPS = 4
EPSILON = 1e-05
MESH = pl.DeviceIdType.MESH
NG = 4
NS = 4
NT = 8
MOST = 1024
QT = 256
KW = QT + MOST
INV_ROOT = HD**-0.5
LOG2E = 1.4426950408889634
TRANS = (((1,), (1,)), ((), ()))
f32 = jnp.float32
bf16 = jnp.bfloat16


def kernel(names, lens_ref, rowp_ref, clen_ref, ds_ref, x_hbm, wkv_hbm, wq_hbm, wo_hbm, cache_hbm, ctx_ref, out_ref, *scratch):
    r = dict(zip(names, scratch))
    xv, wk, wv, wq, wo, raw, ck, cv = (r[n] for n in ("xv", "wk", "wv", "wq", "wo", "raw", "ck", "cv"))
    kk, vv, qh, acc_q, acc_kv, scale, bias = (r[n] for n in ("kk", "vv", "qh", "acc_q", "acc_kv", "scale", "bias"))
    a_recv, xu, xu_send, state = (r[n] for n in ("a_recv", "xu", "xu_send", "state"))
    b_send, b_recv, qs, fkv = (r[n] for n in ("b_send", "b_recv", "qs", "fkv"))
    c_send, c_recv, d_send, d_recv = (r[n] for n in ("c_send", "c_recv", "d_send", "d_recv"))
    e_send, e_recv = r["e_send"], r["e_recv"]

    g = lax.axis_index("group")
    s = lax.axis_index("shard")
    t = lax.axis_index("tensor")
    sc = s + 1 - 2 * lax.rem(s, 2)
    s2 = lax.rem(s + 2, NS)
    s3 = lax.rem(sc + 2, NS)
    tok = xv.shape[0]
    rows = ds_ref.shape[0]
    dblk, qcols = wq.shape[1:]
    piece = dblk // NT
    heads = qcols // HD
    width = NS * dblk
    quarter = dblk // NG
    half = quarter // 2
    wide = qcols // 2

    def up(base, d, n):
        return lax.rem(base + d, n)

    def remote(src, dst, ssem, rsem, **where):
        return pltpu.make_async_remote_copy(
            src_ref=src, dst_ref=dst, send_sem=ssem, recv_sem=rsem, device_id=where, device_id_type=MESH
        )

    sent = []

    def send(src, dst, ssem, rsem, **where):
        c = remote(src, dst, ssem, rsem, **where)
        c.start()
        sent.append(c)
        return c

    def arrive(dst, ssem, rsem, **where):
        remote(dst, dst, ssem, rsem, **where).wait_recv()

    def load(a, b, i):
        c = pltpu.make_async_copy(a, b, r["lsem"].at[i])
        c.start()
        return c

    load_wkv = load(wkv_hbm, r["kraw"], 1)
    load_x = load(x_hbm, xv, 0)

    barrier = pltpu.get_barrier_semaphore()
    flat = g * NS + s
    everyone = NG * NS

    def flat_peer(d):
        f = up(flat, d, everyone)
        return f, {"group": f // NS, "shard": lax.rem(f, NS)}

    for d in range(1, everyone):
        pl.semaphore_signal(barrier, inc=1, device_id=flat_peer(d)[1], device_id_type=MESH)
    for d in range(1, NT):
        pl.semaphore_signal(barrier, inc=1, device_id={"tensor": up(t, d, NT)}, device_id_type=MESH)

    begin = jnp.int32(0)
    prompts = NG * lens_ref.shape[1]
    starts = [jnp.int32(0)] * rows
    sizes = [jnp.int32(0)] * rows
    for i in range(prompts):
        here = lens_ref[i // lens_ref.shape[1], i % lens_ref.shape[1]]
        for row in range(rows):
            hit = (rowp_ref[row] == i).astype(jnp.int32)
            starts[row] = starts[row] + hit * begin
            sizes[row] = sizes[row] + hit * here
        begin = begin + here
    b0 = lens_ref[g, 0]
    b1 = b0 + lens_ref[g, 1]
    is_new = [(rowp_ref[row] < prompts).astype(jnp.int32) for row in range(rows)]
    spots = NG * NS * tok // MOST - 1
    begin = sum(starts)
    spot = jnp.minimum(begin // MOST, spots - 1)
    low = [is_new[row] * (starts[row] - spot * MOST) for row in range(rows)]
    high = [low[row] + is_new[row] * sizes[row] + (1 - is_new[row]) * clen_ref[row] for row in range(rows)]

    out_i = lax.broadcasted_iota(jnp.int32, (256, 256), 0)
    in_i = lax.broadcasted_iota(jnp.int32, (256, 256), 1)
    want = jnp.where(out_i < 128, 2 * out_i, 2 * (out_i - 128) + 1)
    pick = (in_i == want).astype(bf16)

    load_wkv.wait()

    def separate_weights(i, c):
        pair = jnp.concatenate(
            [r["kraw"][pl.ds(pl.multiple_of((2 * i + j) * 256, 256), 256), :] for j in range(2)], axis=1
        )
        split = jnp.dot(pick, pair, preferred_element_type=f32).astype(bf16)
        for j in range(2):
            dst = pl.ds(pl.multiple_of((2 * i + j) * 128, 128), 128)
            wk[s, dst, :] = split[:128, j * HD : (j + 1) * HD]
            wv[s, dst, :] = split[128:, j * HD : (j + 1) * HD]
        return c

    lax.fori_loop(0, dblk // 256, separate_weights, 0)
    ds = r["ds"]
    for i in range(NS):
        ds[i] = ds_ref[:, i * dblk : (i + 1) * dblk].astype(f32)
    pl.semaphore_wait(barrier, everyone - 1 + NT - 1)

    weights_of, cached = (wk, wv), (kk, vv)

    def krows(j, blk, q):
        return weights_of[j].at[blk, pl.ds(pl.multiple_of(q * quarter, quarter), quarter)]

    def qrows(blk, q, h):
        return wq.at[blk, pl.ds(pl.multiple_of(q * quarter, quarter), quarter), h * wide : (h + 1) * wide]

    def qhalf(blk, q, h, n):
        return wq.at[blk, pl.ds(pl.multiple_of(q * quarter + n * half, half), half), h * wide : (h + 1) * wide]

    q_of = [g, up(g, 2, NG), up(g, 3, NG), up(g, 1, NG)]
    ky_s, ky_r, kz_s, kz_r, kc_s, kc_r = (r[n] for n in ("ky_s", "ky_r", "kz_s", "kz_r", "kc_s", "kc_r"))
    qy_s, qy_r, qz_s, qz_r, qc_s, qc_r = (r[n] for n in ("qy_s", "qy_r", "qz_s", "qz_r", "qc_s", "qc_r"))

    def y_start(src, ssem, rsem):
        c = remote(src, src, ssem, rsem, shard=s2)
        c.start()
        return c

    def k_send_y(j, i):
        return y_start(krows(j, s, q_of[i]), ky_s.at[j, i], ky_r.at[j, i])

    y_copy = k_send_y(0, 0)
    for j in range(2):
        ref = weights_of[j].at[s]
        send(ref, ref, kc_s.at[j, 4], kc_r.at[j, 4], shard=sc)
    for d in range(1, NS):
        p = up(s, d, NS)
        send(ds.at[p], a_recv.at[s], r["a_s"].at[d - 1], r["a_r"].at[s], shard=p)
    a_recv[s] = ds[s]
    r["fkv"][...] = jnp.zeros_like(fkv)
    for ref in cached:
        ref[:MOST, :] = jnp.zeros((MOST, HD), bf16)

    def k_arrive_y(j, i):
        arrive(krows(j, s2, q_of[i]), ky_s.at[j, i], ky_r.at[j, i], shard=s2)

    def k_arrive_z(j, i):
        arrive(krows(j, s2, q_of[2 + i]), kz_s.at[j, i], kz_r.at[j, i], group=q_of[2 + i])

    def k_arrive_core(j, role):
        arrive(krows(j, s3, q_of[role]), kc_s.at[j, role], kc_r.at[j, role], shard=sc)

    def k_forward(j, role):
        ref = krows(j, s2, q_of[role])
        send(ref, ref, kc_s.at[j, role], kc_r.at[j, role], shard=sc)

    def k_forward_z(j):
        ref = krows(j, s2, g)
        send(ref, ref, kz_s.at[j, 0], kz_r.at[j, 0], group=up(g, 1, NG))
        send(ref, ref, kz_s.at[j, 1], kz_r.at[j, 1], group=up(g, 3, NG))

    def q_core(q):
        ref = wq.at[s, pl.ds(q * quarter, quarter)]
        send(ref, ref, qc_s.at[8 + q], qc_r.at[8 + q], shard=sc)

    def q_core_ready():
        for q in range(NG):
            ref = wq.at[sc, pl.ds(q * quarter, quarter)]
            arrive(ref, qc_s.at[8 + q], qc_r.at[8 + q], shard=sc)

    def q_send_y(i):
        return y_start(qrows(s, g, i), qy_s.at[i], qy_r.at[i])

    def q_arrive_y(i):
        arrive(qrows(s2, g, i), qy_s.at[i], qy_r.at[i], shard=s2)

    def q_second(h):
        for n in range(2):
            ref = qhalf(s2, q_of[2 + n], h, n)
            i = 4 + 2 * h + n
            send(ref, ref, qz_s.at[i], qz_r.at[i], group=up(g, 1 + 2 * n, NG))

    def q_arrive_second(h):
        for n in range(2):
            i = 4 + 2 * h + n
            arrive(qhalf(s2, q_of[1], h, n), qz_s.at[i], qz_r.at[i], group=q_of[2 + n])

    def q_forward_z(h):
        ref = qrows(s2, g, h)
        send(ref, ref, qz_s.at[h], qz_r.at[h], group=up(g, 1, NG))
        send(ref, ref, qz_s.at[2 + h], qz_r.at[2 + h], group=up(g, 3, NG))

    def q_arrive_z(i):
        arrive(qrows(s2, q_of[2 + i // 2], i % 2), qz_s.at[i], qz_r.at[i], group=q_of[2 + i // 2])

    def q_forward(i):
        ref = qrows(s2, q_of[i // 2], i % 2)
        send(ref, ref, qc_s.at[i], qc_r.at[i], shard=sc)

    def q_arrive_core(i):
        arrive(qrows(s3, q_of[i // 2], i % 2), qc_s.at[i], qc_r.at[i], shard=sc)

    def x_block(blk):
        return xv[:, pl.ds(pl.multiple_of(blk * dblk, dblk), dblk)]

    def kv_block(j, blk, first):
        prod = jnp.dot(x_block(blk), weights_of[j][blk], preferred_element_type=f32)
        acc_kv[j] = prod if first else acc_kv[j] + prod

    def q_block(blk, h, first=False):
        def part(n, c):
            cols = pl.ds(pl.multiple_of(n * 256, 256), 256)
            prod = jnp.dot(x_block(blk), wq[blk, :, cols], preferred_element_type=f32)
            acc_q[:, cols] = prod if first else acc_q[:, cols] + prod
            return c

        lax.fori_loop(h * wide // 256, (h + 1) * wide // 256, part, 0)

    load_x.wait()
    load_wq = load(wq_hbm, wq.at[s], 2)
    load_raw = load(cache_hbm, raw, 3)
    load_wo = load(wo_hbm, wo, 4)

    def squares(i, c):
        part = pl.ds(pl.multiple_of(i * 32, 32), 32)
        v = xv[part, :].astype(f32)
        mean = jnp.sum(v * v, axis=1, keepdims=True) / width
        scale[part, :] = jnp.broadcast_to(lax.rsqrt(mean + EPSILON), (32, HD))
        return c

    def all_shards(src_of, dst, ssem, rsem):
        copies = []
        for d in range(1, NS):
            p = up(s, d, NS)
            c = remote(src_of(p), dst, ssem.at[d - 1], rsem, shard=p)
            c.start()
            copies.append(c)
        return copies

    def all_tensors(src_of, dst, ssem, rsem):
        copies = []
        for d in (4, 6, 2, 5, 3, 7, 1):
            p = up(t, d, NT)
            c = remote(src_of(p), dst, ssem.at[d - 1], rsem, tensor=p)
            c.start()
            copies.append(c)
        return copies

    def settle(copies):
        for c in copies:
            c.wait_send()

    def decode_project():
        acc = jnp.zeros((NS * rows, qcols), f32)
        acc2 = jnp.zeros((NS * rows, 2 * HD), f32)
        square = jnp.zeros((NS * rows, 1), f32)
        for i in range(NT):
            xi = xu[i]
            acc += jnp.dot(xi, wq[s, i * piece : (i + 1) * piece, :], preferred_element_type=f32)
            part = slice(i * piece, (i + 1) * piece)
            joined = jnp.concatenate([wk[s, part, :], wv[s, part, :]], axis=1)
            acc2 += jnp.dot(xi, joined, preferred_element_type=f32)
            xf = xi.astype(f32)
            square += jnp.sum(xf * xf, axis=1, keepdims=True)
        wide = jnp.broadcast_to(square, (NS * rows, HD))
        for i in range(NS):
            b_send[i, :, :qcols] = acc[i * rows : (i + 1) * rows]
            b_send[i, :, qcols : qcols + 2 * HD] = acc2[i * rows : (i + 1) * rows]
            b_send[i, :, qcols + 2 * HD :] = wide[i * rows : (i + 1) * rows]
        copies = []
        for d in range(1, NS):
            p = up(s, d, NS)
            c = remote(b_send.at[p], b_recv.at[s], r["b_s"].at[d - 1], r["b_r"].at[s], shard=p)
            c.start()
            copies.append(c)
        return copies

    def take_fresh(k):
        total = b_send[s]
        for d in range(1, NS):
            src = up(s, NS - d, NS)
            arrive(b_recv.at[src], r["b_s"].at[d - 1], r["b_r"].at[src], shard=src)
            total = total + b_recv[src]
        norm = lax.rsqrt(total[:, qcols + 2 * HD : qcols + 2 * HD + 1] / width + EPSILON)
        fresh = (total[:, : qcols + 2 * HD] * norm).astype(bf16).astype(f32)
        fkv[k] = fresh[:, qcols:]
        for row in range(rows):
            for h in range(heads):
                qs[row, h : h + 1, :] = fresh[row : row + 1, h * HD : (h + 1) * HD]

    cpos = lax.broadcasted_iota(jnp.int32, (heads, ck.shape[1]), 1)

    def attend_stored(row):
        valid = (cpos >= low[row]) & (cpos < high[row])
        scores = lax.dot_general(qs[row].astype(bf16), ck[row], TRANS, preferred_element_type=f32) * INV_ROOT
        scores = jnp.where(valid, scores, -1e30)
        top = jnp.max(scores, axis=1, keepdims=True)
        weights = jnp.where(valid, jnp.exp(scores - top), 0.0)
        summed = jnp.sum(weights, axis=1, keepdims=True)
        return top, summed, jnp.dot(weights.astype(bf16), cv[row], preferred_element_type=f32)

    def join_fresh(k, row, old, summed, mixed):
        q = qs[row]
        top = old
        news = []
        for j in range(k + 1):
            new = jnp.sum(q * fkv[j, row : row + 1, :HD], axis=1, keepdims=True) * INV_ROOT
            news.append(new)
            top = jnp.maximum(top, new)
        rescale = jnp.exp(old - top)
        summed = summed * rescale
        mixed = mixed * rescale
        for j in range(k + 1):
            weight = jnp.exp(news[j] - top)
            summed = summed + weight
            mixed = mixed + weight.astype(bf16).astype(f32) * fkv[j, row : row + 1, HD:]
        context = (mixed / summed).astype(bf16).astype(f32)
        for h in range(heads):
            c_send[row : row + 1, h * HD : (h + 1) * HD] = context[h : h + 1]

    n_send, n_recv, m_send, m_recv, part0 = (r[n] for n in ("n_send", "n_recv", "m_send", "m_recv", "part0"))
    takes32 = [jnp.broadcast_to(is_new[row], (heads, HD)).astype(f32) for row in range(rows)]

    def ask():
        q = jnp.zeros((heads, HD), f32)
        for row in range(rows):
            q = q + qs[row] * takes32[row]
        n_send[:, :HD] = q
        n_send[:, HD : 2 * HD] = jnp.broadcast_to(begin, (heads, HD)).astype(f32)
        n_send[:, 2 * HD :] = jnp.broadcast_to(begin + sum(sizes), (heads, HD)).astype(f32)
        for d in (10, 9, 11, 6, 5, 7, 8, 2, 14, 4, 12, 13, 3, 15, 1):
            send(n_send, n_recv.at[flat], r["n_s"].at[d - 1], r["n_r"].at[flat], **flat_peer(d)[1])
        n_recv[flat] = n_send[...]

    def answer():
        for d in range(1, everyone):
            f, where = flat_peer(d)
            arrive(n_recv.at[f], r["n_s"].at[d - 1], r["n_r"].at[f], **where)
        asked = n_recv[...].reshape(everyone * heads, 3 * HD)
        here = pl.ds(pl.multiple_of(MOST + flat * tok, tok), tok)
        pos = (flat * tok + lax.broadcasted_iota(jnp.int32, (everyone * heads, tok), 1)).astype(f32)
        valid = (pos >= asked[:, HD : HD + 1]) & (pos < asked[:, 2 * HD : 2 * HD + 1])
        scores = lax.dot_general(asked[:, :HD].astype(bf16), kk[here, :], TRANS, preferred_element_type=f32)
        scores = jnp.where(valid, scores * INV_ROOT, -1e30)
        top = jnp.max(scores, axis=1, keepdims=True)
        weights = jnp.where(valid, jnp.exp(scores - top), 0.0)
        summed = jnp.sum(weights, axis=1, keepdims=True)
        mixed = jnp.dot(weights.astype(bf16), vv[here, :], preferred_element_type=f32)
        shape = (everyone, heads, HD)
        m_send[:, :, :HD] = mixed.reshape(shape)
        m_send[:, :, HD : 2 * HD] = jnp.broadcast_to(top, mixed.shape).reshape(shape)
        m_send[:, :, 2 * HD :] = jnp.broadcast_to(summed, mixed.shape).reshape(shape)
        for d in (10, 9, 11, 6, 5, 7, 8, 2, 14, 4, 12, 13, 3, 15, 1):
            f, where = flat_peer(d)
            send(m_send.at[f], m_recv.at[flat], r["m_s"].at[d - 1], r["m_r"].at[flat], **where)
        m_recv[flat] = m_send[flat]

    def first_context():
        for d in range(1, everyone):
            f, where = flat_peer(d)
            arrive(m_recv.at[f], r["m_s"].at[d - 1], r["m_r"].at[f], **where)
        top = m_recv[0, :, HD : 2 * HD]
        for i in range(1, everyone):
            top = jnp.maximum(top, m_recv[i, :, HD : 2 * HD])
        summed = jnp.zeros((heads, HD), f32)
        mixed = jnp.zeros((heads, HD), f32)
        for i in range(everyone):
            rescale = jnp.exp(m_recv[i, :, HD : 2 * HD] - top)
            summed = summed + m_recv[i, :, 2 * HD :] * rescale
            mixed = mixed + m_recv[i, :, :HD] * rescale
        for row in range(rows):
            new = takes32[row] > 0
            mine = [part0[row, :, i * HD : (i + 1) * HD] for i in range(3)]
            join_fresh(
                0,
                row,
                jnp.where(new, top, mine[0])[:, :1],
                jnp.where(new, summed, mine[1])[:, :1],
                jnp.where(new, mixed, mine[2]),
            )

    y_copy.wait_send()
    y_copy = k_send_y(1, 0)
    for j in range(2):
        kv_block(j, s, True)
    k_arrive_y(0, 0)
    k_forward_z(0)
    k_forward(0, 0)
    y_copy.wait_send()
    y_copy = k_send_y(0, 1)

    for d in range(1, NS):
        src = up(s, NS - d, NS)
        arrive(a_recv.at[src], r["a_s"].at[d - 1], r["a_r"].at[src], shard=src)
    x0 = jnp.concatenate([a_recv[i] for i in range(NS)], axis=0)
    for i in range(NT):
        xu[i] = x0[:, i * piece : (i + 1) * piece].astype(bf16)
    mine = pl.ds(pl.multiple_of(t * piece, piece), piece)
    state[...] = jnp.concatenate([a_recv[i, :, mine] for i in range(NS)], axis=0)

    k_arrive_y(1, 0)
    k_forward_z(1)
    k_forward(1, 0)
    y_copy.wait_send()
    y_copy = k_send_y(1, 1)
    load_wq.wait()
    b_copies = decode_project()

    def slot(j, gg, ss):
        return cached[j].at[pl.ds(pl.multiple_of(MOST + (gg * NS + ss) * tok, tok), tok)]

    def half_slot(j, gg, ss, h):
        n = tok // 2
        return cached[j].at[pl.ds(pl.multiple_of(MOST + (gg * NS + ss) * tok + h * n, n), n)]

    vy_s, vy_r, vz_s, vz_r, vc_s, vc_r = (r[n] for n in ("vy_s", "vy_r", "vz_s", "vz_r", "vc_s", "vc_r"))
    below, above = up(g, 3, NG), up(g, 1, NG)

    def v_core(j, ref, i):
        send(ref, ref, vc_s.at[j, i], vc_r.at[j, i], shard=sc)

    def v_sides(j, ss, i):
        ref = slot(j, g, ss)
        send(ref, ref, vz_s.at[j, i], vz_r.at[j, i], group=above)
        send(ref, ref, vz_s.at[j, i + 1], vz_r.at[j, i + 1], group=below)

    def v_pass(j, ss, i, core):
        for h, (source, target) in enumerate([(below, above), (above, below)]):
            arrive(slot(j, source, ss), vz_s.at[j, i + h], vz_r.at[j, i + h], group=source)
            ref = half_slot(j, source, ss, h)
            send(ref, ref, vz_s.at[j, i + 4 + h], vz_r.at[j, i + 4 + h], group=target)
            v_core(j, slot(j, source, ss), core + h)

    def v_last(j, ss, i, core):
        for h, source in enumerate([below, above]):
            ref = half_slot(j, up(g, 2, NG), ss, h)
            arrive(ref, vz_s.at[j, i + 4 + h], vz_r.at[j, i + 4 + h], group=source)
            v_core(j, ref, core + h)

    def v_theirs(j):
        ref = slot(j, g, s2)
        arrive(ref, vy_s.at[j], vy_r.at[j], shard=s2)
        v_sides(j, s2, 2)
        v_core(j, ref, 1)

    def v_core_ready(j):
        for i, ref in enumerate(
            [slot(j, g, sc), slot(j, g, s3)]
            + [slot(j, gg, ss) for ss in (sc, s3) for gg in (below, above)]
            + [half_slot(j, up(g, 2, NG), ss, h) for ss in (sc, s3) for h in range(2)]
        ):
            arrive(ref, vc_s.at[j, i], vc_r.at[j, i], shard=sc)

    def k_gather(j):
        k_arrive_z(j, 0)
        k_forward(j, 2)
        k_arrive_z(j, 1)
        k_forward(j, 3)
        k_arrive_y(j, 1)
        k_forward(j, 1)

    def v_make(j):
        arrive(weights_of[j].at[sc], kc_s.at[j, 4], kc_r.at[j, 4], shard=sc)
        kv_block(j, sc, False)
        kv_block(j, s2, False)
        for role in (0, 2, 3, 1):
            k_arrive_core(j, role)
        kv_block(j, s3, False)
        cached[j][pl.ds(pl.multiple_of(MOST + (g * NS + s) * tok, tok), tok), :] = (acc_kv[j] * scale[...]).astype(
            bf16
        )
        own = slot(j, g, s)
        c = y_start(own, vy_s.at[j], vy_r.at[j])
        v_sides(j, s, 0)
        v_core(j, own, 0)
        return c

    lax.fori_loop(0, tok // 32, squares, 0)
    k_gather(0)
    y_copy.wait_send()
    y_copy = v_make(0)
    k_gather(1)
    take_fresh(0)
    ask()
    y_copy.wait_send()
    y_copy = v_make(1)
    v_theirs(0)
    v_pass(0, s, 0, 2)
    answer()
    y_copy.wait_send()
    q_copies = [q_send_y(0)]
    v_theirs(1)
    v_pass(1, s, 0, 2)

    load_raw.wait()
    def separate(i, c):
        src = pl.ds(pl.multiple_of(i * 256, 256), 256)
        dst = pl.ds(pl.multiple_of(i * 128, 128), 128)
        for row in range(0, rows, 2):
            pair = jnp.concatenate([raw[row, src, :], raw[row + 1, src, :]], axis=1)
            split = jnp.dot(pick, pair, preferred_element_type=f32).astype(bf16)
            for j in range(2):
                ck[row + j, dst, :] = split[:128, j * HD : (j + 1) * HD]
                cv[row + j, dst, :] = split[128:, j * HD : (j + 1) * HD]
        return c

    lax.fori_loop(0, 2 * ck.shape[1] // 256, separate, 0)
    for row in range(rows):
        for i, v in enumerate(attend_stored(row)):
            part0[row, :, i * HD : (i + 1) * HD] = jnp.broadcast_to(v, (heads, HD))
    v_last(0, s, 0, 6)
    v_pass(0, s2, 2, 4)

    def build_mask():
        for i in range(tok // QT):
            q_pos = s * tok + i * QT + lax.broadcasted_iota(jnp.int32, (QT, KW), 0)
            k_pos = s * tok + i * QT - MOST + lax.broadcasted_iota(jnp.int32, (QT, KW), 1)
            start = jnp.where(q_pos >= b1, b1, jnp.where(q_pos >= b0, b0, 0))
            bias[i] = jnp.where((k_pos >= start) & (k_pos <= q_pos), 0.0, -1e30)

    def splat(flag):
        return jnp.broadcast_to(flag, (HD, HD)).astype(f32).astype(bf16)

    at_spot = [splat((spot == j).astype(jnp.int32)) for j in range(spots)]
    takes = [splat(is_new[row]) for row in range(rows)]

    def place(j):
        stored = (ck, cv)[j]

        def part(i, c):
            dst = pl.ds(pl.multiple_of(i * HD, HD), HD)
            window = jnp.zeros((HD, HD), bf16)
            for n in range(spots):
                src = pl.ds(pl.multiple_of((1 + n) * MOST + i * HD, HD), HD)
                window = window + cached[j][src, :] * at_spot[n]
            for row in range(rows):
                stored[row, dst, :] = stored[row, dst, :] * (1 - takes[row]) + window * takes[row]
            return c

        lax.fori_loop(0, 2 * MOST // HD, part, 0)

    def attend(u, c):
        h = u // (tok // QT)
        i = lax.rem(u, tok // QT)
        part = pl.ds(pl.multiple_of(i * QT, QT), QT)
        keys = pl.ds(pl.multiple_of((g * NS + s) * tok + i * QT, QT), KW)
        scores = lax.dot_general(qh[h, part, :], kk[keys, :], TRANS, preferred_element_type=f32)
        scores = scores + bias[i]
        high = jnp.max(scores, axis=1, keepdims=True)
        weights = jnp.exp2((scores - high) * (INV_ROOT * LOG2E))
        summed = jnp.sum(weights, axis=1, keepdims=True)
        mixed = jnp.dot(weights.astype(bf16), vv[keys, :], preferred_element_type=f32)
        cols = pl.ds(pl.multiple_of(h * HD, HD), HD)
        ctx_ref[part, cols] = (mixed / summed).astype(bf16)
        return c

    def attend_units(lo, hi):
        lax.fori_loop(lo, hi, attend, 0)

    def finish_queries(half):
        for h in range(half * heads // 2, (half + 1) * heads // 2):
            qh[h] = (acc_q[:, h * HD : (h + 1) * HD] * scale[...]).astype(bf16)

    def q_stage_y(h):
        q_arrive_y(h)
        q_forward_z(h)
        q_forward(h)

    def q_stage_z(h):
        for i in (h, 2 + h):
            q_arrive_z(i)
            q_forward(4 + i)
        q_second(h)

    def q_stage_last(h):
        q_arrive_second(h)
        q_forward(2 + h)

    def q_rest(h):
        q_block(s2, h)
        for role in range(4):
            q_arrive_core(2 * role + h)
        q_block(s3, h)

    def in_place():
        for j in range(2):
            v_core_ready(j)
            place(j)

    units = heads * (tok // QT)
    per = units // 2
    def q_next():
        q_copies[0].wait_send()
        q_copies.append(q_send_y(1))

    fills = {
        (0, 0): [lambda: v_last(1, s, 0, 6), lambda: v_pass(1, s2, 2, 4)],
        (0, 1): [lambda: v_last(0, s2, 2, 8), lambda: v_last(1, s2, 2, 8), lambda: q_core(0), lambda: q_core(1)],
        (0, 2): [q_next, lambda: q_stage_y(0)],
        (0, 3): [in_place],
        (1, 0): [lambda: q_core(2), lambda: q_core(3), lambda: q_block(s, 0, True), lambda: q_block(s, 1, True)],
        (1, 1): [lambda: q_stage_y(1), build_mask],
        (1, 2): [lambda: q_stage_z(0)],
        (1, 3): [q_core_ready, lambda: q_block(sc, 0), lambda: q_block(sc, 1)],
        (2, 0): [lambda: q_stage_last(0)],
        (2, 1): [lambda: q_stage_z(1), lambda: q_rest(0)],
        (2, 2): [lambda: finish_queries(0), lambda: attend_units(0, 2)],
        (2, 3): [lambda: attend_units(2, 5)],
        (3, 0): [lambda: q_stage_last(1), lambda: attend_units(5, per)],
        (3, 1): [lambda: q_rest(1)],
        (3, 2): [lambda: finish_queries(1), lambda: attend_units(per, per + 3)],
        (3, 3): [lambda: attend_units(per + 3, units)],
    }

    def fill(k, i):
        for task in fills.get((k, i), []):
            task()

    u_send, u_recv = r["u_send"], r["u_recv"]

    def give_update(k):
        sent.extend(all_tensors(lambda p: u_send.at[k], u_recv.at[k, t], r["u_s"].at[k], r["u_r"].at[k, t]))
        u_recv[k, t] = u_send[k]

    def spread_update(k):
        for d in range(1, NT):
            src = up(t, NT - d, NT)
            arrive(u_recv.at[k, src], r["u_s"].at[k, d - 1], r["u_r"].at[k, src], tensor=src)
        for i in range(NT):
            u = u_recv[k, i].astype(f32)
            for j in range(NS):
                e_send[k, j, :, i * piece : (i + 1) * piece] = u[j * rows : (j + 1) * rows]
        sent.extend(all_shards(lambda p: e_send.at[k, p], e_recv.at[k, s], r["e_s"].at[k], r["e_r"].at[k, s]))
        e_recv[k, s] = e_send[k, s]

    load_wo.wait()
    for k in range(STEPS):
        if k == 0:
            first_context()
        else:
            take_fresh(k)
            for row in range(rows):
                join_fresh(k, row, *attend_stored(row))
        c_copies = all_shards(lambda p: c_send, c_recv.at[s], r["c_s"], r["c_r"].at[s])
        c_recv[s] = c_send[...]
        settle(b_copies)
        fill(k, 0)
        for d in range(1, NS):
            src = up(s, NS - d, NS)
            arrive(c_recv.at[src], r["c_s"].at[d - 1], r["c_r"].at[src], shard=src)
        block = jnp.concatenate([c_recv[i] for i in range(NS)], axis=0).astype(bf16)
        for i in range(NT):
            d_send[i] = jnp.dot(block, wo[:, i * piece : (i + 1) * piece], preferred_element_type=f32).astype(bf16)

        d_copies = all_tensors(lambda p: d_send.at[p], d_recv.at[t], r["d_s"], r["d_r"].at[t])
        settle(c_copies)
        if k > 0:
            spread_update(k - 1)
        fill(k, 1)
        update = d_send[t].astype(f32)
        for d in range(1, NT):
            src = up(t, NT - d, NT)
            arrive(d_recv.at[src], r["d_s"].at[d - 1], r["d_r"].at[src], tensor=src)
            update = update + d_recv[src].astype(f32)
        u_send[k] = update.astype(bf16)
        if k == STEPS - 1:
            give_update(k)
            settle(d_copies)
            fill(k, 2)
            spread_update(k)
            fill(k, 3)
            break
        after = state[...] + update
        state[...] = after
        xu_send[...] = after.astype(bf16)
        x_copies = all_tensors(lambda p: xu_send, xu.at[t], r["x_s"], r["x_r"].at[t])
        xu[t] = xu_send[...]
        settle(d_copies)
        fill(k, 2)
        for d in range(1, NT):
            src = up(t, NT - d, NT)
            arrive(xu.at[src], r["x_s"].at[d - 1], r["x_r"].at[src], tensor=src)
        b_copies = decode_project()
        settle(x_copies)
        give_update(k)
        fill(k, 3)

    for k in range(STEPS):
        for d in range(1, NS):
            src = up(s, NS - d, NS)
            arrive(e_recv.at[k, src], r["e_s"].at[k, d - 1], r["e_r"].at[k, src], shard=src)
        for i in range(NS):
            out_ref[k, :, i * dblk : (i + 1) * dblk] = e_recv[k, i].astype(bf16)
    q_copies[1].wait_send()
    settle(sent)


def write_out(context, updates, context_out, updates_out):
    context_out[...] = context[...]
    updates_out[...] = updates[...]


def layer(lens, row_prompt, cache_len, states, x, wkv, wq, wo, cache):
    rows = states.shape[0]
    tok, width = x.shape
    dblk, qcols = wq.shape
    piece = dblk // NT
    heads = qcols // HD
    vm = pltpu.VMEM
    dma = pltpu.SemaphoreType.DMA
    bw = qcols + 3 * HD
    scratch = dict(
        xv=vm((tok, width), bf16),
        wk=vm((NS, dblk, HD), bf16),
        wv=vm((NS, dblk, HD), bf16),
        wq=vm((NS, dblk, qcols), bf16),
        wo=vm(wo.shape, bf16),
        raw=vm(cache.shape, bf16),
        ck=vm((rows, CACHE, HD), bf16),
        cv=vm((rows, CACHE, HD), bf16),
        kk=vm((MOST + NG * NS * tok, HD), bf16),
        vv=vm((MOST + NG * NS * tok, HD), bf16),
        qh=vm((heads, tok, HD), bf16),
        acc_q=vm((tok, qcols), f32),
        acc_kv=vm((2, tok, HD), f32),
        scale=vm((tok, HD), f32),
        bias=vm((tok // QT, QT, KW), f32),
        kraw=vm((2 * dblk, HD), bf16),
        ds=vm((NS, rows, dblk), f32),
        a_recv=vm((NS, rows, dblk), f32),
        xu=vm((NT, NS * rows, piece), bf16),
        xu_send=vm((NS * rows, piece), bf16),
        u_send=vm((STEPS, NS * rows, piece), bf16),
        u_recv=vm((STEPS, NT, NS * rows, piece), bf16),
        state=vm((NS * rows, piece), f32),
        b_send=vm((NS, rows, bw), f32),
        b_recv=vm((NS, rows, bw), f32),
        qs=vm((rows, heads, HD), f32),
        fkv=vm((STEPS, rows, 2 * HD), f32),
        c_send=vm((rows, qcols), f32),
        c_recv=vm((NS, rows, qcols), f32),
        d_send=vm((NT, NS * rows, piece), bf16),
        d_recv=vm((NT, NS * rows, piece), bf16),
        e_send=vm((STEPS, NS, rows, dblk), f32),
        e_recv=vm((STEPS, NS, rows, dblk), f32),
        lsem=dma((5,)),
        ky_s=dma((2, 2)),
        ky_r=dma((2, 2)),
        kz_s=dma((2, 2)),
        kz_r=dma((2, 2)),
        kc_s=dma((2, 5)),
        kc_r=dma((2, 5)),
        qy_s=dma((2,)),
        qy_r=dma((2,)),
        qz_s=dma((8,)),
        qz_r=dma((8,)),
        qc_s=dma((12,)),
        qc_r=dma((12,)),
        vy_s=dma((2,)),
        vy_r=dma((2,)),
        vz_s=dma((2, 8)),
        vz_r=dma((2, 8)),
        vc_s=dma((2, 10)),
        vc_r=dma((2, 10)),
        n_send=vm((heads, 3 * HD), f32),
        n_recv=vm((NG * NS, heads, 3 * HD), f32),
        m_send=vm((NG * NS, heads, 3 * HD), f32),
        m_recv=vm((NG * NS, heads, 3 * HD), f32),
        part0=vm((rows, heads, 3 * HD), f32),
        n_s=dma((NG * NS - 1,)),
        n_r=dma((NG * NS,)),
        m_s=dma((NG * NS - 1,)),
        m_r=dma((NG * NS,)),
        a_s=dma((NS - 1,)),
        a_r=dma((NS,)),
        b_s=dma((NS - 1,)),
        b_r=dma((NS,)),
        c_s=dma((NS - 1,)),
        c_r=dma((NS,)),
        d_s=dma((NT - 1,)),
        d_r=dma((NT,)),
        x_s=dma((NT - 1,)),
        x_r=dma((NT,)),
        u_s=dma((STEPS, NT - 1)),
        u_r=dma((STEPS, NT)),
        e_s=dma((STEPS, NS - 1)),
        e_r=dma((STEPS, NS)),
    )
    smem = pl.BlockSpec(memory_space=pltpu.SMEM)
    vmem = pl.BlockSpec(memory_space=pltpu.VMEM)
    hbm = pl.BlockSpec(memory_space=pl.ANY)
    return pl.pallas_call(
        functools.partial(kernel, tuple(scratch)),
        out_shape=(
            jax.ShapeDtypeStruct((tok, qcols), bf16),
            jax.ShapeDtypeStruct((STEPS, rows, width), bf16),
        ),
        in_specs=[smem, smem, smem, vmem, hbm, hbm, hbm, hbm, hbm],
        out_specs=(vmem, vmem),
        scratch_shapes=list(scratch.values()),
        compiler_params=pltpu.CompilerParams(
            collective_id=0, has_side_effects=True, vmem_limit_bytes=62 * 1024 * 1024
        ),
        name="attention_layer",
    )(lens, row_prompt, cache_len, states, x, wkv, wq, wo, cache)


def body(
    prompt_states,
    prompt_lens,
    w_query,
    w_keyval,
    w_out,
    decode_states,
    kv_cache,
    cache_len,
    row_prompt,
):
    dblk = w_query.shape[0]
    rows = decode_states.shape[0]
    context, updates = layer(
        prompt_lens,
        row_prompt,
        cache_len,
        decode_states,
        prompt_states,
        w_keyval.reshape(2 * dblk, HD),
        w_query,
        w_out,
        kv_cache.reshape(rows, 2 * CACHE, HD),
    )
    vmem = pl.BlockSpec(memory_space=pltpu.VMEM)
    return pl.pallas_call(
        write_out,
        out_shape=tuple(jax.ShapeDtypeStruct(v.shape, v.dtype) for v in (context, updates)),
        in_specs=[vmem, vmem],
        out_specs=(vmem, vmem),
        name="write_out",
    )(context, updates)


def solution(mesh):
    in_specs = (
        P(("group", "shard"), None),
        P(),
        P("shard", "tensor"),
        P("shard", None, "tensor"),
        P("tensor", "shard"),
        P(("group", "shard"), None),
        P(("group", "shard"), None, None, "tensor"),
        P(("group", "shard")),
        P(("group", "shard")),
    )
    out_specs = (P(("group", "shard"), "tensor"), P(None, ("group", "shard"), None))
    return jax.shard_map(body, mesh=mesh, in_specs=in_specs, out_specs=out_specs, check_vma=False)
```

```python
import functools

import jax
import jax.numpy as jnp
from jax import lax
from jax.experimental import pallas as pl
from jax.experimental.pallas import tpu as pltpu
from jax.sharding import PartitionSpec as P

HD = 128
CACHE = 2048
STEPS = 4
EPSILON = 1e-05
MESH = pl.DeviceIdType.MESH
NG = 4
NS = 4
NT = 8
MOST = 1024
QT = 256
KW = QT + MOST
INV_ROOT = HD**-0.5
LOG2E = 1.4426950408889634
TRANS = (((1,), (1,)), ((), ()))
f32 = jnp.float32
bf16 = jnp.bfloat16


def kernel(names, lens_ref, rowp_ref, clen_ref, ds_ref, x_hbm, wkv_hbm, wq_hbm, wo_hbm, cache_hbm, ctx_ref, out_ref, *scratch):
    r = dict(zip(names, scratch))
    xv, wk, wv, wq, wo, raw, ck, cv = (r[n] for n in ("xv", "wk", "wv", "wq", "wo", "raw", "ck", "cv"))
    kk, vv, qh, acc_q, acc_kv, scale, bias = (r[n] for n in ("kk", "vv", "qh", "acc_q", "acc_kv", "scale", "bias"))
    a_recv, xu, xu_send, state = (r[n] for n in ("a_recv", "xu", "xu_send", "state"))
    b_send, b_recv, qs, fkv = (r[n] for n in ("b_send", "b_recv", "qs", "fkv"))
    c_send, c_recv, d_send, d_recv = (r[n] for n in ("c_send", "c_recv", "d_send", "d_recv"))
    e_send, e_recv = r["e_send"], r["e_recv"]

    g = lax.axis_index("group")
    s = lax.axis_index("shard")
    t = lax.axis_index("tensor")
    sc = s + 1 - 2 * lax.rem(s, 2)
    s2 = lax.rem(s + 2, NS)
    s3 = lax.rem(sc + 2, NS)
    tok = xv.shape[0]
    rows = ds_ref.shape[0]
    dblk, qcols = wq.shape[1:]
    piece = dblk // NT
    heads = qcols // HD
    width = NS * dblk
    quarter = dblk // NG
    half = quarter // 2

    def up(base, d, n):
        return lax.rem(base + d, n)

    def remote(src, dst, ssem, rsem, **where):
        return pltpu.make_async_remote_copy(
            src_ref=src, dst_ref=dst, send_sem=ssem, recv_sem=rsem, device_id=where, device_id_type=MESH
        )

    sent = []

    def send(src, dst, ssem, rsem, **where):
        c = remote(src, dst, ssem, rsem, **where)
        c.start()
        sent.append(c)
        return c

    def arrive(dst, ssem, rsem, **where):
        remote(dst, dst, ssem, rsem, **where).wait_recv()

    def load(a, b, i):
        c = pltpu.make_async_copy(a, b, r["lsem"].at[i])
        c.start()
        return c

    load_wkv = load(wkv_hbm, r["kraw"], 1)
    load_x = load(x_hbm, xv, 0)
    load_wq = load(wq_hbm, wq.at[s], 2)

    barrier = pltpu.get_barrier_semaphore()
    for d in range(1, NS):
        pl.semaphore_signal(barrier, inc=1, device_id={"shard": up(s, d, NS)}, device_id_type=MESH)
    for d in range(1, NG):
        pl.semaphore_signal(barrier, inc=1, device_id={"group": up(g, d, NG)}, device_id_type=MESH)
    for d in range(1, NT):
        pl.semaphore_signal(barrier, inc=1, device_id={"tensor": up(t, d, NT)}, device_id_type=MESH)

    begin = jnp.int32(0)
    prompts = NG * lens_ref.shape[1]
    starts = [jnp.int32(0)] * rows
    sizes = [jnp.int32(0)] * rows
    for i in range(prompts):
        here = lens_ref[i // lens_ref.shape[1], i % lens_ref.shape[1]]
        for row in range(rows):
            hit = (rowp_ref[row] == i).astype(jnp.int32)
            starts[row] = starts[row] + hit * begin
            sizes[row] = sizes[row] + hit * here
        begin = begin + here
    b0 = lens_ref[g, 0]
    b1 = b0 + lens_ref[g, 1]
    is_new = [(rowp_ref[row] < prompts).astype(jnp.int32) for row in range(rows)]
    spots = NG * NS * tok // MOST - 1
    begin = sum(starts)
    spot = jnp.minimum(begin // MOST, spots - 1)
    low = [is_new[row] * (starts[row] - spot * MOST) for row in range(rows)]
    high = [low[row] + is_new[row] * sizes[row] + (1 - is_new[row]) * clen_ref[row] for row in range(rows)]

    out_i = lax.broadcasted_iota(jnp.int32, (256, 256), 0)
    in_i = lax.broadcasted_iota(jnp.int32, (256, 256), 1)
    want = jnp.where(out_i < 128, 2 * out_i, 2 * (out_i - 128) + 1)
    pick = (in_i == want).astype(bf16)

    load_wkv.wait()

    def separate_weights(i, c):
        pair = jnp.concatenate(
            [r["kraw"][pl.ds(pl.multiple_of((2 * i + j) * 256, 256), 256), :] for j in range(2)], axis=1
        )
        split = jnp.dot(pick, pair, preferred_element_type=f32).astype(bf16)
        for j in range(2):
            dst = pl.ds(pl.multiple_of((2 * i + j) * 128, 128), 128)
            wk[s, dst, :] = split[:128, j * HD : (j + 1) * HD]
            wv[s, dst, :] = split[128:, j * HD : (j + 1) * HD]
        return c

    lax.fori_loop(0, dblk // 256, separate_weights, 0)
    ds = r["ds"]
    for i in range(NS):
        ds[i] = ds_ref[:, i * dblk : (i + 1) * dblk].astype(f32)
    pl.semaphore_wait(barrier, NS - 1 + NG - 1 + NT - 1)

    weights_of, cached = (wk, wv), (kk, vv)

    def krows(j, blk, q):
        return weights_of[j].at[blk, pl.ds(pl.multiple_of(q * quarter, quarter), quarter)]

    def qrows(blk, q, h):
        return wq.at[blk, pl.ds(pl.multiple_of(q * quarter + h * half, half), half)]

    q_of = [g, up(g, 2, NG), up(g, 3, NG), up(g, 1, NG)]
    ky_s, ky_r, kz_s, kz_r, kc_s, kc_r = (r[n] for n in ("ky_s", "ky_r", "kz_s", "kz_r", "kc_s", "kc_r"))
    qy_s, qy_r, qz_s, qz_r, qc_s, qc_r = (r[n] for n in ("qy_s", "qy_r", "qz_s", "qz_r", "qc_s", "qc_r"))

    for i, j in ((0, 0), (0, 1), (1, 0), (1, 1)):
        ref = krows(j, s, q_of[i])
        send(ref, ref, ky_s.at[j, i], ky_r.at[j, i], shard=s2)
    for j in range(2):
        ref = weights_of[j].at[s]
        send(ref, ref, kc_s.at[j, 4], kc_r.at[j, 4], shard=sc)
    for d in range(1, NS):
        p = up(s, d, NS)
        send(ds.at[p], a_recv.at[s], r["a_s"].at[d - 1], r["a_r"].at[s], shard=p)
    a_recv[s] = ds[s]
    r["fkv"][...] = jnp.zeros_like(fkv)
    for ref in cached:
        ref[:MOST, :] = jnp.zeros((MOST, HD), bf16)

    def k_arrive_y(j, i):
        arrive(krows(j, s2, q_of[i]), ky_s.at[j, i], ky_r.at[j, i], shard=s2)

    def k_arrive_z(j, i):
        arrive(krows(j, s2, q_of[2 + i]), kz_s.at[j, i], kz_r.at[j, i], group=q_of[2 + i])

    def k_arrive_core(j, role):
        arrive(krows(j, s3, q_of[role]), kc_s.at[j, role], kc_r.at[j, role], shard=sc)

    def k_forward(j, role):
        ref = krows(j, s2, q_of[role])
        send(ref, ref, kc_s.at[j, role], kc_r.at[j, role], shard=sc)

    def k_forward_z(j):
        ref = krows(j, s2, g)
        send(ref, ref, kz_s.at[j, 0], kz_r.at[j, 0], group=up(g, 1, NG))
        send(ref, ref, kz_s.at[j, 1], kz_r.at[j, 1], group=up(g, 3, NG))

    def q_core(q):
        ref = wq.at[s, pl.ds(q * quarter, quarter)]
        send(ref, ref, qc_s.at[8 + q], qc_r.at[8 + q], shard=sc)

    def q_core_ready():
        for q in range(NG):
            ref = wq.at[sc, pl.ds(q * quarter, quarter)]
            arrive(ref, qc_s.at[8 + q], qc_r.at[8 + q], shard=sc)

    def q_send_y(i):
        ref = qrows(s, g, i)
        c = remote(ref, ref, qy_s.at[i], qy_r.at[i], shard=s2)
        c.start()
        return c

    def q_arrive_y(i):
        arrive(qrows(s2, g, i), qy_s.at[i], qy_r.at[i], shard=s2)

    def q_second(h):
        ref = qrows(s2, q_of[2 + h], h)
        send(ref, ref, qz_s.at[4 + h], qz_r.at[4 + h], group=up(g, 1 + 2 * h, NG))

    def q_arrive_second(h):
        arrive(qrows(s2, q_of[1], h), qz_s.at[4 + h], qz_r.at[4 + h], group=q_of[2 + h])

    def q_forward_z(h):
        ref = qrows(s2, g, h)
        send(ref, ref, qz_s.at[h], qz_r.at[h], group=up(g, 1, NG))
        send(ref, ref, qz_s.at[2 + h], qz_r.at[2 + h], group=up(g, 3, NG))

    def q_arrive_z(i):
        arrive(qrows(s2, q_of[2 + i // 2], i % 2), qz_s.at[i], qz_r.at[i], group=q_of[2 + i // 2])

    def q_forward(i):
        ref = qrows(s2, q_of[i // 2], i % 2)
        send(ref, ref, qc_s.at[i], qc_r.at[i], shard=sc)

    def q_arrive_core(i):
        arrive(qrows(s3, q_of[i // 2], i % 2), qc_s.at[i], qc_r.at[i], shard=sc)

    def x_block(blk):
        return xv[:, pl.ds(pl.multiple_of(blk * dblk, dblk), dblk)]

    def kv_block(j, blk, first):
        prod = jnp.dot(x_block(blk), weights_of[j][blk], preferred_element_type=f32)
        acc_kv[j] = prod if first else acc_kv[j] + prod

    def q_block(blk, first, lo=0, hi=None):
        hi = qcols // 256 if hi is None else hi

        def part(n, c):
            cols = pl.ds(pl.multiple_of(n * 256, 256), 256)
            prod = jnp.dot(x_block(blk), wq[blk, :, cols], preferred_element_type=f32)
            acc_q[:, cols] = prod if first else acc_q[:, cols] + prod
            return c

        lax.fori_loop(lo, hi, part, 0)

    load_x.wait()
    load_raw = load(cache_hbm, raw, 3)
    load_wo = load(wo_hbm, wo, 4)

    def squares(i, c):
        part = pl.ds(pl.multiple_of(i * 32, 32), 32)
        v = xv[part, :].astype(f32)
        mean = jnp.sum(v * v, axis=1, keepdims=True) / width
        scale[part, :] = jnp.broadcast_to(lax.rsqrt(mean + EPSILON), (32, HD))
        return c

    for j in range(2):
        kv_block(j, s, True)
    k_arrive_y(0, 0)
    k_forward_z(0)
    k_forward(0, 0)
    lax.fori_loop(0, tok // 32, squares, 0)
    k_arrive_y(1, 0)
    k_forward_z(1)
    k_forward(1, 0)

    for d in range(1, NS):
        src = up(s, NS - d, NS)
        arrive(a_recv.at[src], r["a_s"].at[d - 1], r["a_r"].at[src], shard=src)
    x0 = jnp.concatenate([a_recv[i] for i in range(NS)], axis=0)
    for i in range(NT):
        xu[i] = x0[:, i * piece : (i + 1) * piece].astype(bf16)
    mine = pl.ds(pl.multiple_of(t * piece, piece), piece)
    state[...] = jnp.concatenate([a_recv[i, :, mine] for i in range(NS)], axis=0)

    def slot(j, gg, ss):
        return cached[j].at[pl.ds(pl.multiple_of(MOST + (gg * NS + ss) * tok, tok), tok)]

    def half_slot(j, gg, ss, h):
        n = tok // 2
        return cached[j].at[pl.ds(pl.multiple_of(MOST + (gg * NS + ss) * tok + h * n, n), n)]

    vy_s, vy_r, vz_s, vz_r, vc_s, vc_r = (r[n] for n in ("vy_s", "vy_r", "vz_s", "vz_r", "vc_s", "vc_r"))
    below, above = up(g, 3, NG), up(g, 1, NG)

    def v_core(j, ref, i):
        send(ref, ref, vc_s.at[j, i], vc_r.at[j, i], shard=sc)

    def v_sides(j, ss, i):
        ref = slot(j, g, ss)
        send(ref, ref, vz_s.at[j, i], vz_r.at[j, i], group=above)
        send(ref, ref, vz_s.at[j, i + 1], vz_r.at[j, i + 1], group=below)

    def v_pass(j, ss, i, core):
        for h, (source, target) in enumerate([(below, above), (above, below)]):
            arrive(slot(j, source, ss), vz_s.at[j, i + h], vz_r.at[j, i + h], group=source)
            ref = half_slot(j, source, ss, h)
            send(ref, ref, vz_s.at[j, i + 4 + h], vz_r.at[j, i + 4 + h], group=target)
            v_core(j, slot(j, source, ss), core + h)

    def v_last(j, ss, i, core):
        for h, source in enumerate([below, above]):
            ref = half_slot(j, up(g, 2, NG), ss, h)
            arrive(ref, vz_s.at[j, i + 4 + h], vz_r.at[j, i + 4 + h], group=source)
            v_core(j, ref, core + h)

    def v_theirs(j):
        ref = slot(j, g, s2)
        arrive(ref, vy_s.at[j], vy_r.at[j], shard=s2)
        v_sides(j, s2, 2)
        v_core(j, ref, 1)

    def v_core_ready(j):
        for i, ref in enumerate(
            [slot(j, g, sc), slot(j, g, s3)]
            + [slot(j, gg, ss) for ss in (sc, s3) for gg in (below, above)]
            + [half_slot(j, up(g, 2, NG), ss, h) for ss in (sc, s3) for h in range(2)]
        ):
            arrive(ref, vc_s.at[j, i], vc_r.at[j, i], shard=sc)

    for j in range(2):
        k_arrive_z(j, 0)
        k_forward(j, 2)
        k_arrive_z(j, 1)
        k_forward(j, 3)
        k_arrive_y(j, 1)
        k_forward(j, 1)
        arrive(weights_of[j].at[sc], kc_s.at[j, 4], kc_r.at[j, 4], shard=sc)
        kv_block(j, sc, False)
        kv_block(j, s2, False)
        for role in (0, 2, 3, 1):
            k_arrive_core(j, role)
        kv_block(j, s3, False)
        cached[j][pl.ds(pl.multiple_of(MOST + (g * NS + s) * tok, tok), tok), :] = (acc_kv[j] * scale[...]).astype(
            bf16
        )
        own = slot(j, g, s)
        send(own, own, vy_s.at[j], vy_r.at[j], shard=s2)
        v_sides(j, s, 0)
        v_core(j, own, 0)

    def decode_project():
        acc = jnp.zeros((NS * rows, qcols), f32)
        acc2 = jnp.zeros((NS * rows, 2 * HD), f32)
        square = jnp.zeros((NS * rows, 1), f32)
        for i in range(NT):
            xi = xu[i]
            acc += jnp.dot(xi, wq[s, i * piece : (i + 1) * piece, :], preferred_element_type=f32)
            part = slice(i * piece, (i + 1) * piece)
            joined = jnp.concatenate([wk[s, part, :], wv[s, part, :]], axis=1)
            acc2 += jnp.dot(xi, joined, preferred_element_type=f32)
            xf = xi.astype(f32)
            square += jnp.sum(xf * xf, axis=1, keepdims=True)
        wide = jnp.broadcast_to(square, (NS * rows, HD))
        for i in range(NS):
            b_send[i, :, :qcols] = acc[i * rows : (i + 1) * rows]
            b_send[i, :, qcols : qcols + 2 * HD] = acc2[i * rows : (i + 1) * rows]
            b_send[i, :, qcols + 2 * HD :] = wide[i * rows : (i + 1) * rows]
        copies = []
        for d in range(1, NS):
            p = up(s, d, NS)
            c = remote(b_send.at[p], b_recv.at[s], r["b_s"].at[d - 1], r["b_r"].at[s], shard=p)
            c.start()
            copies.append(c)
        return copies

    load_wq.wait()
    b_copies = decode_project()
    q_copy = q_send_y(0)

    load_raw.wait()
    def separate(i, c):
        src = pl.ds(pl.multiple_of(i * 256, 256), 256)
        dst = pl.ds(pl.multiple_of(i * 128, 128), 128)
        for row in range(0, rows, 2):
            pair = jnp.concatenate([raw[row, src, :], raw[row + 1, src, :]], axis=1)
            split = jnp.dot(pick, pair, preferred_element_type=f32).astype(bf16)
            for j in range(2):
                ck[row + j, dst, :] = split[:128, j * HD : (j + 1) * HD]
                cv[row + j, dst, :] = split[128:, j * HD : (j + 1) * HD]
        return c

    for i in range(tok // QT):
        q_pos = s * tok + i * QT + lax.broadcasted_iota(jnp.int32, (QT, KW), 0)
        k_pos = s * tok + i * QT - MOST + lax.broadcasted_iota(jnp.int32, (QT, KW), 1)
        start = jnp.where(q_pos >= b1, b1, jnp.where(q_pos >= b0, b0, 0))
        bias[i] = jnp.where((k_pos >= start) & (k_pos <= q_pos), 0.0, -1e30)

    v_theirs(0)
    v_pass(0, s, 0, 2)
    v_theirs(1)
    v_pass(1, s, 0, 2)
    lax.fori_loop(0, 2 * ck.shape[1] // 256, separate, 0)
    v_last(0, s, 0, 6)
    v_pass(0, s2, 2, 4)
    v_last(1, s, 0, 6)
    v_pass(1, s2, 2, 4)
    v_last(0, s2, 2, 8)
    v_core_ready(0)

    def splat(flag):
        return jnp.broadcast_to(flag, (HD, HD)).astype(f32).astype(bf16)

    at_spot = [splat((spot == j).astype(jnp.int32)) for j in range(spots)]
    takes = [splat(is_new[row]) for row in range(rows)]

    def place(j):
        stored = (ck, cv)[j]

        def part(i, c):
            dst = pl.ds(pl.multiple_of(i * HD, HD), HD)
            window = jnp.zeros((HD, HD), bf16)
            for n in range(spots):
                src = pl.ds(pl.multiple_of((1 + n) * MOST + i * HD, HD), HD)
                window = window + cached[j][src, :] * at_spot[n]
            for row in range(rows):
                stored[row, dst, :] = stored[row, dst, :] * (1 - takes[row]) + window * takes[row]
            return c

        lax.fori_loop(0, 2 * MOST // HD, part, 0)

    place(0)
    v_last(1, s2, 2, 8)
    q_copy.wait_send()
    q_copy = q_send_y(1)
    v_core_ready(1)
    place(1)
    q_arrive_y(0)
    q_forward_z(0)
    q_forward(0)

    def attend(u, c):
        h = lax.rem(u, heads)
        i = u // heads
        part = pl.ds(pl.multiple_of(i * QT, QT), QT)
        keys = pl.ds(pl.multiple_of((g * NS + s) * tok + i * QT, QT), KW)
        scores = lax.dot_general(qh[h, part, :], kk[keys, :], TRANS, preferred_element_type=f32)
        scores = scores + bias[i]
        high = jnp.max(scores, axis=1, keepdims=True)
        weights = jnp.exp2((scores - high) * (INV_ROOT * LOG2E))
        summed = jnp.sum(weights, axis=1, keepdims=True)
        mixed = jnp.dot(weights.astype(bf16), vv[keys, :], preferred_element_type=f32)
        cols = pl.ds(pl.multiple_of(h * HD, HD), HD)
        ctx_ref[part, cols] = (mixed / summed).astype(bf16)
        return c

    def attend_units(lo, hi):
        lax.fori_loop(lo, hi, attend, 0)

    def finish_queries():
        for h in range(heads):
            qh[h] = (acc_q[:, h * HD : (h + 1) * HD] * scale[...]).astype(bf16)

    def s2_early():
        q_arrive_y(1)
        q_forward_z(1)
        q_forward(1)

    def s2_sides(h):
        for i in (h, 2 + h):
            q_arrive_z(i)
            q_forward(4 + i)
        q_second(h)

    def s2_last():
        for h in range(2):
            q_arrive_second(h)
            q_forward(2 + h)

    def s3_ready():
        for i in range(8):
            q_arrive_core(i)

    units = heads * (tok // QT)
    fills = {
        (0, 0): [lambda: q_core(0), lambda: q_block(s, True)],
        (0, 1): [lambda: q_core(1)],
        (0, 2): [s2_early, lambda: q_core(2)],
        (0, 3): [lambda: s2_sides(0), lambda: q_core(3)],
        (1, 0): [q_core_ready, lambda: q_block(sc, False)],
        (1, 1): [lambda: s2_sides(1)],
        (2, 0): [s2_last, lambda: q_block(s2, False)],
        (2, 1): [s3_ready, lambda: q_block(s3, False)],
        (2, 2): [finish_queries, lambda: attend_units(0, 2)],
        (2, 3): [lambda: attend_units(2, 5)],
        (3, 0): [lambda: attend_units(5, 8)],
        (3, 1): [lambda: attend_units(8, 11)],
        (3, 2): [lambda: attend_units(11, 13)],
        (3, 3): [lambda: attend_units(13, units)],
    }

    def fill(k, i):
        for task in fills.get((k, i), []):
            task()

    def all_shards(src_of, dst, ssem, rsem):
        copies = []
        for d in range(1, NS):
            p = up(s, d, NS)
            c = remote(src_of(p), dst, ssem.at[d - 1], rsem, shard=p)
            c.start()
            copies.append(c)
        return copies

    def all_tensors(src_of, dst, ssem, rsem):
        copies = []
        for d in (4, 6, 2, 5, 3, 7, 1):
            p = up(t, d, NT)
            c = remote(src_of(p), dst, ssem.at[d - 1], rsem, tensor=p)
            c.start()
            copies.append(c)
        return copies

    def settle(copies):
        for c in copies:
            c.wait_send()

    u_send, u_recv = r["u_send"], r["u_recv"]

    def give_update(k):
        sent.extend(all_tensors(lambda p: u_send.at[k], u_recv.at[k, t], r["u_s"].at[k], r["u_r"].at[k, t]))
        u_recv[k, t] = u_send[k]

    def spread_update(k):
        for d in range(1, NT):
            src = up(t, NT - d, NT)
            arrive(u_recv.at[k, src], r["u_s"].at[k, d - 1], r["u_r"].at[k, src], tensor=src)
        for i in range(NT):
            u = u_recv[k, i].astype(f32)
            for j in range(NS):
                e_send[k, j, :, i * piece : (i + 1) * piece] = u[j * rows : (j + 1) * rows]
        sent.extend(all_shards(lambda p: e_send.at[k, p], e_recv.at[k, s], r["e_s"].at[k], r["e_r"].at[k, s]))
        e_recv[k, s] = e_send[k, s]

    cpos = lax.broadcasted_iota(jnp.int32, (heads, ck.shape[1]), 1)
    load_wo.wait()
    for k in range(STEPS):
        total = b_send[s]
        for d in range(1, NS):
            src = up(s, NS - d, NS)
            arrive(b_recv.at[src], r["b_s"].at[d - 1], r["b_r"].at[src], shard=src)
            total = total + b_recv[src]
        norm = lax.rsqrt(total[:, qcols + 2 * HD : qcols + 2 * HD + 1] / width + EPSILON)
        fresh = (total[:, : qcols + 2 * HD] * norm).astype(bf16).astype(f32)
        fkv[k] = fresh[:, qcols:]
        for row in range(rows):
            for h in range(heads):
                qs[row, h : h + 1, :] = fresh[row : row + 1, h * HD : (h + 1) * HD]
        for row in range(rows):
            q = qs[row]
            valid = (cpos >= low[row]) & (cpos < high[row])
            scores = lax.dot_general(q.astype(bf16), ck[row], TRANS, preferred_element_type=f32) * INV_ROOT
            scores = jnp.where(valid, scores, -1e30)
            top = jnp.max(scores, axis=1, keepdims=True)
            news = []
            for j in range(k + 1):
                new = jnp.sum(q * fkv[j, row : row + 1, :HD], axis=1, keepdims=True) * INV_ROOT
                news.append(new)
                top = jnp.maximum(top, new)
            weights = jnp.where(valid, jnp.exp(scores - top), 0.0)
            summed = jnp.sum(weights, axis=1, keepdims=True)
            mixed = jnp.dot(weights.astype(bf16), cv[row], preferred_element_type=f32)
            for j in range(k + 1):
                weight = jnp.exp(news[j] - top)
                summed = summed + weight
                mixed = mixed + weight.astype(bf16).astype(f32) * fkv[j, row : row + 1, HD:]
            context = (mixed / summed).astype(bf16).astype(f32)
            for h in range(heads):
                c_send[row : row + 1, h * HD : (h + 1) * HD] = context[h : h + 1]

        c_copies = all_shards(lambda p: c_send, c_recv.at[s], r["c_s"], r["c_r"].at[s])
        c_recv[s] = c_send[...]
        settle(b_copies)
        fill(k, 0)
        for d in range(1, NS):
            src = up(s, NS - d, NS)
            arrive(c_recv.at[src], r["c_s"].at[d - 1], r["c_r"].at[src], shard=src)
        block = jnp.concatenate([c_recv[i] for i in range(NS)], axis=0).astype(bf16)
        for i in range(NT):
            d_send[i] = jnp.dot(block, wo[:, i * piece : (i + 1) * piece], preferred_element_type=f32).astype(bf16)

        d_copies = all_tensors(lambda p: d_send.at[p], d_recv.at[t], r["d_s"], r["d_r"].at[t])
        settle(c_copies)
        if k > 0:
            spread_update(k - 1)
        fill(k, 1)
        update = d_send[t].astype(f32)
        for d in range(1, NT):
            src = up(t, NT - d, NT)
            arrive(d_recv.at[src], r["d_s"].at[d - 1], r["d_r"].at[src], tensor=src)
            update = update + d_recv[src].astype(f32)
        u_send[k] = update.astype(bf16)
        if k == STEPS - 1:
            give_update(k)
            settle(d_copies)
            fill(k, 2)
            spread_update(k)
            fill(k, 3)
            break
        after = state[...] + update
        state[...] = after
        xu_send[...] = after.astype(bf16)
        x_copies = all_tensors(lambda p: xu_send, xu.at[t], r["x_s"], r["x_r"].at[t])
        xu[t] = xu_send[...]
        settle(d_copies)
        fill(k, 2)
        for d in range(1, NT):
            src = up(t, NT - d, NT)
            arrive(xu.at[src], r["x_s"].at[d - 1], r["x_r"].at[src], tensor=src)
        b_copies = decode_project()
        settle(x_copies)
        give_update(k)
        fill(k, 3)

    for k in range(STEPS):
        for d in range(1, NS):
            src = up(s, NS - d, NS)
            arrive(e_recv.at[k, src], r["e_s"].at[k, d - 1], r["e_r"].at[k, src], shard=src)
        for i in range(NS):
            out_ref[k, :, i * dblk : (i + 1) * dblk] = e_recv[k, i].astype(bf16)
    q_copy.wait_send()
    settle(sent)


def write_out(context, updates, context_out, updates_out):
    context_out[...] = context[...]
    updates_out[...] = updates[...]


def layer(lens, row_prompt, cache_len, states, x, wkv, wq, wo, cache):
    rows = states.shape[0]
    tok, width = x.shape
    dblk, qcols = wq.shape
    piece = dblk // NT
    heads = qcols // HD
    vm = pltpu.VMEM
    dma = pltpu.SemaphoreType.DMA
    bw = qcols + 3 * HD
    scratch = dict(
        xv=vm((tok, width), bf16),
        wk=vm((NS, dblk, HD), bf16),
        wv=vm((NS, dblk, HD), bf16),
        wq=vm((NS, dblk, qcols), bf16),
        wo=vm(wo.shape, bf16),
        raw=vm(cache.shape, bf16),
        ck=vm((rows, CACHE, HD), bf16),
        cv=vm((rows, CACHE, HD), bf16),
        kk=vm((MOST + NG * NS * tok, HD), bf16),
        vv=vm((MOST + NG * NS * tok, HD), bf16),
        qh=vm((heads, tok, HD), bf16),
        acc_q=vm((tok, qcols), f32),
        acc_kv=vm((2, tok, HD), f32),
        scale=vm((tok, HD), f32),
        bias=vm((tok // QT, QT, KW), f32),
        kraw=vm((2 * dblk, HD), bf16),
        ds=vm((NS, rows, dblk), f32),
        a_recv=vm((NS, rows, dblk), f32),
        xu=vm((NT, NS * rows, piece), bf16),
        xu_send=vm((NS * rows, piece), bf16),
        u_send=vm((STEPS, NS * rows, piece), bf16),
        u_recv=vm((STEPS, NT, NS * rows, piece), bf16),
        state=vm((NS * rows, piece), f32),
        b_send=vm((NS, rows, bw), f32),
        b_recv=vm((NS, rows, bw), f32),
        qs=vm((rows, heads, HD), f32),
        fkv=vm((STEPS, rows, 2 * HD), f32),
        c_send=vm((rows, qcols), f32),
        c_recv=vm((NS, rows, qcols), f32),
        d_send=vm((NT, NS * rows, piece), bf16),
        d_recv=vm((NT, NS * rows, piece), bf16),
        e_send=vm((STEPS, NS, rows, dblk), f32),
        e_recv=vm((STEPS, NS, rows, dblk), f32),
        lsem=dma((5,)),
        ky_s=dma((2, 2)),
        ky_r=dma((2, 2)),
        kz_s=dma((2, 2)),
        kz_r=dma((2, 2)),
        kc_s=dma((2, 5)),
        kc_r=dma((2, 5)),
        qy_s=dma((2,)),
        qy_r=dma((2,)),
        qz_s=dma((6,)),
        qz_r=dma((6,)),
        qc_s=dma((12,)),
        qc_r=dma((12,)),
        vy_s=dma((2,)),
        vy_r=dma((2,)),
        vz_s=dma((2, 8)),
        vz_r=dma((2, 8)),
        vc_s=dma((2, 10)),
        vc_r=dma((2, 10)),
        a_s=dma((NS - 1,)),
        a_r=dma((NS,)),
        b_s=dma((NS - 1,)),
        b_r=dma((NS,)),
        c_s=dma((NS - 1,)),
        c_r=dma((NS,)),
        d_s=dma((NT - 1,)),
        d_r=dma((NT,)),
        x_s=dma((NT - 1,)),
        x_r=dma((NT,)),
        u_s=dma((STEPS, NT - 1)),
        u_r=dma((STEPS, NT)),
        e_s=dma((STEPS, NS - 1)),
        e_r=dma((STEPS, NS)),
    )
    smem = pl.BlockSpec(memory_space=pltpu.SMEM)
    vmem = pl.BlockSpec(memory_space=pltpu.VMEM)
    hbm = pl.BlockSpec(memory_space=pl.ANY)
    return pl.pallas_call(
        functools.partial(kernel, tuple(scratch)),
        out_shape=(
            jax.ShapeDtypeStruct((tok, qcols), bf16),
            jax.ShapeDtypeStruct((STEPS, rows, width), bf16),
        ),
        in_specs=[smem, smem, smem, vmem, hbm, hbm, hbm, hbm, hbm],
        out_specs=(vmem, vmem),
        scratch_shapes=list(scratch.values()),
        compiler_params=pltpu.CompilerParams(
            collective_id=0, has_side_effects=True, vmem_limit_bytes=62 * 1024 * 1024
        ),
        name="attention_layer",
    )(lens, row_prompt, cache_len, states, x, wkv, wq, wo, cache)


def body(
    prompt_states,
    prompt_lens,
    w_query,
    w_keyval,
    w_out,
    decode_states,
    kv_cache,
    cache_len,
    row_prompt,
):
    dblk = w_query.shape[0]
    rows = decode_states.shape[0]
    context, updates = layer(
        prompt_lens,
        row_prompt,
        cache_len,
        decode_states,
        prompt_states,
        w_keyval.reshape(2 * dblk, HD),
        w_query,
        w_out,
        kv_cache.reshape(rows, 2 * CACHE, HD),
    )
    vmem = pl.BlockSpec(memory_space=pltpu.VMEM)
    return pl.pallas_call(
        write_out,
        out_shape=tuple(jax.ShapeDtypeStruct(v.shape, v.dtype) for v in (context, updates)),
        in_specs=[vmem, vmem],
        out_specs=(vmem, vmem),
        name="write_out",
    )(context, updates)


def solution(mesh):
    in_specs = (
        P(("group", "shard"), None),
        P(),
        P("shard", "tensor"),
        P("shard", None, "tensor"),
        P("tensor", "shard"),
        P(("group", "shard"), None),
        P(("group", "shard"), None, None, "tensor"),
        P(("group", "shard")),
        P(("group", "shard")),
    )
    out_specs = (P(("group", "shard"), "tensor"), P(None, ("group", "shard"), None))
    return jax.shard_map(body, mesh=mesh, in_specs=in_specs, out_specs=out_specs, check_vma=False)
```

```python
import functools

import jax
import jax.numpy as jnp
from jax import lax
from jax.experimental import pallas as pl
from jax.experimental.pallas import tpu as pltpu
from jax.sharding import PartitionSpec as P

HD = 128
CACHE = 2048
STEPS = 4
EPSILON = 1e-05
MESH = pl.DeviceIdType.MESH
NG = 4
NS = 4
NT = 8
MOST = 1024
QT = 256
KW = QT + MOST
INV_ROOT = HD**-0.5
LOG2E = 1.4426950408889634
TRANS = (((1,), (1,)), ((), ()))
f32 = jnp.float32
bf16 = jnp.bfloat16


def kernel(names, lens_ref, rowp_ref, clen_ref, ds_ref, x_hbm, wkv_hbm, wq_hbm, wo_hbm, cache_hbm, ctx_ref, out_ref, *scratch):
    r = dict(zip(names, scratch))
    xv, wk, wv, wq, wo, raw, ck, cv = (r[n] for n in ("xv", "wk", "wv", "wq", "wo", "raw", "ck", "cv"))
    kk, vv, qh, acc_q, acc_kv, scale, bias = (r[n] for n in ("kk", "vv", "qh", "acc_q", "acc_kv", "scale", "bias"))
    a_recv, xu, xu_send, state = (r[n] for n in ("a_recv", "xu", "xu_send", "state"))
    b_send, b_recv, qs, fkv = (r[n] for n in ("b_send", "b_recv", "qs", "fkv"))
    c_send, c_recv, d_send, d_recv = (r[n] for n in ("c_send", "c_recv", "d_send", "d_recv"))
    e_send, e_recv = r["e_send"], r["e_recv"]

    g = lax.axis_index("group")
    s = lax.axis_index("shard")
    t = lax.axis_index("tensor")
    sc = s + 1 - 2 * lax.rem(s, 2)
    s2 = lax.rem(s + 2, NS)
    s3 = lax.rem(sc + 2, NS)
    tok = xv.shape[0]
    rows = ds_ref.shape[0]
    dblk, qcols = wq.shape[1:]
    piece = dblk // NT
    heads = qcols // HD
    width = NS * dblk
    quarter = dblk // NG
    half = quarter // 2

    def up(base, d, n):
        return lax.rem(base + d, n)

    def remote(src, dst, ssem, rsem, **where):
        return pltpu.make_async_remote_copy(
            src_ref=src, dst_ref=dst, send_sem=ssem, recv_sem=rsem, device_id=where, device_id_type=MESH
        )

    sent = []

    def send(src, dst, ssem, rsem, **where):
        c = remote(src, dst, ssem, rsem, **where)
        c.start()
        sent.append(c)
        return c

    def arrive(dst, ssem, rsem, **where):
        remote(dst, dst, ssem, rsem, **where).wait_recv()

    def load(a, b, i):
        c = pltpu.make_async_copy(a, b, r["lsem"].at[i])
        c.start()
        return c

    load_wkv = load(wkv_hbm, r["kraw"], 1)
    load_x = load(x_hbm, xv, 0)
    load_wq = load(wq_hbm, wq.at[s], 2)

    barrier = pltpu.get_barrier_semaphore()
    for d in range(1, NS):
        pl.semaphore_signal(barrier, inc=1, device_id={"shard": up(s, d, NS)}, device_id_type=MESH)
    for d in range(1, NG):
        pl.semaphore_signal(barrier, inc=1, device_id={"group": up(g, d, NG)}, device_id_type=MESH)
    for d in range(1, NT):
        pl.semaphore_signal(barrier, inc=1, device_id={"tensor": up(t, d, NT)}, device_id_type=MESH)

    begin = jnp.int32(0)
    prompts = NG * lens_ref.shape[1]
    starts = [jnp.int32(0)] * rows
    sizes = [jnp.int32(0)] * rows
    for i in range(prompts):
        here = lens_ref[i // lens_ref.shape[1], i % lens_ref.shape[1]]
        for row in range(rows):
            hit = (rowp_ref[row] == i).astype(jnp.int32)
            starts[row] = starts[row] + hit * begin
            sizes[row] = sizes[row] + hit * here
        begin = begin + here
    b0 = lens_ref[g, 0]
    b1 = b0 + lens_ref[g, 1]
    is_new = [(rowp_ref[row] < prompts).astype(jnp.int32) for row in range(rows)]
    spots = NG * NS * tok // MOST - 1
    begin = sum(starts)
    spot = jnp.minimum(begin // MOST, spots - 1)
    low = [is_new[row] * (starts[row] - spot * MOST) for row in range(rows)]
    high = [low[row] + is_new[row] * sizes[row] + (1 - is_new[row]) * clen_ref[row] for row in range(rows)]

    out_i = lax.broadcasted_iota(jnp.int32, (256, 256), 0)
    in_i = lax.broadcasted_iota(jnp.int32, (256, 256), 1)
    want = jnp.where(out_i < 128, 2 * out_i, 2 * (out_i - 128) + 1)
    pick = (in_i == want).astype(bf16)

    load_wkv.wait()

    def separate_weights(i, c):
        pair = jnp.concatenate(
            [r["kraw"][pl.ds(pl.multiple_of((2 * i + j) * 256, 256), 256), :] for j in range(2)], axis=1
        )
        split = jnp.dot(pick, pair, preferred_element_type=f32).astype(bf16)
        for j in range(2):
            dst = pl.ds(pl.multiple_of((2 * i + j) * 128, 128), 128)
            wk[s, dst, :] = split[:128, j * HD : (j + 1) * HD]
            wv[s, dst, :] = split[128:, j * HD : (j + 1) * HD]
        return c

    lax.fori_loop(0, dblk // 256, separate_weights, 0)
    ds = r["ds"]
    for i in range(NS):
        ds[i] = ds_ref[:, i * dblk : (i + 1) * dblk].astype(f32)
    pl.semaphore_wait(barrier, NS - 1 + NG - 1 + NT - 1)

    weights_of, cached = (wk, wv), (kk, vv)

    def krows(j, blk, q):
        return weights_of[j].at[blk, pl.ds(pl.multiple_of(q * quarter, quarter), quarter)]

    def qrows(blk, q, h):
        return wq.at[blk, pl.ds(pl.multiple_of(q * quarter + h * half, half), half)]

    q_of = [g, up(g, 2, NG), up(g, 3, NG), up(g, 1, NG)]
    ky_s, ky_r, kz_s, kz_r, kc_s, kc_r = (r[n] for n in ("ky_s", "ky_r", "kz_s", "kz_r", "kc_s", "kc_r"))
    qy_s, qy_r, qz_s, qz_r, qc_s, qc_r = (r[n] for n in ("qy_s", "qy_r", "qz_s", "qz_r", "qc_s", "qc_r"))

    for i, j in ((0, 0), (0, 1), (1, 0), (1, 1)):
        ref = krows(j, s, q_of[i])
        send(ref, ref, ky_s.at[j, i], ky_r.at[j, i], shard=s2)
    for j in range(2):
        ref = weights_of[j].at[s]
        send(ref, ref, kc_s.at[j, 4], kc_r.at[j, 4], shard=sc)
    for d in range(1, NS):
        p = up(s, d, NS)
        send(ds.at[p], a_recv.at[s], r["a_s"].at[d - 1], r["a_r"].at[s], shard=p)
    a_recv[s] = ds[s]
    r["fkv"][...] = jnp.zeros_like(fkv)
    for ref in cached:
        ref[:MOST, :] = jnp.zeros((MOST, HD), bf16)

    def k_arrive_y(j, i):
        arrive(krows(j, s2, q_of[i]), ky_s.at[j, i], ky_r.at[j, i], shard=s2)

    def k_arrive_z(j, i):
        arrive(krows(j, s2, q_of[2 + i]), kz_s.at[j, i], kz_r.at[j, i], group=q_of[2 + i])

    def k_arrive_core(j, role):
        arrive(krows(j, s3, q_of[role]), kc_s.at[j, role], kc_r.at[j, role], shard=sc)

    def k_forward(j, role):
        ref = krows(j, s2, q_of[role])
        send(ref, ref, kc_s.at[j, role], kc_r.at[j, role], shard=sc)

    def k_forward_z(j):
        ref = krows(j, s2, g)
        send(ref, ref, kz_s.at[j, 0], kz_r.at[j, 0], group=up(g, 1, NG))
        send(ref, ref, kz_s.at[j, 1], kz_r.at[j, 1], group=up(g, 3, NG))

    def q_core(q):
        ref = wq.at[s, pl.ds(q * quarter, quarter)]
        send(ref, ref, qc_s.at[8 + q], qc_r.at[8 + q], shard=sc)

    def q_core_ready():
        for q in range(NG):
            ref = wq.at[sc, pl.ds(q * quarter, quarter)]
            arrive(ref, qc_s.at[8 + q], qc_r.at[8 + q], shard=sc)

    def q_send_y(i):
        ref = qrows(s, g, i)
        send(ref, ref, qy_s.at[i], qy_r.at[i], shard=s2)

    def q_arrive_y(i):
        arrive(qrows(s2, g, i), qy_s.at[i], qy_r.at[i], shard=s2)

    def q_second(h):
        ref = qrows(s2, q_of[2 + h], h)
        send(ref, ref, qz_s.at[4 + h], qz_r.at[4 + h], group=up(g, 1 + 2 * h, NG))

    def q_arrive_second(h):
        arrive(qrows(s2, q_of[1], h), qz_s.at[4 + h], qz_r.at[4 + h], group=q_of[2 + h])

    def q_forward_z(h):
        ref = qrows(s2, g, h)
        send(ref, ref, qz_s.at[h], qz_r.at[h], group=up(g, 1, NG))
        send(ref, ref, qz_s.at[2 + h], qz_r.at[2 + h], group=up(g, 3, NG))

    def q_arrive_z(i):
        arrive(qrows(s2, q_of[2 + i // 2], i % 2), qz_s.at[i], qz_r.at[i], group=q_of[2 + i // 2])

    def q_forward(i):
        ref = qrows(s2, q_of[i // 2], i % 2)
        send(ref, ref, qc_s.at[i], qc_r.at[i], shard=sc)

    def q_arrive_core(i):
        arrive(qrows(s3, q_of[i // 2], i % 2), qc_s.at[i], qc_r.at[i], shard=sc)

    def x_block(blk):
        return xv[:, pl.ds(pl.multiple_of(blk * dblk, dblk), dblk)]

    def kv_block(j, blk, first):
        prod = jnp.dot(x_block(blk), weights_of[j][blk], preferred_element_type=f32)
        acc_kv[j] = prod if first else acc_kv[j] + prod

    def q_block(blk, first, lo=0, hi=None):
        hi = qcols // 256 if hi is None else hi

        def part(n, c):
            cols = pl.ds(pl.multiple_of(n * 256, 256), 256)
            prod = jnp.dot(x_block(blk), wq[blk, :, cols], preferred_element_type=f32)
            acc_q[:, cols] = prod if first else acc_q[:, cols] + prod
            return c

        lax.fori_loop(lo, hi, part, 0)

    load_x.wait()
    load_raw = load(cache_hbm, raw, 3)
    load_wo = load(wo_hbm, wo, 4)

    def squares(i, c):
        part = pl.ds(pl.multiple_of(i * 32, 32), 32)
        v = xv[part, :].astype(f32)
        mean = jnp.sum(v * v, axis=1, keepdims=True) / width
        scale[part, :] = jnp.broadcast_to(lax.rsqrt(mean + EPSILON), (32, HD))
        return c

    for j in range(2):
        kv_block(j, s, True)
    k_arrive_y(0, 0)
    k_forward_z(0)
    k_forward(0, 0)
    lax.fori_loop(0, tok // 32, squares, 0)
    k_arrive_y(1, 0)
    k_forward_z(1)
    k_forward(1, 0)

    for d in range(1, NS):
        src = up(s, NS - d, NS)
        arrive(a_recv.at[src], r["a_s"].at[d - 1], r["a_r"].at[src], shard=src)
    x0 = jnp.concatenate([a_recv[i] for i in range(NS)], axis=0)
    for i in range(NT):
        xu[i] = x0[:, i * piece : (i + 1) * piece].astype(bf16)
    mine = pl.ds(pl.multiple_of(t * piece, piece), piece)
    state[...] = jnp.concatenate([a_recv[i, :, mine] for i in range(NS)], axis=0)

    def slot(j, gg, ss):
        return cached[j].at[pl.ds(pl.multiple_of(MOST + (gg * NS + ss) * tok, tok), tok)]

    def half_slot(j, gg, ss, h):
        n = tok // 2
        return cached[j].at[pl.ds(pl.multiple_of(MOST + (gg * NS + ss) * tok + h * n, n), n)]

    vy_s, vy_r, vz_s, vz_r, vc_s, vc_r = (r[n] for n in ("vy_s", "vy_r", "vz_s", "vz_r", "vc_s", "vc_r"))
    below, above = up(g, 3, NG), up(g, 1, NG)

    def v_core(j, ref, i):
        send(ref, ref, vc_s.at[j, i], vc_r.at[j, i], shard=sc)

    def v_sides(j, ss, i):
        ref = slot(j, g, ss)
        send(ref, ref, vz_s.at[j, i], vz_r.at[j, i], group=above)
        send(ref, ref, vz_s.at[j, i + 1], vz_r.at[j, i + 1], group=below)

    def v_pass(j, ss, i, core):
        for h, (source, target) in enumerate([(below, above), (above, below)]):
            arrive(slot(j, source, ss), vz_s.at[j, i + h], vz_r.at[j, i + h], group=source)
            ref = half_slot(j, source, ss, h)
            send(ref, ref, vz_s.at[j, i + 4 + h], vz_r.at[j, i + 4 + h], group=target)
            v_core(j, slot(j, source, ss), core + h)

    def v_last(j, ss, i, core):
        for h, source in enumerate([below, above]):
            ref = half_slot(j, up(g, 2, NG), ss, h)
            arrive(ref, vz_s.at[j, i + 4 + h], vz_r.at[j, i + 4 + h], group=source)
            v_core(j, ref, core + h)

    def v_theirs(j):
        ref = slot(j, g, s2)
        arrive(ref, vy_s.at[j], vy_r.at[j], shard=s2)
        v_sides(j, s2, 2)
        v_core(j, ref, 1)

    def v_core_ready(j):
        for i, ref in enumerate(
            [slot(j, g, sc), slot(j, g, s3)]
            + [slot(j, gg, ss) for ss in (sc, s3) for gg in (below, above)]
            + [half_slot(j, up(g, 2, NG), ss, h) for ss in (sc, s3) for h in range(2)]
        ):
            arrive(ref, vc_s.at[j, i], vc_r.at[j, i], shard=sc)

    for j in range(2):
        k_arrive_z(j, 0)
        k_forward(j, 2)
        k_arrive_z(j, 1)
        k_forward(j, 3)
        k_arrive_y(j, 1)
        k_forward(j, 1)
        arrive(weights_of[j].at[sc], kc_s.at[j, 4], kc_r.at[j, 4], shard=sc)
        kv_block(j, sc, False)
        kv_block(j, s2, False)
        for role in (0, 2, 3, 1):
            k_arrive_core(j, role)
        kv_block(j, s3, False)
        cached[j][pl.ds(pl.multiple_of(MOST + (g * NS + s) * tok, tok), tok), :] = (acc_kv[j] * scale[...]).astype(
            bf16
        )
        own = slot(j, g, s)
        send(own, own, vy_s.at[j], vy_r.at[j], shard=s2)
        v_sides(j, s, 0)
        v_core(j, own, 0)

    def decode_project():
        acc = jnp.zeros((NS * rows, qcols), f32)
        acc2 = jnp.zeros((NS * rows, 2 * HD), f32)
        square = jnp.zeros((NS * rows, 1), f32)
        for i in range(NT):
            xi = xu[i]
            acc += jnp.dot(xi, wq[s, i * piece : (i + 1) * piece, :], preferred_element_type=f32)
            part = slice(i * piece, (i + 1) * piece)
            joined = jnp.concatenate([wk[s, part, :], wv[s, part, :]], axis=1)
            acc2 += jnp.dot(xi, joined, preferred_element_type=f32)
            xf = xi.astype(f32)
            square += jnp.sum(xf * xf, axis=1, keepdims=True)
        wide = jnp.broadcast_to(square, (NS * rows, HD))
        for i in range(NS):
            b_send[i, :, :qcols] = acc[i * rows : (i + 1) * rows]
            b_send[i, :, qcols : qcols + 2 * HD] = acc2[i * rows : (i + 1) * rows]
            b_send[i, :, qcols + 2 * HD :] = wide[i * rows : (i + 1) * rows]
        copies = []
        for d in range(1, NS):
            p = up(s, d, NS)
            c = remote(b_send.at[p], b_recv.at[s], r["b_s"].at[d - 1], r["b_r"].at[s], shard=p)
            c.start()
            copies.append(c)
        return copies

    load_wq.wait()
    b_copies = decode_project()
    q_send_y(0)
    q_send_y(1)

    load_raw.wait()
    def separate(i, c):
        src = pl.ds(pl.multiple_of(i * 256, 256), 256)
        dst = pl.ds(pl.multiple_of(i * 128, 128), 128)
        for row in range(0, rows, 2):
            pair = jnp.concatenate([raw[row, src, :], raw[row + 1, src, :]], axis=1)
            split = jnp.dot(pick, pair, preferred_element_type=f32).astype(bf16)
            for j in range(2):
                ck[row + j, dst, :] = split[:128, j * HD : (j + 1) * HD]
                cv[row + j, dst, :] = split[128:, j * HD : (j + 1) * HD]
        return c

    for i in range(tok // QT):
        q_pos = s * tok + i * QT + lax.broadcasted_iota(jnp.int32, (QT, KW), 0)
        k_pos = s * tok + i * QT - MOST + lax.broadcasted_iota(jnp.int32, (QT, KW), 1)
        start = jnp.where(q_pos >= b1, b1, jnp.where(q_pos >= b0, b0, 0))
        bias[i] = jnp.where((k_pos >= start) & (k_pos <= q_pos), 0.0, -1e30)

    v_theirs(0)
    v_pass(0, s, 0, 2)
    v_theirs(1)
    v_pass(1, s, 0, 2)
    lax.fori_loop(0, 2 * ck.shape[1] // 256, separate, 0)
    v_last(0, s, 0, 6)
    v_pass(0, s2, 2, 4)
    v_last(1, s, 0, 6)
    v_pass(1, s2, 2, 4)
    v_last(0, s2, 2, 8)
    v_core_ready(0)

    def splat(flag):
        return jnp.broadcast_to(flag, (HD, HD)).astype(f32).astype(bf16)

    at_spot = [splat((spot == j).astype(jnp.int32)) for j in range(spots)]
    takes = [splat(is_new[row]) for row in range(rows)]

    def place(j):
        stored = (ck, cv)[j]

        def part(i, c):
            dst = pl.ds(pl.multiple_of(i * HD, HD), HD)
            window = jnp.zeros((HD, HD), bf16)
            for n in range(spots):
                src = pl.ds(pl.multiple_of((1 + n) * MOST + i * HD, HD), HD)
                window = window + cached[j][src, :] * at_spot[n]
            for row in range(rows):
                stored[row, dst, :] = stored[row, dst, :] * (1 - takes[row]) + window * takes[row]
            return c

        lax.fori_loop(0, 2 * MOST // HD, part, 0)

    place(0)
    v_last(1, s2, 2, 8)
    v_core_ready(1)
    place(1)
    q_arrive_y(0)
    q_forward_z(0)
    q_forward(0)

    def attend(u, c):
        h = lax.rem(u, heads)
        i = u // heads
        part = pl.ds(pl.multiple_of(i * QT, QT), QT)
        keys = pl.ds(pl.multiple_of((g * NS + s) * tok + i * QT, QT), KW)
        scores = lax.dot_general(qh[h, part, :], kk[keys, :], TRANS, preferred_element_type=f32)
        scores = scores + bias[i]
        high = jnp.max(scores, axis=1, keepdims=True)
        weights = jnp.exp2((scores - high) * (INV_ROOT * LOG2E))
        summed = jnp.sum(weights, axis=1, keepdims=True)
        mixed = jnp.dot(weights.astype(bf16), vv[keys, :], preferred_element_type=f32)
        cols = pl.ds(pl.multiple_of(h * HD, HD), HD)
        ctx_ref[part, cols] = (mixed / summed).astype(bf16)
        return c

    def attend_units(lo, hi):
        lax.fori_loop(lo, hi, attend, 0)

    def finish_queries():
        for h in range(heads):
            qh[h] = (acc_q[:, h * HD : (h + 1) * HD] * scale[...]).astype(bf16)

    def s2_early():
        q_arrive_y(1)
        q_forward_z(1)
        q_forward(1)

    def s2_sides(h):
        for i in (h, 2 + h):
            q_arrive_z(i)
            q_forward(4 + i)
        q_second(h)

    def s2_last():
        for h in range(2):
            q_arrive_second(h)
            q_forward(2 + h)

    def s3_ready():
        for i in range(8):
            q_arrive_core(i)

    units = heads * (tok // QT)
    fills = {
        (0, 0): [lambda: q_core(0), lambda: q_block(s, True)],
        (0, 1): [s2_early, lambda: q_core(1)],
        (0, 2): [lambda: q_core(2)],
        (0, 3): [lambda: s2_sides(0), lambda: q_core(3)],
        (1, 0): [q_core_ready, lambda: q_block(sc, False)],
        (1, 1): [lambda: s2_sides(1)],
        (2, 0): [s2_last, lambda: q_block(s2, False)],
        (2, 1): [s3_ready, lambda: q_block(s3, False)],
        (2, 2): [finish_queries, lambda: attend_units(0, 2)],
        (2, 3): [lambda: attend_units(2, 5)],
        (3, 0): [lambda: attend_units(5, 8)],
        (3, 1): [lambda: attend_units(8, 12)],
        (3, 2): [lambda: attend_units(12, units)],
    }

    def fill(k, i):
        for task in fills.get((k, i), []):
            task()

    def all_shards(src_of, dst, ssem, rsem):
        copies = []
        for d in range(1, NS):
            p = up(s, d, NS)
            c = remote(src_of(p), dst, ssem.at[d - 1], rsem, shard=p)
            c.start()
            copies.append(c)
        return copies

    def all_tensors(src_of, dst, ssem, rsem):
        copies = []
        for d in (4, 6, 2, 5, 3, 7, 1):
            p = up(t, d, NT)
            c = remote(src_of(p), dst, ssem.at[d - 1], rsem, tensor=p)
            c.start()
            copies.append(c)
        return copies

    def settle(copies):
        for c in copies:
            c.wait_send()

    u_send, u_recv = r["u_send"], r["u_recv"]

    def give_update(k):
        sent.extend(all_tensors(lambda p: u_send.at[k], u_recv.at[k, t], r["u_s"].at[k], r["u_r"].at[k, t]))
        u_recv[k, t] = u_send[k]

    def spread_update(k):
        for d in range(1, NT):
            src = up(t, NT - d, NT)
            arrive(u_recv.at[k, src], r["u_s"].at[k, d - 1], r["u_r"].at[k, src], tensor=src)
        for i in range(NT):
            u = u_recv[k, i].astype(f32)
            for j in range(NS):
                e_send[k, j, :, i * piece : (i + 1) * piece] = u[j * rows : (j + 1) * rows]
        sent.extend(all_shards(lambda p: e_send.at[k, p], e_recv.at[k, s], r["e_s"].at[k], r["e_r"].at[k, s]))
        e_recv[k, s] = e_send[k, s]

    cpos = lax.broadcasted_iota(jnp.int32, (heads, ck.shape[1]), 1)
    load_wo.wait()
    for k in range(STEPS):
        total = b_send[s]
        for d in range(1, NS):
            src = up(s, NS - d, NS)
            arrive(b_recv.at[src], r["b_s"].at[d - 1], r["b_r"].at[src], shard=src)
            total = total + b_recv[src]
        norm = lax.rsqrt(total[:, qcols + 2 * HD : qcols + 2 * HD + 1] / width + EPSILON)
        fresh = (total[:, : qcols + 2 * HD] * norm).astype(bf16).astype(f32)
        fkv[k] = fresh[:, qcols:]
        for row in range(rows):
            for h in range(heads):
                qs[row, h : h + 1, :] = fresh[row : row + 1, h * HD : (h + 1) * HD]
        for row in range(rows):
            q = qs[row]
            valid = (cpos >= low[row]) & (cpos < high[row])
            scores = lax.dot_general(q.astype(bf16), ck[row], TRANS, preferred_element_type=f32) * INV_ROOT
            scores = jnp.where(valid, scores, -1e30)
            top = jnp.max(scores, axis=1, keepdims=True)
            news = []
            for j in range(k + 1):
                new = jnp.sum(q * fkv[j, row : row + 1, :HD], axis=1, keepdims=True) * INV_ROOT
                news.append(new)
                top = jnp.maximum(top, new)
            weights = jnp.where(valid, jnp.exp(scores - top), 0.0)
            summed = jnp.sum(weights, axis=1, keepdims=True)
            mixed = jnp.dot(weights.astype(bf16), cv[row], preferred_element_type=f32)
            for j in range(k + 1):
                weight = jnp.exp(news[j] - top)
                summed = summed + weight
                mixed = mixed + weight.astype(bf16).astype(f32) * fkv[j, row : row + 1, HD:]
            context = (mixed / summed).astype(bf16).astype(f32)
            for h in range(heads):
                c_send[row : row + 1, h * HD : (h + 1) * HD] = context[h : h + 1]

        c_copies = all_shards(lambda p: c_send, c_recv.at[s], r["c_s"], r["c_r"].at[s])
        c_recv[s] = c_send[...]
        settle(b_copies)
        fill(k, 0)
        for d in range(1, NS):
            src = up(s, NS - d, NS)
            arrive(c_recv.at[src], r["c_s"].at[d - 1], r["c_r"].at[src], shard=src)
        block = jnp.concatenate([c_recv[i] for i in range(NS)], axis=0).astype(bf16)
        for i in range(NT):
            d_send[i] = jnp.dot(block, wo[:, i * piece : (i + 1) * piece], preferred_element_type=f32).astype(bf16)

        d_copies = all_tensors(lambda p: d_send.at[p], d_recv.at[t], r["d_s"], r["d_r"].at[t])
        settle(c_copies)
        if k > 0:
            spread_update(k - 1)
        fill(k, 1)
        update = d_send[t].astype(f32)
        for d in range(1, NT):
            src = up(t, NT - d, NT)
            arrive(d_recv.at[src], r["d_s"].at[d - 1], r["d_r"].at[src], tensor=src)
            update = update + d_recv[src].astype(f32)
        u_send[k] = update.astype(bf16)
        if k == STEPS - 1:
            give_update(k)
            settle(d_copies)
            fill(k, 2)
            spread_update(k)
            break
        after = state[...] + update
        state[...] = after
        xu_send[...] = after.astype(bf16)
        x_copies = all_tensors(lambda p: xu_send, xu.at[t], r["x_s"], r["x_r"].at[t])
        xu[t] = xu_send[...]
        settle(d_copies)
        fill(k, 2)
        for d in range(1, NT):
            src = up(t, NT - d, NT)
            arrive(xu.at[src], r["x_s"].at[d - 1], r["x_r"].at[src], tensor=src)
        b_copies = decode_project()
        settle(x_copies)
        give_update(k)
        fill(k, 3)

    for k in range(STEPS):
        for d in range(1, NS):
            src = up(s, NS - d, NS)
            arrive(e_recv.at[k, src], r["e_s"].at[k, d - 1], r["e_r"].at[k, src], shard=src)
        for i in range(NS):
            out_ref[k, :, i * dblk : (i + 1) * dblk] = e_recv[k, i].astype(bf16)
    settle(sent)


def write_out(context, updates, context_out, updates_out):
    context_out[...] = context[...]
    updates_out[...] = updates[...]


def layer(lens, row_prompt, cache_len, states, x, wkv, wq, wo, cache):
    rows = states.shape[0]
    tok, width = x.shape
    dblk, qcols = wq.shape
    piece = dblk // NT
    heads = qcols // HD
    vm = pltpu.VMEM
    dma = pltpu.SemaphoreType.DMA
    bw = qcols + 3 * HD
    scratch = dict(
        xv=vm((tok, width), bf16),
        wk=vm((NS, dblk, HD), bf16),
        wv=vm((NS, dblk, HD), bf16),
        wq=vm((NS, dblk, qcols), bf16),
        wo=vm(wo.shape, bf16),
        raw=vm(cache.shape, bf16),
        ck=vm((rows, CACHE, HD), bf16),
        cv=vm((rows, CACHE, HD), bf16),
        kk=vm((MOST + NG * NS * tok, HD), bf16),
        vv=vm((MOST + NG * NS * tok, HD), bf16),
        qh=vm((heads, tok, HD), bf16),
        acc_q=vm((tok, qcols), f32),
        acc_kv=vm((2, tok, HD), f32),
        scale=vm((tok, HD), f32),
        bias=vm((tok // QT, QT, KW), f32),
        kraw=vm((2 * dblk, HD), bf16),
        ds=vm((NS, rows, dblk), f32),
        a_recv=vm((NS, rows, dblk), f32),
        xu=vm((NT, NS * rows, piece), bf16),
        xu_send=vm((NS * rows, piece), bf16),
        u_send=vm((STEPS, NS * rows, piece), bf16),
        u_recv=vm((STEPS, NT, NS * rows, piece), bf16),
        state=vm((NS * rows, piece), f32),
        b_send=vm((NS, rows, bw), f32),
        b_recv=vm((NS, rows, bw), f32),
        qs=vm((rows, heads, HD), f32),
        fkv=vm((STEPS, rows, 2 * HD), f32),
        c_send=vm((rows, qcols), f32),
        c_recv=vm((NS, rows, qcols), f32),
        d_send=vm((NT, NS * rows, piece), bf16),
        d_recv=vm((NT, NS * rows, piece), bf16),
        e_send=vm((STEPS, NS, rows, dblk), f32),
        e_recv=vm((STEPS, NS, rows, dblk), f32),
        lsem=dma((5,)),
        ky_s=dma((2, 2)),
        ky_r=dma((2, 2)),
        kz_s=dma((2, 2)),
        kz_r=dma((2, 2)),
        kc_s=dma((2, 5)),
        kc_r=dma((2, 5)),
        qy_s=dma((2,)),
        qy_r=dma((2,)),
        qz_s=dma((6,)),
        qz_r=dma((6,)),
        qc_s=dma((12,)),
        qc_r=dma((12,)),
        vy_s=dma((2,)),
        vy_r=dma((2,)),
        vz_s=dma((2, 8)),
        vz_r=dma((2, 8)),
        vc_s=dma((2, 10)),
        vc_r=dma((2, 10)),
        a_s=dma((NS - 1,)),
        a_r=dma((NS,)),
        b_s=dma((NS - 1,)),
        b_r=dma((NS,)),
        c_s=dma((NS - 1,)),
        c_r=dma((NS,)),
        d_s=dma((NT - 1,)),
        d_r=dma((NT,)),
        x_s=dma((NT - 1,)),
        x_r=dma((NT,)),
        u_s=dma((STEPS, NT - 1)),
        u_r=dma((STEPS, NT)),
        e_s=dma((STEPS, NS - 1)),
        e_r=dma((STEPS, NS)),
    )
    smem = pl.BlockSpec(memory_space=pltpu.SMEM)
    vmem = pl.BlockSpec(memory_space=pltpu.VMEM)
    hbm = pl.BlockSpec(memory_space=pl.ANY)
    return pl.pallas_call(
        functools.partial(kernel, tuple(scratch)),
        out_shape=(
            jax.ShapeDtypeStruct((tok, qcols), bf16),
            jax.ShapeDtypeStruct((STEPS, rows, width), bf16),
        ),
        in_specs=[smem, smem, smem, vmem, hbm, hbm, hbm, hbm, hbm],
        out_specs=(vmem, vmem),
        scratch_shapes=list(scratch.values()),
        compiler_params=pltpu.CompilerParams(
            collective_id=0, has_side_effects=True, vmem_limit_bytes=62 * 1024 * 1024
        ),
        name="attention_layer",
    )(lens, row_prompt, cache_len, states, x, wkv, wq, wo, cache)


def body(
    prompt_states,
    prompt_lens,
    w_query,
    w_keyval,
    w_out,
    decode_states,
    kv_cache,
    cache_len,
    row_prompt,
):
    dblk = w_query.shape[0]
    rows = decode_states.shape[0]
    context, updates = layer(
        prompt_lens,
        row_prompt,
        cache_len,
        decode_states,
        prompt_states,
        w_keyval.reshape(2 * dblk, HD),
        w_query,
        w_out,
        kv_cache.reshape(rows, 2 * CACHE, HD),
    )
    vmem = pl.BlockSpec(memory_space=pltpu.VMEM)
    return pl.pallas_call(
        write_out,
        out_shape=tuple(jax.ShapeDtypeStruct(v.shape, v.dtype) for v in (context, updates)),
        in_specs=[vmem, vmem],
        out_specs=(vmem, vmem),
        name="write_out",
    )(context, updates)


def solution(mesh):
    in_specs = (
        P(("group", "shard"), None),
        P(),
        P("shard", "tensor"),
        P("shard", None, "tensor"),
        P("tensor", "shard"),
        P(("group", "shard"), None),
        P(("group", "shard"), None, None, "tensor"),
        P(("group", "shard")),
        P(("group", "shard")),
    )
    out_specs = (P(("group", "shard"), "tensor"), P(None, ("group", "shard"), None))
    return jax.shard_map(body, mesh=mesh, in_specs=in_specs, out_specs=out_specs, check_vma=False)
```
